128 devices in a mesh: row: 4 (over y), col: 32 (over z, x, core).
Axes of the slice: x: 4, y: 4, z: 4, core: 2. Of those that a mesh axis runs over, the one named last changes fastest.
Arguments:
- coarse: bfloat16 [64, 256, 256], P('row', 'col'), may hold values from -3.5 to 3.5
- norm1_gain: float32 [256], replicated, may hold values from 0.25 to 1.75
- norm1_bias: float32 [256], replicated, may hold values from -2.5 to 2.5
- w_qkv: bfloat16 [256, 768], replicated, may hold values from -1.25 to 1.25
- w_proj: bfloat16 [256, 256], replicated, may hold values from -0.375 to 0.375
- second_norm2_gain: float32 [256], replicated, may hold values from 0.25 to 1.75
- second_norm2_bias: float32 [256], replicated, may hold values from -2.5 to 2.5
- conv_weight: bfloat16 [3, 3, 256, 256], replicated, may hold values from -0.125 to 0.125
- conv_bias: float32 [256], replicated, may hold values from -2.5 to 2.5
- cotangent: bfloat16 [128, 512, 256], P('row', 'col'), may hold values from -6 to 6
Outputs:
- fine_out: bfloat16 [128, 512, 256], P('row', 'col')
- gradient_upsampled_field: bfloat16 [128, 512, 256], P('row', 'col')
- grad_conv: float32 [3, 3, 256, 256], replicated
- grad_norm: float32 [2, 256], replicated
The draws below stay inside these ranges and needn't reach their ends.
All inputs are finite; a program needn't handle non-finite values.
Results may differ from the reference program's by a relative error of at most 0.009.
The reference program's roundings to bfloat16 on the way (of `normed1`, `triple`, `attended`, `merged` and `hidden`) count: a program that leaves them out, or rounds other values in their place, can miss the bound.
Values may be sent and summed in bfloat16 or wider, within the bound.
No kernel may reach another device: no remote copies, remote signals or barrier semaphores. Data moves between devices by JAX's collectives and lax.ppermute only.
A program may use at most 128 MiB of HBM per device.

```python
import jax
import jax.numpy as jnp
from jax import lax

C = 256
HEADS = 4
HD = 64
GROUPS = 32
BR = 16
BC = 8
HC = 64
WC = 256
FH = 128
FW = 512


def draw_coarse(key, part):
    key = jax.random.fold_in(key, 11)
    base = jnp.clip(jax.random.normal(key, (HC, WC, C), jnp.float32), -3.5, 3.5)
    cell_rows = lax.broadcasted_iota(jnp.int32, (HC, WC), 0)
    cell_cols = lax.broadcasted_iota(jnp.int32, (HC, WC), 1)
    region_rows = cell_rows // BR * BR
    region_cols = (cell_cols - cell_cols % 2) // BC * BC
    scale_table = jnp.exp(jax.random.uniform(jax.random.fold_in(key, 31), (HC, WC), jnp.float32, jnp.log(0.5), jnp.log(1.6)))
    shift_table = jax.random.uniform(jax.random.fold_in(key, 37), (HC, WC), jnp.float32, -0.5, 0.5)
    region_scale = scale_table[region_rows, region_cols]
    region_shift = shift_table[region_rows, region_cols]
    channel_scale = jnp.exp(jax.random.uniform(jax.random.fold_in(key, 41), (C,), jnp.float32, jnp.log(0.25), jnp.log(1.6)))
    channel_shift = jax.random.uniform(jax.random.fold_in(key, 43), (C,), jnp.float32, -1.2, 1.2)
    value = channel_shift[None, None, :] + region_shift[:, :, None] + base * channel_scale[None, None, :] * region_scale[:, :, None]
    return jnp.clip(value, -3.5, 3.5).astype(jnp.bfloat16)


def draw_w_qkv(key, part):
    key = jax.random.fold_in(key, 23)
    base = jnp.clip(jax.random.normal(key, (C, 3 * C), jnp.float32), -2.5, 2.5) * C ** (-0.5)
    return base.astype(jnp.bfloat16)


def block_scale(rng, dims, split, least, top_value):
    loudness = 1.0
    for dim, parts in split:
        steps = jax.random.uniform(jax.random.fold_in(jax.random.fold_in(rng, 6), dim), (parts,), jnp.float32, least / len(split), top_value / len(split))
        loudness = loudness * jnp.repeat(jnp.exp(steps), dims[dim] // parts).reshape((-1,) + (1,) * (len(dims) - 1 - dim))
    return loudness


def normal_values(key, extent, deviation, bound, split=(), dtype=jnp.bfloat16):
    result = deviation * jax.random.normal(key, extent, jnp.float32)
    if split:
        result = result * block_scale(key, extent, split, -0.22, 0.18)
    return jnp.clip(result, -bound, bound).astype(dtype)


def setup_inputs(seed: int = 0) -> dict:
    streams_of = jax.random.split(jax.random.key(seed), 11)
    coarse = draw_coarse(jax.random.fold_in(streams_of[10], 71), 0)
    norm1_gain = jnp.clip(1.0 + 0.15 * jax.random.normal(streams_of[1], (C,), jnp.float32), 0.25, 1.75)
    norm1_bias = normal_values(streams_of[2], (C,), 0.4, 2.5, (), jnp.float32)
    w_qkv = draw_w_qkv(jax.random.fold_in(streams_of[10], 71), 0)
    w_proj = normal_values(streams_of[4], (C, C), C ** -0.5, 0.375)
    second_norm2_gain = jnp.clip(1.0 + 0.15 * jax.random.normal(streams_of[5], (C,), jnp.float32), 0.25, 1.75)
    second_norm2_bias = normal_values(streams_of[6], (C,), 0.4, 2.5, (), jnp.float32)
    conv_weight = normal_values(streams_of[7], (3, 3, C, C), (9 * C) ** -0.5, 0.125)
    conv_bias = normal_values(streams_of[8], (C,), 0.4, 2.5, (), jnp.float32)
    cotangent = normal_values(streams_of[9], (FH, FW, C), 1.0, 6.0, ((0, 4), (1, 32)))
    return dict(coarse=coarse, norm1_gain=norm1_gain, norm1_bias=norm1_bias, w_qkv=w_qkv, w_proj=w_proj, second_norm2_gain=second_norm2_gain, second_norm2_bias=second_norm2_bias, conv_weight=conv_weight, conv_bias=conv_bias, cotangent=cotangent)


EPS = 1e-05

def group_statistics(values):
    cells = values.shape[0] * values.shape[1]
    grouped = values.reshape(cells, GROUPS, C // GROUPS)
    centre = lax.optimization_barrier(jnp.mean(grouped, axis=(0, 2)))
    centered = grouped - centre[None, :, None]
    spread = lax.optimization_barrier(jnp.mean(centered * centered, axis=(0, 2)))
    inverse = lax.rsqrt(spread + EPS)
    normed = (centered * inverse[None, :, None]).reshape(values.shape)
    return (normed, jnp.repeat(inverse, C // GROUPS))

def upsample(padded):
    upper_even = 0.25 * padded[:-2] + 0.75 * padded[1:-1]
    upper_odd = 0.75 * padded[1:-1] + 0.25 * padded[2:]
    rows_done = jnp.stack([upper_even, upper_odd], axis=1).reshape((-1,) + padded.shape[1:])
    left_even = 0.25 * rows_done[:, :-2] + 0.75 * rows_done[:, 1:-1]
    right_odd = 0.75 * rows_done[:, 1:-1] + 0.25 * rows_done[:, 2:]
    return jnp.stack([left_even, right_odd], axis=2).reshape(rows_done.shape[0], -1, padded.shape[2])

def head_attention(triple):
    queries, keys, values = triple
    length = queries.shape[0]
    block = 512 if length % 512 == 0 else length

    def one_block(query_block):
        scores = jnp.dot(query_block, keys.T, preferred_element_type=jnp.float32) * HD ** (-0.5)
        top = lax.optimization_barrier(jnp.max(scores, axis=1, keepdims=True))
        weights = jnp.exp(scores - top)
        total = lax.optimization_barrier(jnp.sum(weights, axis=1, keepdims=True))
        mixed = jnp.dot(weights.astype(jnp.bfloat16), values, preferred_element_type=jnp.float32)
        return mixed / total
    return lax.map(one_block, queries.reshape(length // block, block, HD)).reshape(length, HD)

def reference(coarse, norm1_gain, norm1_bias, w_qkv, w_proj, second_norm2_gain, second_norm2_bias, conv_weight, conv_bias, cotangent):
    tokens = HC * WC
    base = coarse.astype(jnp.float32)
    normed1, unused = group_statistics(base)
    normed1 = (normed1 * norm1_gain + norm1_bias).astype(jnp.bfloat16).reshape(tokens, C)
    triple = jnp.dot(normed1, w_qkv, preferred_element_type=jnp.float32).astype(jnp.bfloat16)
    per_head = jnp.transpose(triple.reshape(tokens, 3, HEADS, HD), (1, 2, 0, 3))
    attended = lax.map(head_attention, (per_head[0], per_head[1], per_head[2]))
    attended = jnp.transpose(attended.astype(jnp.bfloat16), (1, 0, 2)).reshape(tokens, C)
    merged = (base.reshape(tokens, C) + jnp.dot(attended, w_proj, preferred_element_type=jnp.float32)).astype(jnp.bfloat16)
    merged = merged.reshape(HC, WC, C)
    upsampled_field = upsample(jnp.pad(merged.astype(jnp.float32), ((1, 1), (1, 1), (0, 0))))
    normalized_input2, inverse_deviation2 = group_statistics(upsampled_field)
    offset_values = normalized_input2 * second_norm2_gain + second_norm2_bias
    hidden = jax.nn.silu(offset_values).astype(jnp.bfloat16)
    fine_rows, fine_cols = (upsampled_field.shape[0], upsampled_field.shape[1])
    hidden_pad = jnp.pad(hidden, ((1, 1), (1, 1), (0, 0)))
    grad_pad = jnp.pad(cotangent, ((1, 1), (1, 1), (0, 0)))
    output = jnp.zeros((fine_rows * fine_cols, C), jnp.float32) + conv_bias
    grad_hidden = jnp.zeros((fine_rows * fine_cols, C), jnp.float32)
    flat_grad = cotangent.reshape(-1, C)
    weight_rows = []
    for tap_row in range(3):
        weight_cols = []
        for tap_col in range(3):
            window = hidden_pad[tap_row:tap_row + fine_rows, tap_col:tap_col + fine_cols].reshape(-1, C)
            output = output + jnp.dot(window, conv_weight[tap_row, tap_col], preferred_element_type=jnp.float32)
            weight_cols.append(jnp.dot(window.T, flat_grad, preferred_element_type=jnp.float32))
            back_window = grad_pad[2 - tap_row:2 - tap_row + fine_rows, 2 - tap_col:2 - tap_col + fine_cols].reshape(-1, C)
            grad_hidden = grad_hidden + jnp.dot(back_window, conv_weight[tap_row, tap_col].T, preferred_element_type=jnp.float32)
        weight_rows.append(jnp.stack(weight_cols))
    root = jnp.sqrt(jnp.float32(fine_rows * fine_cols))
    grad_conv = jnp.stack(weight_rows) / root
    fine_out = output.astype(jnp.bfloat16).reshape(fine_rows, fine_cols, C)
    grad_hidden = grad_hidden.reshape(fine_rows, fine_cols, C)
    sigmoid_value = jax.nn.sigmoid(offset_values)
    gradient_of_offset = grad_hidden * sigmoid_value * (1.0 + offset_values * (1.0 - sigmoid_value))
    weighted_sum_total = lax.optimization_barrier(jnp.sum(gradient_of_offset * normalized_input2, axis=(0, 1)))
    sum_b = lax.optimization_barrier(jnp.sum(gradient_of_offset, axis=(0, 1)))
    grad_norm = jnp.stack([weighted_sum_total, sum_b]) / root
    count = jnp.float32(fine_rows * fine_cols * (C // GROUPS))
    mean_over_bias = jnp.repeat(lax.optimization_barrier(jnp.sum((second_norm2_gain * sum_b).reshape(GROUPS, -1), axis=1)) / count, C // GROUPS)
    mean_over_weight = jnp.repeat(lax.optimization_barrier(jnp.sum((second_norm2_gain * weighted_sum_total).reshape(GROUPS, -1), axis=1)) / count, C // GROUPS)
    gradient_upsampled_field = (inverse_deviation2 * (gradient_of_offset * second_norm2_gain - mean_over_bias - normalized_input2 * mean_over_weight)).astype(jnp.bfloat16)
    return (fine_out, gradient_upsampled_field, grad_conv, grad_norm)
```

```python
import functools

import jax
import jax.numpy as jnp
import numpy as np
from jax import lax
from jax.experimental import pallas as pl
from jax.experimental.pallas import tpu as pltpu
from jax.sharding import Mesh, PartitionSpec as P

HEADS = 4
HD = 64
C = 256
SHARE = 8
EPS = 1e-05
F32 = jnp.float32
BF16 = jnp.bfloat16
VMEM_LIMIT = 50 * 2**20
ZXC = ("z", "x", "c")
ALL = ("y", "z", "x", "c")

CELLS_IN = 192
FINE_ROWS = 34
WIN = FINE_ROWS * 16


def upsample_matrix():
    def line(f):
        i = f // 2
        return {i: 0.75, (i - 1 if f % 2 == 0 else i + 1): 0.25}

    table = np.zeros((3, FINE_ROWS, 16, CELLS_IN), np.float32)
    for b in range(3):
        for fr in range(FINE_ROWS):
            for j in range(16):
                for r, wr in line(fr - 1).items():
                    for c, wc in line(j + b - 1).items():
                        table[b, fr, j, (r + 1) * 10 + c + 1] += wr * wc
    return table.reshape(3 * WIN, CELLS_IN)


UPSAMPLE = upsample_matrix()


def params(grid=None):
    return pltpu.CompilerParams(
        vmem_limit_bytes=VMEM_LIMIT,
        dimension_semantics=None if grid is None else ("arbitrary",) * grid,
    )


def dot(a, b, contract=((1,), (0,))):
    return lax.dot_general(a, b, (contract, ((), ())), preferred_element_type=F32)


def dot_exact(a, b, contract=((1,), (0,))):
    return lax.dot_general(
        a, b, (contract, ((), ())), preferred_element_type=F32, precision=lax.Precision.HIGHEST
    )


def iota(shape, dim):
    return lax.broadcasted_iota(jnp.int32, shape, dim)


def group_row(mean_c, var_c):
    same = jnp.where((iota((C, C), 0) >> 3) == (iota((C, C), 1) >> 3), 1.0 / SHARE, 0.0)
    mean8 = jnp.broadcast_to(mean_c, (8, C))
    spread = mean8 - dot_exact(mean8, same)
    var8 = jnp.broadcast_to(var_c, (8, C)) + spread * spread
    lane = iota((C, 128), 1)
    group = iota((C, 128), 0) >> 3
    to_mean = jnp.where(lane == group, 1.0 / SHARE, 0.0)
    to_var = jnp.where(lane == group + 32, 1.0 / SHARE, 0.0)
    return dot_exact(mean8, to_mean) + dot_exact(var8, to_var)


def combine_groups(rows):
    count = rows.shape[0]
    mean = jnp.sum(rows, axis=0, keepdims=True) / count
    off = rows - mean
    scatter = jnp.sum(off * off, axis=0, keepdims=True) / count
    group = iota((128, C), 1) >> 3
    lane = iota((128, C), 0)
    from_mean = jnp.where(lane == group, 1.0, 0.0)
    from_var = jnp.where(lane == group + 32, 1.0, 0.0)
    mean8 = jnp.broadcast_to(mean, (8, 128))
    scatter8 = jnp.broadcast_to(scatter, (8, 128))
    mean_c = dot_exact(mean8, from_mean)
    var_c = dot_exact(mean8, from_var) + dot_exact(scatter8, from_mean)
    return mean_c[:1], lax.rsqrt(var_c + EPS)[:1]


def split3(value):
    high = value.astype(BF16)
    rest = value - high.astype(F32)
    middle = rest.astype(BF16)
    low = (rest - middle.astype(F32)).astype(BF16)
    return high, middle, low


def channel_stats(value):
    count = value.shape[0]
    mean = jnp.sum(value, axis=0, keepdims=True) / count
    off = value - mean
    return mean, jnp.sum(off * off, axis=0, keepdims=True) / count


def stats_kernel(a, b, c, d, out):
    parts = [r[...].astype(F32) for r in (a, b, c, d)]
    count = 4 * parts[0].shape[0]
    mean = sum(jnp.sum(p, axis=0, keepdims=True) for p in parts) / count
    var = 0.0
    for p in parts:
        off = p - mean
        var = var + jnp.sum(off * off, axis=0, keepdims=True)
    out[...] = group_row(mean, var / count)


def local_stats(pieces):
    return pl.pallas_call(
        stats_kernel,
        out_shape=jax.ShapeDtypeStruct((8, 128), F32),
        compiler_params=params(),
    )(*pieces)


def attention_kernel(
    order, q_ref, k0, k1, k2, k3, s0, s1, s2, s3, gain, bias, w_qkv, out, keys, values, norm
):
    step = pl.program_id(0)

    @pl.when(step == 0)
    def _():
        rows = jnp.concatenate([s0[...], s1[...], s2[...], s3[...]], axis=0)
        mean, inverse = combine_groups(rows)
        norm[0:1, :] = mean
        norm[1:2, :] = inverse
        for i, piece in enumerate((k0, k1, k2, k3)):
            normed = (piece[...].astype(F32) - mean) * inverse
            normed = (normed * gain[...] + bias[...]).astype(BF16)
            both = dot(normed, w_qkv[:, C:])
            size = piece.shape[0]
            keys[pl.ds(i * size, size), :] = both[:, :C].astype(BF16)
            values[pl.ds(i * size, size), :] = both[:, C:].astype(BF16)

    normed = (q_ref[0].astype(F32) - norm[0:1, :]) * norm[1:2, :]
    normed = (normed * gain[...] + bias[...]).astype(BF16)
    queries = dot(normed, w_qkv[:, :C]).astype(BF16) * jnp.asarray(HD**-0.5, BF16)
    head_of = iota((CELLS_IN, C), 1) >> 6
    lane = iota((CELLS_IN, 128), 1)
    result = jnp.zeros((CELLS_IN, C), F32)
    logs = jnp.zeros((CELLS_IN, 128), F32)
    for head in range(HEADS):
        mine = head_of == head
        masked = jnp.where(mine, queries, jnp.zeros_like(queries))
        scores = dot(masked, keys[...], ((1,), (1,)))
        top = jnp.max(scores, axis=1, keepdims=True)
        weights = jnp.exp(scores - top)
        total = jnp.sum(weights, axis=1, keepdims=True)
        mixed = dot(weights.astype(BF16), values[...])
        result = jnp.where(mine, mixed / total, result)
        logs = jnp.where(lane == head, top + jnp.log(total), logs)
    out[0, :CELLS_IN, :] = result.astype(BF16)
    turned = jnp.concatenate([logs.T[:8], jnp.zeros((8, 64), F32)], axis=1)
    high, middle, low = split3(turned)
    line = iota((16, C), 0)
    packed = jnp.zeros((16, C), F32)
    for i, part in enumerate((high, middle, low)):
        wide = part.astype(F32)
        wide = jnp.concatenate([wide, wide], axis=0)
        if i:
            wide = pltpu.roll(wide, 4 * i, 0)
        packed = jnp.where((line >= 4 * i) & (line < 4 * i + 4), wide, packed)
    out[0, CELLS_IN:, :] = packed.astype(BF16)


def partial_attention(order, queries, pieces, stats, gain, bias, w_qkv):
    whole = lambda shape: pl.BlockSpec(shape, lambda i, o: (0,) * len(shape))
    key_count = sum(p.shape[0] for p in pieces)
    return pl.pallas_call(
        attention_kernel,
        out_shape=jax.ShapeDtypeStruct((8, CELLS_IN + 16, C), BF16),
        grid_spec=pltpu.PrefetchScalarGridSpec(
            num_scalar_prefetch=1,
            grid=(8,),
            in_specs=[pl.BlockSpec((1, CELLS_IN, C), lambda i, o: (i, 0, 0))]
            + [whole(p.shape) for p in pieces]
            + [whole(s.shape) for s in stats]
            + [whole((1, C)), whole((1, C)), whole(w_qkv.shape)],
            out_specs=pl.BlockSpec((1, CELLS_IN + 16, C), lambda i, o: (o[i], 0, 0)),
            scratch_shapes=[
                pltpu.VMEM((key_count, C), BF16),
                pltpu.VMEM((key_count, C), BF16),
                pltpu.VMEM((8, C), F32),
            ],
        ),
        compiler_params=params(1),
    )(order, queries, *pieces, *stats, gain, bias, w_qkv)


def merge_kernel(flags, parts, coarse, w_proj, up, merged_out, stats_out):
    count = parts.shape[0]
    logs = []
    for i in range(count):
        tail = parts[i, CELLS_IN:, :].astype(F32)
        logs.append(tail[0:4] + tail[4:8] + tail[8:12])
    top = functools.reduce(jnp.maximum, logs)
    shares = [jnp.exp(v - top) for v in logs]
    total = sum(shares)
    spread = jnp.where((iota((8, C), 1) >> 6) == iota((8, C), 0), 1.0, 0.0)
    attended = jnp.zeros((CELLS_IN, C), F32)
    for i in range(count):
        share = shares[i] / total
        share = jnp.concatenate([share, jnp.zeros_like(share)], axis=0)[:, :CELLS_IN]
        wide = dot_exact(share, spread, ((0,), (0,)))
        attended = attended + wide * parts[i, :CELLS_IN, :].astype(F32)
    merged = coarse[...].astype(F32) + dot(attended.astype(BF16), w_proj[...])
    cell = iota((CELLS_IN, C), 0)
    col = lax.rem(cell, 10)
    outside = (
        ((cell < 10) & (flags[0] == 1))
        | ((cell >= 170) & (flags[1] == 1))
        | ((col == 0) & (flags[2] == 1))
        | ((col == 9) & (flags[3] == 1))
        | (cell >= 180)
    )
    merged = jnp.where(outside, 0.0, merged).astype(BF16)
    merged_out[...] = merged
    field = dot(up[WIN + 16 : WIN + 528, :], merged)
    mean, var = channel_stats(field)
    stats_out[...] = jnp.broadcast_to(group_row(mean, var)[:1], stats_out.shape)


def merge(flags, parts, coarse, w_proj, up):
    vmem = pl.BlockSpec(memory_space=pltpu.VMEM)
    return pl.pallas_call(
        merge_kernel,
        out_shape=(
            jax.ShapeDtypeStruct((CELLS_IN, C), BF16),
            jax.ShapeDtypeStruct((128, 128), F32),
        ),
        in_specs=[pl.BlockSpec(memory_space=pltpu.SMEM)] + [vmem] * 4,
        out_specs=(vmem, vmem),
        compiler_params=params(),
    )(flags, parts, coarse, w_proj, up)


def back_kernel(c0, c1, c2, weight, out):
    windows = (c0, c1, c2)
    total = jnp.zeros((512, C), F32)
    for a in range(3):
        for b in range(3):
            window = windows[2 - b][16 * (2 - a) : 16 * (2 - a) + 512, :]
            total = total + dot(window, weight[3 * a + b], ((1,), (1,)))
    out[...] = total


def back_conv(windows, weight):
    return pl.pallas_call(
        back_kernel,
        out_shape=jax.ShapeDtypeStruct((512, C), F32),
        compiler_params=params(),
        cost_estimate=pl.CostEstimate(
            flops=9 * 2 * 512 * C * C, bytes_accessed=3 * 10**6, transcendentals=0
        ),
    )(*windows, weight)


def conv_kernel(
    flags,
    merged,
    up,
    stats,
    gain,
    bias,
    weight,
    conv_bias,
    cot,
    grad_hidden,
    fine_out,
    halves,
    shift_out,
    xhat_out,
    inverse_out,
    hid0,
    hid1,
    hid2,
):
    mean, inverse = combine_groups(stats[...])
    inverse_out[...] = jnp.broadcast_to(inverse, (8, C))
    hidden = (hid0, hid1, hid2)
    row = iota((WIN, C), 0)
    col = row & 15
    for b in range(3):
        field = dot(up[b * WIN : (b + 1) * WIN, :], merged[...])
        xhat = (field - mean) * inverse
        shifted = xhat * gain[...] + bias[...]
        sig = 1.0 / (1.0 + jnp.exp(-shifted))
        outside = ((row < 16) & (flags[0] == 1)) | ((row >= 528) & (flags[1] == 1))
        if b == 0:
            outside = outside | ((col == 0) & (flags[2] == 1))
        if b == 2:
            outside = outside | ((col == 15) & (flags[3] == 1))
        hidden[b][...] = jnp.where(outside, 0.0, shifted * sig).astype(BF16)
        if b == 1:
            inner = slice(16, 528)
            s, t = sig[inner], shifted[inner]
            grad_shift = grad_hidden[...] * s * (1.0 + t * (1.0 - s))
            shift_out[...] = grad_shift
            xhat_out[...] = xhat[inner]
            sum_w = jnp.sum(grad_shift * xhat[inner], axis=0, keepdims=True)
            sum_b = jnp.sum(grad_shift, axis=0, keepdims=True)
            rows = []
            for part in range(3):
                for value in (sum_w, sum_b):
                    piece = split3(value)[part].astype(F32)
                    rows += [piece[:, :128], piece[:, 128:]]
            tail = jnp.concatenate(rows + [jnp.zeros((4, 128), F32)], axis=0).astype(BF16)
            halves[0, 2304:, :] = tail
            halves[1, 2304:, :] = tail
    total = jnp.zeros((512, C), F32) + conv_bias[...]
    for a in range(3):
        for b in range(3):
            tap = 3 * a + b
            window = hidden[b][16 * a : 16 * a + 512, :]
            total = total + dot(window, weight[tap])
            product = dot(window, cot[...], ((0,), (0,)))
            halves[0, tap * C : (tap + 1) * C, :] = product[:, :128].astype(BF16)
            halves[1, tap * C : (tap + 1) * C, :] = product[:, 128:].astype(BF16)
    fine_out[...] = total.astype(BF16)


def conv(flags, merged, up, stats, gain, bias, weight, conv_bias, cot, grad_hidden):
    vmem = pl.BlockSpec(memory_space=pltpu.VMEM)
    return pl.pallas_call(
        conv_kernel,
        out_shape=(
            jax.ShapeDtypeStruct((512, C), BF16),
            jax.ShapeDtypeStruct((2, 2320, 128), BF16),
            jax.ShapeDtypeStruct((512, C), F32),
            jax.ShapeDtypeStruct((512, C), F32),
            jax.ShapeDtypeStruct((8, C), F32),
        ),
        in_specs=[pl.BlockSpec(memory_space=pltpu.SMEM)] + [vmem] * 9,
        out_specs=(vmem,) * 5,
        scratch_shapes=[pltpu.VMEM((WIN, C), BF16)] * 3,
        compiler_params=params(),
    )(flags, merged, up, stats, gain, bias, weight, conv_bias, cot, grad_hidden)


def pair_kernel(kept, got, out, total):
    total[...] = kept[...].astype(F32) + got[...].astype(F32)
    tails = [r[2304:, :].astype(F32) for r in (kept, got)]
    sums = sum(t[0:4] + t[4:8] + t[8:12] for t in tails)
    parts = [p.astype(F32) for p in split3(sums)]
    tail = jnp.concatenate([jnp.zeros((36, 128), F32)] + parts, axis=0)
    own = iota((48, 128), 0) < 36
    for i in range(64):
        out[i] = jnp.where(own, total[36 * i : 36 * i + 48, :], tail).astype(BF16)


def pair_sum(kept, got):
    return pl.pallas_call(
        pair_kernel,
        out_shape=jax.ShapeDtypeStruct((64, 48, 128), BF16),
        scratch_shapes=[pltpu.VMEM((2320, 128), F32)],
        compiler_params=params(),
    )(kept, got)


def shift(value, axis, count, step):
    return lax.ppermute(value, axis, [((i + step) % count, i) for i in range(count)])


def line_halo(value, axis, count, dim):
    size = value.shape[dim]
    tail = lax.slice_in_dim(value, size - 1, size, axis=dim)
    head = lax.slice_in_dim(value, 0, 1, axis=dim)
    before = lax.ppermute(tail, axis, [(i, i + 1) for i in range(count - 1)])
    after = lax.ppermute(head, axis, [(i + 1, i) for i in range(count - 1)])
    return jnp.concatenate([before, value, after], axis=dim)


def per_device(
    coarse,
    norm1_gain,
    norm1_bias,
    w_qkv,
    w_proj,
    second_norm2_gain,
    second_norm2_bias,
    conv_weight,
    conv_bias,
    cotangent,
):
    y, c = lax.axis_index("y"), lax.axis_index("c")
    block = lax.axis_index(ZXC)
    flags = jnp.stack([y == 0, y == 3, block == 0, block == 31]).astype(jnp.int32)
    up = jnp.asarray(UPSAMPLE, BF16)
    taps = conv_weight.reshape(9, C, C)

    own = coarse.reshape(128, C)
    line = jnp.concatenate([own] + [shift(own, "x", 4, k) for k in (1, 3, 2)], axis=0)
    pieces = [line] + [shift(line, "z", 4, k) for k in (1, 3, 2)]

    wide = line_halo(coarse, ZXC, 32, 1)
    blocks = [wide] + [shift(wide, "y", 4, k) for k in (1, 2, 3)]
    around = []
    for k in range(4):
        cells = jnp.concatenate([blocks[k - 1][-1:], blocks[k], blocks[(k + 1) % 4][:1]], axis=0)
        around.append(jnp.pad(cells.reshape(180, C), ((0, CELLS_IN - 180), (0, 0))))
    mine = jnp.stack(around)
    queries = jnp.concatenate([mine, shift(mine, "c", 2, 1)], axis=0)
    order = jnp.stack(
        [((y + k) % 4) * 2 + (c + j) % 2 for j in range(2) for k in range(4)]
    ).astype(jnp.int32)

    grad = line_halo(line_halo(cotangent, "y", 4, 0), ZXC, 32, 1)
    windows = [grad[:, b : b + 16].reshape(WIN, C) for b in range(3)]
    grad_hidden = back_conv(windows, taps)

    stats = local_stats(pieces)
    stats = jnp.concatenate([stats, shift(stats, "c", 2, 1)], axis=0)
    stats = [stats] + [shift(stats, "y", 4, k) for k in (1, 2, 3)]
    partial = partial_attention(
        order, queries, pieces, stats, norm1_gain[None], norm1_bias[None], w_qkv
    )
    partial = lax.all_to_all(partial, ("y", "c"), 0, 0, tiled=True)
    merged, stats2 = merge(flags, partial, mine[0], w_proj, up)
    stats2 = lax.all_to_all(stats2.reshape(128, 1, 128), ALL, 0, 0, tiled=True)
    fine, halves, grad_shift, xhat, inverse = conv(
        flags,
        merged,
        up,
        stats2.reshape(128, 128),
        second_norm2_gain[None],
        second_norm2_bias[None],
        taps,
        conv_bias[None],
        cotangent.reshape(512, C),
        grad_hidden,
    )

    kept = lax.dynamic_index_in_dim(halves, c, 0, keepdims=False)
    given = lax.dynamic_index_in_dim(halves, 1 - c, 0, keepdims=False)
    sent = pair_sum(kept, shift(given, "c", 2, 1))
    got = lax.all_to_all(sent, ("y", "z", "x"), 0, 0, tiled=True)
    total = jnp.sum(got.astype(F32), axis=0)
    root = jnp.sqrt(jnp.float32(65536))
    sums = jnp.sum(total[36:].reshape(3, 2, C), axis=0)
    chunk = (total[:36] / root).astype(BF16)
    spread = lax.all_to_all(
        jnp.broadcast_to(chunk[None], (64, 36, 128)), ("y", "z", "x"), 0, 0, tiled=True
    ).reshape(2304, 128)
    other = shift(spread, "c", 2, 1)
    left = jnp.where(c == 0, spread, other)
    right = jnp.where(c == 0, other, spread)
    grad_conv = jnp.concatenate([left, right], axis=1).astype(F32).reshape(3, 3, C, C)
    grad_norm = sums / root

    count = jnp.float32(65536 * SHARE)
    per_group = (second_norm2_gain * sums).reshape(2, 32, SHARE).sum(axis=2) / count
    mean_w, mean_b = jnp.repeat(per_group, SHARE, axis=1)
    field = inverse[0] * (grad_shift * second_norm2_gain - mean_b - xhat * mean_w)
    return (
        fine.reshape(32, 16, C),
        field.astype(BF16).reshape(32, 16, C),
        grad_conv,
        grad_norm,
    )


def solution(mesh):
    split = Mesh(mesh.devices.reshape(4, 4, 4, 2), ALL)
    cells = P("y", ZXC, None)
    return jax.shard_map(
        per_device,
        mesh=split,
        in_specs=(cells,) + (P(),) * 8 + (cells,),
        out_specs=(cells, cells, P(), P()),
        check_vma=False,
    )
```

```python
import functools

import jax
import jax.numpy as jnp
import numpy as np
from jax import lax
from jax.experimental import pallas as pl
from jax.experimental.pallas import tpu as pltpu
from jax.sharding import Mesh, PartitionSpec as P

HEADS = 4
HD = 64
C = 256
SHARE = 8
EPS = 1e-05
F32 = jnp.float32
BF16 = jnp.bfloat16
VMEM_LIMIT = 50 * 2**20
ZXC = ("z", "x", "c")
ALL = ("y", "z", "x", "c")

CELLS_IN = 192
STRIP = 1200
FINE_ROWS = 34
WIN = FINE_ROWS * 16


def upsample_matrix():
    def line(f):
        i = f // 2
        return {i: 0.75, (i - 1 if f % 2 == 0 else i + 1): 0.25}

    table = np.zeros((3, FINE_ROWS, 16, CELLS_IN), np.float32)
    for b in range(3):
        for fr in range(FINE_ROWS):
            for j in range(16):
                for r, wr in line(fr - 1).items():
                    for c, wc in line(j + b - 1).items():
                        table[b, fr, j, (r + 1) * 10 + c + 1] += wr * wc
    return table.reshape(3 * WIN, CELLS_IN)


UPSAMPLE = upsample_matrix()


def params(grid=None):
    return pltpu.CompilerParams(
        vmem_limit_bytes=VMEM_LIMIT,
        dimension_semantics=None if grid is None else ("arbitrary",) * grid,
    )


def dot(a, b, contract=((1,), (0,))):
    return lax.dot_general(a, b, (contract, ((), ())), preferred_element_type=F32)


def dot_exact(a, b, contract=((1,), (0,))):
    return lax.dot_general(
        a, b, (contract, ((), ())), preferred_element_type=F32, precision=lax.Precision.HIGHEST
    )


def iota(shape, dim):
    return lax.broadcasted_iota(jnp.int32, shape, dim)


def group_row(mean_c, var_c):
    same = jnp.where((iota((C, C), 0) >> 3) == (iota((C, C), 1) >> 3), 1.0 / SHARE, 0.0)
    mean8 = jnp.broadcast_to(mean_c, (8, C))
    spread = mean8 - dot_exact(mean8, same)
    var8 = jnp.broadcast_to(var_c, (8, C)) + spread * spread
    lane = iota((C, 128), 1)
    group = iota((C, 128), 0) >> 3
    to_mean = jnp.where(lane == group, 1.0 / SHARE, 0.0)
    to_var = jnp.where(lane == group + 32, 1.0 / SHARE, 0.0)
    return dot_exact(mean8, to_mean) + dot_exact(var8, to_var)


def combine_groups(rows):
    count = rows.shape[0]
    mean = jnp.sum(rows, axis=0, keepdims=True) / count
    off = rows - mean
    scatter = jnp.sum(off * off, axis=0, keepdims=True) / count
    group = iota((128, C), 1) >> 3
    lane = iota((128, C), 0)
    from_mean = jnp.where(lane == group, 1.0, 0.0)
    from_var = jnp.where(lane == group + 32, 1.0, 0.0)
    mean8 = jnp.broadcast_to(mean, (8, 128))
    scatter8 = jnp.broadcast_to(scatter, (8, 128))
    mean_c = dot_exact(mean8, from_mean)
    var_c = dot_exact(mean8, from_var) + dot_exact(scatter8, from_mean)
    return mean_c[:1], lax.rsqrt(var_c + EPS)[:1]


def split3(value):
    high = value.astype(BF16)
    rest = value - high.astype(F32)
    middle = rest.astype(BF16)
    low = (rest - middle.astype(F32)).astype(BF16)
    return high, middle, low


def channel_stats(value):
    count = value.shape[0]
    mean = jnp.sum(value, axis=0, keepdims=True) / count
    off = value - mean
    return mean, jnp.sum(off * off, axis=0, keepdims=True) / count


def stats_kernel(cells, out):
    mean, var = channel_stats(cells[...].astype(F32))
    out[...] = jnp.broadcast_to(group_row(mean, var)[:1], out.shape)


def local_stats(cells):
    return pl.pallas_call(
        stats_kernel,
        out_shape=jax.ShapeDtypeStruct((128, 128), F32),
        compiler_params=params(),
    )(cells)


def attention_kernel(
    order, q_ref, k0, k1, k2, k3, stats, gain, bias, w_qkv, pick, out, keys, values, found, logs
):
    mean, inverse = combine_groups(stats[...])

    def norm(cells):
        normed = (cells.astype(F32) - mean) * inverse
        return (normed * gain[...] + bias[...]).astype(BF16)

    head_of = iota((512, C), 1) >> 6
    for i, piece in enumerate((k0, k1, k2, k3)):
        both = dot(norm(piece[...]), w_qkv[:, C:])
        rows = slice(512 * i, 512 * i + 512)
        keys[rows, :] = both[:, :C].astype(BF16)
        for head in range(HEADS):
            values[head, rows, :] = jnp.where(head_of == head, both[:, C:], 1.0).astype(BF16)

    scale = HD**-0.5 * float(np.log2(np.e))
    queries = (dot(norm(q_ref[...]), w_qkv[:, :C]) * scale).astype(BF16)
    head_of = iota((STRIP, C), 1) >> 6
    lane = iota((STRIP, 128), 1)
    result = jnp.zeros((STRIP, C), F32)
    packed = jnp.zeros((STRIP, 128), F32)
    for head in range(HEADS):
        mine = head_of == head
        masked = jnp.where(mine, queries, jnp.zeros_like(queries))
        best, mixed = None, None
        for i in range(4):
            rows = slice(512 * i, 512 * i + 512)
            scores = dot(masked, keys[rows, :], ((1,), (1,)))
            top = jnp.max(scores, axis=1, keepdims=True)
            fresh = top if i == 0 else jnp.maximum(best, top)
            product = dot(jnp.exp2(scores - fresh).astype(BF16), values[head, rows, :])
            mixed = product if i == 0 else mixed * jnp.exp2(best - fresh) + product
            best = fresh
        total = pltpu.roll(mixed, HD, 1)
        result = jnp.where(mine, mixed / total, result)
        spot = 0 if head else 128
        log = best + jnp.log2(mixed[:, spot : spot + 128])
        for part, value in enumerate(split3(log)):
            packed = jnp.where(lane == 4 * part + head, value.astype(F32), packed)
    found[...] = result.astype(BF16)
    logs[...] = packed.astype(BF16)
    for step in range(4):
        rows = slice(288 * step, 288 * step + 336)
        for side in range(2):
            chosen = pick[side]
            place = order[2 * step + side]
            out[place, :CELLS_IN, :] = dot(chosen, found[rows, :]).astype(BF16)
            turned = dot(logs[rows, :], chosen, ((0,), (1,)))[:16]
            turned = jnp.concatenate([turned, jnp.zeros((16, 64), F32)], axis=1)
            out[place, CELLS_IN:, :] = turned.astype(BF16)


def pick_matrix():
    table = np.zeros((2, CELLS_IN, 336), np.float32)
    for side in range(2):
        for r in range(18):
            for q in range(10):
                table[side, r * 10 + q, r * 18 + 8 * side + q] = 1.0
    return table


PICK = pick_matrix()


def partial_attention(order, queries, pieces, stats, gain, bias, w_qkv):
    vmem = pl.BlockSpec(memory_space=pltpu.VMEM)
    return pl.pallas_call(
        attention_kernel,
        out_shape=jax.ShapeDtypeStruct((8, CELLS_IN + 16, C), BF16),
        in_specs=[pl.BlockSpec(memory_space=pltpu.SMEM)] + [vmem] * 10,
        out_specs=vmem,
        scratch_shapes=[
            pltpu.VMEM((2048, C), BF16),
            pltpu.VMEM((HEADS, 2048, C), BF16),
            pltpu.VMEM((STRIP, C), BF16),
            pltpu.VMEM((STRIP, 128), BF16),
        ],
        compiler_params=params(),
    )(order, queries, *pieces, stats, gain, bias, w_qkv, jnp.asarray(PICK, BF16))


def merge_kernel(flags, parts, coarse, w_proj, up, merged_out, stats_out):
    count = parts.shape[0]
    logs = []
    for i in range(count):
        tail = parts[i, CELLS_IN:, :].astype(F32)
        logs.append(tail[0:4] + tail[4:8] + tail[8:12])
    top = functools.reduce(jnp.maximum, logs)
    shares = [jnp.exp2(v - top) for v in logs]
    total = sum(shares)
    spread = jnp.where((iota((8, C), 1) >> 6) == iota((8, C), 0), 1.0, 0.0)
    attended = jnp.zeros((CELLS_IN, C), F32)
    for i in range(count):
        share = shares[i] / total
        share = jnp.concatenate([share, jnp.zeros_like(share)], axis=0)[:, :CELLS_IN]
        wide = dot_exact(share, spread, ((0,), (0,)))
        attended = attended + wide * parts[i, :CELLS_IN, :].astype(F32)
    merged = coarse[...].astype(F32) + dot(attended.astype(BF16), w_proj[...])
    cell = iota((CELLS_IN, C), 0)
    col = lax.rem(cell, 10)
    outside = (
        ((cell < 10) & (flags[0] == 1))
        | ((cell >= 170) & (flags[1] == 1))
        | ((col == 0) & (flags[2] == 1))
        | ((col == 9) & (flags[3] == 1))
        | (cell >= 180)
    )
    merged = jnp.where(outside, 0.0, merged).astype(BF16)
    merged_out[...] = merged
    field = dot(up[WIN + 16 : WIN + 528, :], merged)
    mean, var = channel_stats(field)
    stats_out[...] = jnp.broadcast_to(group_row(mean, var)[:1], stats_out.shape)


def merge(flags, parts, coarse, w_proj, up):
    vmem = pl.BlockSpec(memory_space=pltpu.VMEM)
    return pl.pallas_call(
        merge_kernel,
        out_shape=(
            jax.ShapeDtypeStruct((CELLS_IN, C), BF16),
            jax.ShapeDtypeStruct((128, 128), F32),
        ),
        in_specs=[pl.BlockSpec(memory_space=pltpu.SMEM)] + [vmem] * 4,
        out_specs=(vmem, vmem),
        compiler_params=params(),
    )(flags, parts, coarse, w_proj, up)


def back_kernel(c0, c1, c2, weight, out):
    windows = (c0, c1, c2)
    total = jnp.zeros((512, C), F32)
    for a in range(3):
        for b in range(3):
            window = windows[2 - b][16 * (2 - a) : 16 * (2 - a) + 512, :]
            total = total + dot(window, weight[3 * a + b], ((1,), (1,)))
    out[...] = total


def back_conv(windows, weight):
    return pl.pallas_call(
        back_kernel,
        out_shape=jax.ShapeDtypeStruct((512, C), F32),
        compiler_params=params(),
        cost_estimate=pl.CostEstimate(
            flops=9 * 2 * 512 * C * C, bytes_accessed=3 * 10**6, transcendentals=0
        ),
    )(*windows, weight)


def conv_kernel(
    flags,
    merged,
    up,
    stats,
    gain,
    bias,
    weight,
    conv_bias,
    cot,
    grad_hidden,
    fine_out,
    halves,
    shift_out,
    xhat_out,
    inverse_out,
    hid0,
    hid1,
    hid2,
):
    mean, inverse = combine_groups(stats[...])
    inverse_out[...] = jnp.broadcast_to(inverse, (8, C))
    hidden = (hid0, hid1, hid2)
    row = iota((WIN, C), 0)
    col = row & 15
    for b in range(3):
        field = dot(up[b * WIN : (b + 1) * WIN, :], merged[...])
        xhat = (field - mean) * inverse
        shifted = xhat * gain[...] + bias[...]
        sig = 1.0 / (1.0 + jnp.exp(-shifted))
        outside = ((row < 16) & (flags[0] == 1)) | ((row >= 528) & (flags[1] == 1))
        if b == 0:
            outside = outside | ((col == 0) & (flags[2] == 1))
        if b == 2:
            outside = outside | ((col == 15) & (flags[3] == 1))
        hidden[b][...] = jnp.where(outside, 0.0, shifted * sig).astype(BF16)
        if b == 1:
            inner = slice(16, 528)
            s, t = sig[inner], shifted[inner]
            grad_shift = grad_hidden[...] * s * (1.0 + t * (1.0 - s))
            shift_out[...] = grad_shift
            xhat_out[...] = xhat[inner]
            sum_w = jnp.sum(grad_shift * xhat[inner], axis=0, keepdims=True)
            sum_b = jnp.sum(grad_shift, axis=0, keepdims=True)
            rows = []
            for part in range(3):
                for value in (sum_w, sum_b):
                    piece = split3(value)[part].astype(F32)
                    rows += [piece[:, :128], piece[:, 128:]]
            tail = jnp.concatenate(rows + [jnp.zeros((4, 128), F32)], axis=0).astype(BF16)
            halves[0, 2304:, :] = tail
            halves[1, 2304:, :] = tail
    total = jnp.zeros((512, C), F32) + conv_bias[...]
    for a in range(3):
        for b in range(3):
            tap = 3 * a + b
            window = hidden[b][16 * a : 16 * a + 512, :]
            total = total + dot(window, weight[tap])
            product = dot(window, cot[...], ((0,), (0,)))
            halves[0, tap * C : (tap + 1) * C, :] = product[:, :128].astype(BF16)
            halves[1, tap * C : (tap + 1) * C, :] = product[:, 128:].astype(BF16)
    fine_out[...] = total.astype(BF16)


def conv(flags, merged, up, stats, gain, bias, weight, conv_bias, cot, grad_hidden):
    vmem = pl.BlockSpec(memory_space=pltpu.VMEM)
    return pl.pallas_call(
        conv_kernel,
        out_shape=(
            jax.ShapeDtypeStruct((512, C), BF16),
            jax.ShapeDtypeStruct((2, 2320, 128), BF16),
            jax.ShapeDtypeStruct((512, C), F32),
            jax.ShapeDtypeStruct((512, C), F32),
            jax.ShapeDtypeStruct((8, C), F32),
        ),
        in_specs=[pl.BlockSpec(memory_space=pltpu.SMEM)] + [vmem] * 9,
        out_specs=(vmem,) * 5,
        scratch_shapes=[pltpu.VMEM((WIN, C), BF16)] * 3,
        compiler_params=params(),
    )(flags, merged, up, stats, gain, bias, weight, conv_bias, cot, grad_hidden)


def pair_kernel(kept, got, out, total):
    total[...] = kept[...].astype(F32) + got[...].astype(F32)
    tails = [r[2304:, :].astype(F32) for r in (kept, got)]
    sums = sum(t[0:4] + t[4:8] + t[8:12] for t in tails)
    parts = [p.astype(F32) for p in split3(sums)]
    tail = jnp.concatenate([jnp.zeros((36, 128), F32)] + parts, axis=0)
    own = iota((48, 128), 0) < 36
    for i in range(64):
        out[i] = jnp.where(own, total[36 * i : 36 * i + 48, :], tail).astype(BF16)


def pair_sum(kept, got):
    return pl.pallas_call(
        pair_kernel,
        out_shape=jax.ShapeDtypeStruct((64, 48, 128), BF16),
        scratch_shapes=[pltpu.VMEM((2320, 128), F32)],
        compiler_params=params(),
    )(kept, got)


def shift(value, axis, count, step):
    return lax.ppermute(value, axis, [((i + step) % count, i) for i in range(count)])


def line_halo(value, axis, count, dim):
    size = value.shape[dim]
    tail = lax.slice_in_dim(value, size - 1, size, axis=dim)
    head = lax.slice_in_dim(value, 0, 1, axis=dim)
    before = lax.ppermute(tail, axis, [(i, i + 1) for i in range(count - 1)])
    after = lax.ppermute(head, axis, [(i + 1, i) for i in range(count - 1)])
    return jnp.concatenate([before, value, after], axis=dim)


def per_device(
    coarse,
    norm1_gain,
    norm1_bias,
    w_qkv,
    w_proj,
    second_norm2_gain,
    second_norm2_bias,
    conv_weight,
    conv_bias,
    cotangent,
):
    y, c = lax.axis_index("y"), lax.axis_index("c")
    block = lax.axis_index(ZXC)
    flags = jnp.stack([y == 0, y == 3, block == 0, block == 31]).astype(jnp.int32)
    up = jnp.asarray(UPSAMPLE, BF16)
    taps = conv_weight.reshape(9, C, C)

    own = coarse.reshape(128, C)
    stats = local_stats(own)
    stats = lax.all_to_all(stats.reshape(128, 1, 128), ALL, 0, 0, tiled=True).reshape(128, 128)

    line = jnp.concatenate([own] + [shift(own, "x", 4, k) for k in (1, 3, 2)], axis=0)
    pieces = [line] + [shift(line, "z", 4, k) for k in (1, 3, 2)]

    wide = line_halo(coarse, ZXC, 32, 1)
    blocks = [wide] + [shift(wide, "y", 4, k) for k in (1, 2, 3)]
    rows = jnp.concatenate([blocks[3][-1:]] + blocks + [blocks[0][:1]], axis=0)
    other = shift(rows, "c", 2, 1)
    left = jnp.where(c == 0, rows, other)[:, :9]
    right = jnp.where(c == 0, other, rows)[:, 1:]
    queries = jnp.concatenate([left, right], axis=1).reshape(66 * 18, C)
    queries = jnp.pad(queries, ((0, STRIP - 66 * 18), (0, 0)))
    mine = jnp.pad(rows[:18].reshape(180, C), ((0, CELLS_IN - 180), (0, 0)))
    order = jnp.stack([((y + k) % 4) * 2 + j for k in range(4) for j in range(2)])
    order = order.astype(jnp.int32)

    grad = line_halo(line_halo(cotangent, "y", 4, 0), ZXC, 32, 1)
    windows = [grad[:, b : b + 16].reshape(WIN, C) for b in range(3)]
    grad_hidden = back_conv(windows, taps)

    partial = partial_attention(
        order, queries, pieces, stats, norm1_gain[None], norm1_bias[None], w_qkv
    )
    partial = lax.all_to_all(partial, ("y", "c"), 0, 0, tiled=True)
    merged, stats2 = merge(flags, partial, mine, w_proj, up)
    stats2 = lax.all_to_all(stats2.reshape(128, 1, 128), ALL, 0, 0, tiled=True)
    fine, halves, grad_shift, xhat, inverse = conv(
        flags,
        merged,
        up,
        stats2.reshape(128, 128),
        second_norm2_gain[None],
        second_norm2_bias[None],
        taps,
        conv_bias[None],
        cotangent.reshape(512, C),
        grad_hidden,
    )

    kept = lax.dynamic_index_in_dim(halves, c, 0, keepdims=False)
    given = lax.dynamic_index_in_dim(halves, 1 - c, 0, keepdims=False)
    sent = pair_sum(kept, shift(given, "c", 2, 1))
    got = lax.all_to_all(sent, ("y", "z", "x"), 0, 0, tiled=True)
    total = jnp.sum(got.astype(F32), axis=0)
    root = jnp.sqrt(jnp.float32(65536))
    sums = jnp.sum(total[36:].reshape(3, 2, C), axis=0)
    chunk = (total[:36] / root).astype(BF16)
    spread = lax.all_to_all(
        jnp.broadcast_to(chunk[None], (64, 36, 128)), ("y", "z", "x"), 0, 0, tiled=True
    ).reshape(2304, 128)
    other = shift(spread, "c", 2, 1)
    left = jnp.where(c == 0, spread, other)
    right = jnp.where(c == 0, other, spread)
    grad_conv = jnp.concatenate([left, right], axis=1).astype(F32).reshape(3, 3, C, C)
    grad_norm = sums / root

    count = jnp.float32(65536 * SHARE)
    per_group = (second_norm2_gain * sums).reshape(2, 32, SHARE).sum(axis=2) / count
    mean_w, mean_b = jnp.repeat(per_group, SHARE, axis=1)
    field = inverse[0] * (grad_shift * second_norm2_gain - mean_b - xhat * mean_w)
    return (
        fine.reshape(32, 16, C),
        field.astype(BF16).reshape(32, 16, C),
        grad_conv,
        grad_norm,
    )


def solution(mesh):
    split = Mesh(mesh.devices.reshape(4, 4, 4, 2), ALL)
    cells = P("y", ZXC, None)
    return jax.shard_map(
        per_device,
        mesh=split,
        in_specs=(cells,) + (P(),) * 8 + (cells,),
        out_specs=(cells, cells, P(), P()),
        check_vma=False,
    )
```

```python
import functools

import jax
import jax.numpy as jnp
import numpy as np
from jax import lax
from jax.experimental import pallas as pl
from jax.experimental.pallas import tpu as pltpu
from jax.sharding import Mesh, PartitionSpec as P

HEADS = 4
HD = 64
C = 256
SHARE = 8
EPS = 1e-05
F32 = jnp.float32
BF16 = jnp.bfloat16
VMEM_LIMIT = 50 * 2**20
ZXC = ("z", "x", "c")
ALL = ("y", "z", "x", "c")

CELLS_IN = 192
STRIP = 672
KEY_BLOCK = 512
FINE_ROWS = 34
WIN = FINE_ROWS * 16


def upsample_matrix():
    def line(f):
        i = f // 2
        return {i: 0.75, (i - 1 if f % 2 == 0 else i + 1): 0.25}

    table = np.zeros((3, FINE_ROWS, 16, CELLS_IN), np.float32)
    for b in range(3):
        for fr in range(FINE_ROWS):
            for j in range(16):
                for r, wr in line(fr - 1).items():
                    for c, wc in line(j + b - 1).items():
                        table[b, fr, j, (r + 1) * 10 + c + 1] += wr * wc
    return table.reshape(3 * WIN, CELLS_IN)


UPSAMPLE = upsample_matrix()


def params(grid=None):
    return pltpu.CompilerParams(
        vmem_limit_bytes=VMEM_LIMIT,
        dimension_semantics=None if grid is None else ("arbitrary",) * grid,
    )


def dot(a, b, contract=((1,), (0,))):
    return lax.dot_general(a, b, (contract, ((), ())), preferred_element_type=F32)


def dot_exact(a, b, contract=((1,), (0,))):
    return lax.dot_general(
        a, b, (contract, ((), ())), preferred_element_type=F32, precision=lax.Precision.HIGHEST
    )


def iota(shape, dim):
    return lax.broadcasted_iota(jnp.int32, shape, dim)


def group_row(mean_c, var_c):
    same = jnp.where((iota((C, C), 0) >> 3) == (iota((C, C), 1) >> 3), 1.0 / SHARE, 0.0)
    mean8 = jnp.broadcast_to(mean_c, (8, C))
    spread = mean8 - dot_exact(mean8, same)
    var8 = jnp.broadcast_to(var_c, (8, C)) + spread * spread
    lane = iota((C, 128), 1)
    group = iota((C, 128), 0) >> 3
    to_mean = jnp.where(lane == group, 1.0 / SHARE, 0.0)
    to_var = jnp.where(lane == group + 32, 1.0 / SHARE, 0.0)
    return dot_exact(mean8, to_mean) + dot_exact(var8, to_var)


def combine_groups(rows):
    count = rows.shape[0]
    mean = jnp.sum(rows, axis=0, keepdims=True) / count
    off = rows - mean
    scatter = jnp.sum(off * off, axis=0, keepdims=True) / count
    group = iota((128, C), 1) >> 3
    lane = iota((128, C), 0)
    from_mean = jnp.where(lane == group, 1.0, 0.0)
    from_var = jnp.where(lane == group + 32, 1.0, 0.0)
    mean8 = jnp.broadcast_to(mean, (8, 128))
    scatter8 = jnp.broadcast_to(scatter, (8, 128))
    mean_c = dot_exact(mean8, from_mean)
    var_c = dot_exact(mean8, from_var) + dot_exact(scatter8, from_mean)
    return mean_c[:1], lax.rsqrt(var_c + EPS)[:1]


def split3(value):
    high = value.astype(BF16)
    rest = value - high.astype(F32)
    middle = rest.astype(BF16)
    low = (rest - middle.astype(F32)).astype(BF16)
    return high, middle, low


def channel_stats(value):
    count = value.shape[0]
    mean = jnp.sum(value, axis=0, keepdims=True) / count
    off = value - mean
    return mean, jnp.sum(off * off, axis=0, keepdims=True) / count


def stats_kernel(mine, other, out):
    parts = [r[...].astype(F32) for r in (mine, other)]
    count = 2 * parts[0].shape[0]
    mean = sum(jnp.sum(p, axis=0, keepdims=True) for p in parts) / count
    var = 0.0
    for part in parts:
        off = part - mean
        var = var + jnp.sum(off * off, axis=0, keepdims=True)
    out[...] = group_row(mean, var / count)


def local_stats(mine, other):
    return pl.pallas_call(
        stats_kernel,
        out_shape=jax.ShapeDtypeStruct((8, 128), F32),
        compiler_params=params(),
    )(mine, other)


def attention_kernel(
    order, q_ref, mine, other, s0, s1, s2, s3, gain, bias, w_qkv, out, keys, values
):
    stats = jnp.concatenate([s0[...], s1[...], s2[...], s3[...]], axis=0)
    mean, inverse = combine_groups(stats)

    def norm(cells):
        normed = (cells.astype(F32) - mean) * inverse
        return (normed * gain[...] + bias[...]).astype(BF16)

    head_of = iota((512, C), 1) >> 6
    for i in range(8):
        rows = slice(512 * i, 512 * i + 512)
        cells = (mine, other)[i // 4][512 * (i % 4) : 512 * (i % 4) + 512, :]
        both = dot(norm(cells), w_qkv[:, C:])
        keys[rows, :] = both[:, :C].astype(BF16)
        for head in range(HEADS):
            values[head, rows, :] = jnp.where(head_of == head, both[:, C:], 1.0).astype(BF16)

    scale = HD**-0.5 * float(np.log2(np.e))
    queries = (dot(norm(q_ref[...]), w_qkv[:, :C]) * scale).astype(BF16)
    head_of = iota((STRIP, C), 1) >> 6
    lane = iota((STRIP, 128), 1)
    result = jnp.zeros((STRIP, C), F32)
    packed = jnp.zeros((STRIP, 128), F32)
    for head in range(HEADS):
        own = head_of == head
        masked = jnp.where(own, queries, jnp.zeros_like(queries))
        best, mixed = None, None
        for i in range(4096 // KEY_BLOCK):
            rows = slice(KEY_BLOCK * i, KEY_BLOCK * (i + 1))
            scores = dot(masked, keys[rows, :], ((1,), (1,)))
            top = jnp.max(scores, axis=1, keepdims=True)
            fresh = top if i == 0 else jnp.maximum(best, top)
            product = dot(jnp.exp2(scores - fresh).astype(BF16), values[head, rows, :])
            mixed = product if i == 0 else mixed * jnp.exp2(best - fresh) + product
            best = fresh
        result = jnp.where(own, mixed / pltpu.roll(mixed, HD, 1), result)
        spot = 0 if head else 128
        log = best + jnp.log2(mixed[:, spot : spot + 128])
        for part, value in enumerate(split3(log)):
            packed = jnp.where(lane == 4 * part + head, value.astype(F32), packed)
    result = result.astype(BF16)
    for step in range(4):
        rows = slice(160 * step, 160 * step + CELLS_IN)
        place = order[step]
        out[place, :CELLS_IN, :] = result[rows]
        turned = jnp.concatenate([packed[rows], jnp.zeros((64, 128), F32)], axis=0).T[:16]
        out[place, CELLS_IN:, :] = turned.astype(BF16)


def partial_attention(order, queries, mine, other, stats, gain, bias, w_qkv):
    vmem = pl.BlockSpec(memory_space=pltpu.VMEM)
    return pl.pallas_call(
        attention_kernel,
        out_shape=jax.ShapeDtypeStruct((4, CELLS_IN + 16, C), BF16),
        in_specs=[pl.BlockSpec(memory_space=pltpu.SMEM)] + [vmem] * 10,
        out_specs=vmem,
        scratch_shapes=[pltpu.VMEM((4096, C), BF16), pltpu.VMEM((HEADS, 4096, C), BF16)],
        compiler_params=params(),
    )(order, queries, mine, other, *stats, gain, bias, w_qkv)


def merge_kernel(flags, parts, coarse, w_proj, up, merged_out, stats_out):
    count = parts.shape[0]
    logs = []
    for i in range(count):
        tail = parts[i, CELLS_IN:, :].astype(F32)
        logs.append(tail[0:4] + tail[4:8] + tail[8:12])
    top = functools.reduce(jnp.maximum, logs)
    shares = [jnp.exp2(v - top) for v in logs]
    total = sum(shares)
    spread = jnp.where((iota((8, C), 1) >> 6) == iota((8, C), 0), 1.0, 0.0)
    attended = jnp.zeros((CELLS_IN, C), F32)
    for i in range(count):
        share = shares[i] / total
        share = jnp.concatenate([share, jnp.zeros_like(share)], axis=0)[:, :CELLS_IN]
        wide = dot_exact(share, spread, ((0,), (0,)))
        attended = attended + wide * parts[i, :CELLS_IN, :].astype(F32)
    merged = coarse[...].astype(F32) + dot(attended.astype(BF16), w_proj[...])
    cell = iota((CELLS_IN, C), 0)
    col = lax.rem(cell, 10)
    outside = (
        ((cell < 10) & (flags[0] == 1))
        | ((cell >= 170) & (flags[1] == 1))
        | ((col == 0) & (flags[2] == 1))
        | ((col == 9) & (flags[3] == 1))
        | (cell >= 180)
    )
    merged = jnp.where(outside, 0.0, merged).astype(BF16)
    merged_out[...] = merged
    field = dot(up[WIN + 16 : WIN + 528, :], merged)
    mean, var = channel_stats(field)
    stats_out[...] = jnp.broadcast_to(group_row(mean, var)[:1], stats_out.shape)


def merge(flags, parts, coarse, w_proj, up):
    vmem = pl.BlockSpec(memory_space=pltpu.VMEM)
    return pl.pallas_call(
        merge_kernel,
        out_shape=(
            jax.ShapeDtypeStruct((CELLS_IN, C), BF16),
            jax.ShapeDtypeStruct((128, 128), F32),
        ),
        in_specs=[pl.BlockSpec(memory_space=pltpu.SMEM)] + [vmem] * 4,
        out_specs=(vmem, vmem),
        compiler_params=params(),
    )(flags, parts, coarse, w_proj, up)


def back_kernel(c0, c1, c2, weight, out):
    windows = (c0, c1, c2)
    total = jnp.zeros((512, C), F32)
    for a in range(3):
        for b in range(3):
            window = windows[2 - b][16 * (2 - a) : 16 * (2 - a) + 512, :]
            total = total + dot(window, weight[3 * a + b], ((1,), (1,)))
    out[...] = total


def back_conv(windows, weight):
    return pl.pallas_call(
        back_kernel,
        out_shape=jax.ShapeDtypeStruct((512, C), F32),
        compiler_params=params(),
        cost_estimate=pl.CostEstimate(
            flops=9 * 2 * 512 * C * C, bytes_accessed=3 * 10**6, transcendentals=0
        ),
    )(*windows, weight)


def hidden_kernel(
    flags,
    merged,
    up,
    stats,
    gain,
    bias,
    cot,
    grad_hidden,
    kept,
    given,
    hidden,
    shift_out,
    xhat_out,
    inverse_out,
):
    mean, inverse = combine_groups(stats[...])
    inverse_out[...] = jnp.broadcast_to(inverse, (8, C))
    row = iota((WIN, C), 0)
    col = row & 15
    for b in range(3):
        field = dot(up[b * WIN : (b + 1) * WIN, :], merged[...])
        xhat = (field - mean) * inverse
        shifted = xhat * gain[...] + bias[...]
        sig = 1.0 / (1.0 + jnp.exp(-shifted))
        outside = ((row < 16) & (flags[0] == 1)) | ((row >= 528) & (flags[1] == 1))
        if b == 0:
            outside = outside | ((col == 0) & (flags[2] == 1))
        if b == 2:
            outside = outside | ((col == 15) & (flags[3] == 1))
        hidden[b] = jnp.where(outside, 0.0, shifted * sig).astype(BF16)
        if b == 1:
            inner = slice(16, 528)
            s, t = sig[inner], shifted[inner]
            grad_shift = grad_hidden[...] * s * (1.0 + t * (1.0 - s))
            shift_out[...] = grad_shift
            xhat_out[...] = xhat[inner]
            sum_w = jnp.sum(grad_shift * xhat[inner], axis=0, keepdims=True)
            sum_b = jnp.sum(grad_shift, axis=0, keepdims=True)
            rows = []
            for part in range(3):
                for value in (sum_w, sum_b):
                    piece = split3(value)[part].astype(F32)
                    rows += [piece[:, :128], piece[:, 128:]]
            tail = jnp.concatenate(rows + [jnp.zeros((4, 128), F32)], axis=0).astype(BF16)
            kept[2304:, :] = tail
            given[2304:, :] = tail
    first = flags[4] == 0
    for a in range(3):
        for b in range(3):
            rows = slice((3 * a + b) * C, (3 * a + b + 1) * C)
            product = dot(hidden[b, 16 * a : 16 * a + 512, :], cot[...], ((0,), (0,)))
            left, right = product[:, :128].astype(BF16), product[:, 128:].astype(BF16)
            kept[rows, :] = jnp.where(first, left, right)
            given[rows, :] = jnp.where(first, right, left)


def hidden_and_kernel_gradient(flags, merged, up, stats, gain, bias, cot, grad_hidden):
    vmem = pl.BlockSpec(memory_space=pltpu.VMEM)
    return pl.pallas_call(
        hidden_kernel,
        out_shape=(
            jax.ShapeDtypeStruct((2320, 128), BF16),
            jax.ShapeDtypeStruct((2320, 128), BF16),
            jax.ShapeDtypeStruct((3, WIN, C), BF16),
            jax.ShapeDtypeStruct((512, C), F32),
            jax.ShapeDtypeStruct((512, C), F32),
            jax.ShapeDtypeStruct((8, C), F32),
        ),
        in_specs=[pl.BlockSpec(memory_space=pltpu.SMEM)] + [vmem] * 7,
        out_specs=(vmem,) * 6,
        compiler_params=params(),
    )(flags, merged, up, stats, gain, bias, cot, grad_hidden)


def conv_kernel(hidden, weight, conv_bias, fine_out):
    total = jnp.zeros((512, C), F32) + conv_bias[...]
    for a in range(3):
        for b in range(3):
            total = total + dot(hidden[b, 16 * a : 16 * a + 512, :], weight[3 * a + b])
    fine_out[...] = total.astype(BF16)


def conv(hidden, weight, conv_bias):
    return pl.pallas_call(
        conv_kernel,
        out_shape=jax.ShapeDtypeStruct((512, C), BF16),
        compiler_params=params(),
        cost_estimate=pl.CostEstimate(
            flops=9 * 2 * 512 * C * C, bytes_accessed=3 * 10**6, transcendentals=0
        ),
    )(hidden, weight, conv_bias)


def pair_kernel(kept, got, out, total):
    total[...] = kept[...].astype(F32) + got[...].astype(F32)
    tails = [r[2304:, :].astype(F32) for r in (kept, got)]
    sums = sum(t[0:4] + t[4:8] + t[8:12] for t in tails)
    parts = [p.astype(F32) for p in split3(sums)]
    tail = jnp.concatenate([jnp.zeros((36, 128), F32)] + parts, axis=0)
    own = iota((48, 128), 0) < 36
    for i in range(64):
        out[i] = jnp.where(own, total[36 * i : 36 * i + 48, :], tail).astype(BF16)


def pair_sum(kept, got):
    return pl.pallas_call(
        pair_kernel,
        out_shape=jax.ShapeDtypeStruct((64, 48, 128), BF16),
        scratch_shapes=[pltpu.VMEM((2320, 128), F32)],
        compiler_params=params(),
    )(kept, got)


def shift(value, axis, count, step):
    return lax.ppermute(value, axis, [((i + step) % count, i) for i in range(count)])


def per_device(
    coarse,
    norm1_gain,
    norm1_bias,
    w_qkv,
    w_proj,
    second_norm2_gain,
    second_norm2_bias,
    conv_weight,
    conv_bias,
    cotangent,
):
    y, c = lax.axis_index("y"), lax.axis_index("c")
    block = lax.axis_index(ZXC)
    flags = jnp.stack([y == 0, y == 3, block == 0, block == 31, c == 1]).astype(jnp.int32)
    up = jnp.asarray(UPSAMPLE, BF16)
    taps = conv_weight.reshape(9, C, C)

    own = coarse.reshape(128, C)
    cells = lax.all_to_all(
        jnp.broadcast_to(own[None], (16, 128, C)), ("z", "x"), 0, 0, tiled=True
    ).reshape(2048, C)

    first = jnp.concatenate([coarse[:, 0], cotangent[:, 0]], axis=0)
    last = jnp.concatenate([coarse[:, -1], cotangent[:, -1]], axis=0)
    before = lax.ppermute(last, ZXC, [(i, i + 1) for i in range(31)])[:, None]
    after = lax.ppermute(first, ZXC, [(i + 1, i) for i in range(31)])[:, None]
    wide = jnp.concatenate([before[:16], coarse, after[:16]], axis=1).reshape(160, C)
    grad = jnp.concatenate([before[16:], cotangent, after[16:]], axis=1)
    below = shift(jnp.concatenate([wide, grad[0]], axis=0), "y", 4, 1)
    above = shift(jnp.concatenate([wide, grad[-1]], axis=0), "y", 4, 3)
    blocks = [above[150:160], wide, below[:160], shift(wide, "y", 4, 2), above[:160], wide[:10]]
    queries = jnp.pad(jnp.concatenate(blocks, axis=0), ((0, STRIP - 660), (0, 0)))
    top = jnp.where(y == 0, 0, above[160:])[None].astype(BF16)
    bottom = jnp.where(y == 3, 0, below[160:])[None].astype(BF16)
    grad = jnp.concatenate([top, grad, bottom], axis=0)
    windows = [grad[:, b : b + 16].reshape(WIN, C) for b in range(3)]
    cells, queries = lax.optimization_barrier((cells, queries))
    other = shift(cells, "c", 2, 1)

    stats = local_stats(cells, other)
    stats = [stats] + [shift(stats, "y", 4, k) for k in (1, 2, 3)]
    order = jnp.stack([(y + k) % 4 for k in range(4)]).astype(jnp.int32)

    partial = partial_attention(
        order, queries, cells, other, stats, norm1_gain[None], norm1_bias[None], w_qkv
    )
    partial = lax.all_to_all(partial, "y", 0, 0, tiled=True)
    merged, stats2 = merge(flags, partial, queries[:CELLS_IN], w_proj, up)
    stats2 = lax.all_to_all(stats2.reshape(128, 1, 128), ALL, 0, 0, tiled=True)
    grad_hidden = back_conv(windows, taps)
    kept, given, hidden, grad_shift, xhat, inverse = hidden_and_kernel_gradient(
        flags,
        merged,
        up,
        stats2.reshape(128, 128),
        second_norm2_gain[None],
        second_norm2_bias[None],
        cotangent.reshape(512, C),
        grad_hidden,
    )

    sent = pair_sum(kept, shift(given, "c", 2, 1))
    sent, hidden = lax.optimization_barrier((sent, hidden))
    got = lax.all_to_all(sent, ("y", "z", "x"), 0, 0, tiled=True)
    fine = conv(hidden, taps, conv_bias[None])

    total = jnp.sum(got.astype(F32), axis=0)
    root = jnp.sqrt(jnp.float32(65536))
    chunk = (total[:36] / root).astype(BF16)
    spread = lax.all_to_all(
        jnp.broadcast_to(chunk[None], (64, 36, 128)), ("y", "z", "x"), 0, 0, tiled=True
    ).reshape(2304, 128)
    other = shift(spread, "c", 2, 1)
    left = jnp.where(c == 0, spread, other)
    right = jnp.where(c == 0, other, spread)
    grad_conv = jnp.concatenate([left, right], axis=1).astype(F32).reshape(3, 3, C, C)
    sums = jnp.sum(total[36:].reshape(3, 2, C), axis=0)
    grad_norm = sums / root

    count = jnp.float32(65536 * SHARE)
    per_group = (second_norm2_gain * sums).reshape(2, 32, SHARE).sum(axis=2) / count
    mean_w, mean_b = jnp.repeat(per_group, SHARE, axis=1)
    field = inverse[0] * (grad_shift * second_norm2_gain - mean_b - xhat * mean_w)
    return (
        fine.reshape(32, 16, C),
        field.astype(BF16).reshape(32, 16, C),
        grad_conv,
        grad_norm,
    )


def solution(mesh):
    split = Mesh(mesh.devices.reshape(4, 4, 4, 2), ALL)
    cells = P("y", ZXC, None)
    return jax.shard_map(
        per_device,
        mesh=split,
        in_specs=(cells,) + (P(),) * 8 + (cells,),
        out_specs=(cells, cells, P(), P()),
        check_vma=False,
    )
```

```python
import functools

import jax
import jax.numpy as jnp
import numpy as np
from jax import lax
from jax.experimental import pallas as pl
from jax.experimental.pallas import tpu as pltpu
from jax.sharding import Mesh, PartitionSpec as P

HEADS = 4
HD = 64
C = 256
SHARE = 8
EPS = 1e-05
F32 = jnp.float32
BF16 = jnp.bfloat16
VMEM_LIMIT = 50 * 2**20
HBM = pl.BlockSpec(memory_space=pltpu.HBM)
ZXC = ("z", "x", "c")
ALL = ("y", "z", "x", "c")

CELLS_IN = 192
STRIP = 672
KEY_BLOCK = 512
FINE_ROWS = 34
WIN = FINE_ROWS * 16


def upsample_matrix():
    def line(f):
        i = f // 2
        return {i: 0.75, (i - 1 if f % 2 == 0 else i + 1): 0.25}

    table = np.zeros((3, FINE_ROWS, 16, CELLS_IN), np.float32)
    for b in range(3):
        for fr in range(FINE_ROWS):
            for j in range(16):
                for r, wr in line(fr - 1).items():
                    for c, wc in line(j + b - 1).items():
                        table[b, fr, j, (r + 1) * 10 + c + 1] += wr * wc
    return table.reshape(3 * WIN, CELLS_IN)


UPSAMPLE = upsample_matrix()


def params(grid=None):
    return pltpu.CompilerParams(
        vmem_limit_bytes=VMEM_LIMIT,
        dimension_semantics=None if grid is None else ("arbitrary",) * grid,
    )


def in_hbm(value):
    return pltpu.with_memory_space_constraint(value, pltpu.HBM)


def dot(a, b, contract=((1,), (0,))):
    return lax.dot_general(a, b, (contract, ((), ())), preferred_element_type=F32)


def dot_exact(a, b):
    size = a.shape[0]
    parts = jnp.concatenate([p.astype(F32) for p in split3(a)], axis=0).astype(BF16)
    result = dot(parts, b.astype(BF16))
    return result[:size] + result[size : 2 * size] + result[2 * size :]


def iota(shape, dim):
    return lax.broadcasted_iota(jnp.int32, shape, dim)


def split3(value):
    high = value.astype(BF16)
    rest = value - high.astype(F32)
    middle = rest.astype(BF16)
    low = (rest - middle.astype(F32)).astype(BF16)
    return high, middle, low


def group_row(mean_c, var_c):
    same = jnp.where((iota((C, C), 0) >> 3) == (iota((C, C), 1) >> 3), 1.0 / SHARE, 0.0)
    mean8 = jnp.broadcast_to(mean_c, (8, C))
    spread = mean8 - dot_exact(mean8, same)
    var8 = jnp.broadcast_to(var_c, (8, C)) + spread * spread
    to_group = jnp.where(iota((C, 128), 1) == (iota((C, 128), 0) >> 3), 1.0 / SHARE, 0.0)
    both = dot_exact(jnp.concatenate([mean8, var8], axis=0), to_group)
    return both[:8] + pltpu.roll(both[8:], 32, 1)


def combine_groups(rows):
    count = rows.shape[0]
    mean = jnp.sum(rows, axis=0, keepdims=True) / count
    off = rows - mean
    scatter = jnp.sum(off * off, axis=0, keepdims=True) / count
    mean8 = jnp.broadcast_to(mean, (8, 128))
    var8 = pltpu.roll(mean8, 96, 1) + scatter
    from_group = jnp.where(iota((128, C), 0) == (iota((128, C), 1) >> 3), 1.0, 0.0)
    both = dot_exact(jnp.concatenate([mean8, var8], axis=0), from_group)
    return both[:1], lax.rsqrt(both[8:9] + EPS)


def channel_stats(value):
    count = value.shape[0]
    mean = jnp.sum(value, axis=0, keepdims=True) / count
    off = value - mean
    return mean, jnp.sum(off * off, axis=0, keepdims=True) / count


def stats_kernel(mine, other, wide, edges, next_out, last_out, far_out):
    parts = [r[...].astype(F32) for r in (mine, other)]
    count = 2 * parts[0].shape[0]
    mean = sum(jnp.sum(p, axis=0, keepdims=True) for p in parts) / count
    var = 0.0
    for part in parts:
        off = part - mean
        var = var + jnp.sum(off * off, axis=0, keepdims=True)
    high, middle, low = [p.astype(F32) for p in split3(group_row(mean, var / count))]
    packed = jnp.concatenate(
        [
            jnp.concatenate([high, middle], axis=1),
            jnp.concatenate([low, jnp.zeros_like(low)], axis=1),
        ],
        axis=0,
    ).astype(BF16)
    for out in (next_out, last_out, far_out):
        out[:16, :] = packed
        out[16:176, :] = wide[...]
    next_out[176:, :] = edges[0]
    last_out[176:, :] = edges[1]


def stats_and_rows(mine, other, wide, edges):
    return pl.pallas_call(
        stats_kernel,
        out_shape=(
            jax.ShapeDtypeStruct((208, C), BF16),
            jax.ShapeDtypeStruct((208, C), BF16),
            jax.ShapeDtypeStruct((176, C), BF16),
        ),
        compiler_params=params(),
    )(mine, other, wide, edges)


def attention_kernel(
    order,
    mine,
    other,
    near,
    far,
    down,
    up,
    gain,
    bias,
    w_far,
    out_far,
    block_far,
    keys,
    values,
    strip,
    w_qkv,
    out,
    block,
    w_sem,
    block_sem,
    out_sems,
):
    load = pltpu.make_async_copy(w_far, w_qkv, w_sem)
    load.start()
    rows = []
    for ref in (near, down, far, up):
        packed = ref[:16, :].astype(F32)
        rows.append(packed[:8, :128] + packed[:8, 128:] + packed[8:, :128])
    mean, inverse = combine_groups(jnp.concatenate(rows, axis=0))

    def norm(cells):
        normed = (cells.astype(F32) - mean) * inverse
        return (normed * gain[...] + bias[...]).astype(BF16)

    for i, ref in enumerate((near, down, far, up)):
        cells = ref[16:176, :].astype(F32)
        strip[10 + 160 * i : 170 + 160 * i, :] = cells
        if i == 0:
            strip[650:660, :] = cells[:10]
        if i == 3:
            strip[:10, :] = cells[150:]
    strip[660:, :] = jnp.zeros((STRIP - 660, C), F32)
    block[...] = strip[:CELLS_IN, :].astype(BF16)
    keep = pltpu.make_async_copy(block, block_far, block_sem)
    keep.start()
    load.wait()

    head_of = iota((512, C), 1) >> 6
    for i in range(8):
        rows = slice(512 * i, 512 * i + 512)
        cells = (mine, other)[i // 4][512 * (i % 4) : 512 * (i % 4) + 512, :]
        both = dot(norm(cells), w_qkv[:, C:])
        keys[rows, :] = both[:, :C].astype(BF16)
        for head in range(HEADS):
            values[head, rows, :] = jnp.where(head_of == head, both[:, C:], 1.0).astype(BF16)

    scale = HD**-0.5 * float(np.log2(np.e))
    queries = (dot(norm(strip[...]), w_qkv[:, :C]) * scale).astype(BF16)
    head_of = iota((STRIP, C), 1) >> 6
    lane = iota((STRIP, 128), 1)
    result = jnp.zeros((STRIP, C), F32)
    packed = jnp.zeros((STRIP, 128), F32)
    for head in range(HEADS):
        own = head_of == head
        masked = jnp.where(own, queries, jnp.zeros_like(queries))
        best, mixed = None, None
        for i in range(4096 // KEY_BLOCK):
            rows = slice(KEY_BLOCK * i, KEY_BLOCK * (i + 1))
            scores = dot(masked, keys[rows, :], ((1,), (1,)))
            top = jnp.max(scores, axis=1, keepdims=True)
            fresh = top if i == 0 else jnp.maximum(best, top)
            product = dot(jnp.exp2(scores - fresh).astype(BF16), values[head, rows, :])
            mixed = product if i == 0 else mixed * jnp.exp2(best - fresh) + product
            best = fresh
        result = jnp.where(own, mixed / pltpu.roll(mixed, HD, 1), result)
        spot = 0 if head else 128
        log = best + jnp.log2(mixed[:, spot : spot + 128])
        for part, value in enumerate(split3(log)):
            packed = jnp.where(lane == 4 * part + head, value.astype(F32), packed)
    result = result.astype(BF16)
    copies = []
    for step in range(4):
        rows = slice(160 * step, 160 * step + CELLS_IN)
        out[step, :CELLS_IN, :] = result[rows]
        turned = jnp.concatenate([packed[rows], jnp.zeros((64, 128), F32)], axis=0).T[:16]
        out[step, CELLS_IN:, :] = turned.astype(BF16)
        copy = pltpu.make_async_copy(out.at[step], out_far.at[order[step]], out_sems.at[step])
        copy.start()
        copies.append(copy)
    keep.wait()
    for copy in copies:
        copy.wait()


def partial_attention(order, mine, other, near, far, down, up, gain, bias, w_qkv):
    vmem = pl.BlockSpec(memory_space=pltpu.VMEM)
    return pl.pallas_call(
        attention_kernel,
        out_shape=(
            pltpu.HBM((4, CELLS_IN + 16, C), BF16),
            pltpu.HBM((CELLS_IN, C), BF16),
        ),
        in_specs=[pl.BlockSpec(memory_space=pltpu.SMEM)] + [vmem] * 8 + [HBM],
        out_specs=(HBM, HBM),
        scratch_shapes=[
            pltpu.VMEM((4096, C), BF16),
            pltpu.VMEM((HEADS, 4096, C), BF16),
            pltpu.VMEM((STRIP, C), F32),
            pltpu.VMEM((C, 3 * C), BF16),
            pltpu.VMEM((4, CELLS_IN + 16, C), BF16),
            pltpu.VMEM((CELLS_IN, C), BF16),
            pltpu.SemaphoreType.DMA,
            pltpu.SemaphoreType.DMA,
            pltpu.SemaphoreType.DMA((4,)),
        ],
        compiler_params=params(),
    )(order, mine, other, near, far, down, up, gain, bias, in_hbm(w_qkv))


def merge_kernel(
    flags, parts, coarse_far, w_far, up, merged_out, stats_out, coarse, w_proj, coarse_sem, w_sem
):
    loads = [
        pltpu.make_async_copy(coarse_far, coarse, coarse_sem),
        pltpu.make_async_copy(w_far, w_proj, w_sem),
    ]
    for load in loads:
        load.start()
    count = parts.shape[0]
    logs = []
    for i in range(count):
        tail = parts[i, CELLS_IN:, :].astype(F32)
        logs.append(tail[0:4] + tail[4:8] + tail[8:12])
    top = functools.reduce(jnp.maximum, logs)
    shares = [jnp.exp2(v - top) for v in logs]
    total = sum(shares)
    spread = jnp.where((iota((16, C), 1) >> 6) == (iota((16, C), 0) & 3), 1.0, 0.0).astype(BF16)
    attended = jnp.zeros((CELLS_IN, C), F32)
    for i in range(count):
        pieces = [p.astype(F32) for p in split3((shares[i] / total)[:, :CELLS_IN])]
        pieces.append(jnp.zeros_like(pieces[0]))
        wide = dot(jnp.concatenate(pieces, axis=0).astype(BF16), spread, ((0,), (0,)))
        attended = attended + wide * parts[i, :CELLS_IN, :].astype(F32)
    for load in loads:
        load.wait()
    merged = coarse[...].astype(F32) + dot(attended.astype(BF16), w_proj[...])
    cell = iota((CELLS_IN, C), 0)
    col = lax.rem(cell, 10)
    outside = (
        ((cell < 10) & (flags[0] == 1))
        | ((cell >= 170) & (flags[1] == 1))
        | ((col == 0) & (flags[2] == 1))
        | ((col == 9) & (flags[3] == 1))
        | (cell >= 180)
    )
    merged = jnp.where(outside, 0.0, merged).astype(BF16)
    merged_out[...] = merged
    field = dot(up[WIN + 16 : WIN + 528, :], merged)
    mean, var = channel_stats(field)
    stats_out[...] = jnp.broadcast_to(group_row(mean, var)[:1], stats_out.shape)


def merge(flags, parts, coarse, w_proj, up):
    vmem = pl.BlockSpec(memory_space=pltpu.VMEM)
    return pl.pallas_call(
        merge_kernel,
        out_shape=(
            jax.ShapeDtypeStruct((CELLS_IN, C), BF16),
            jax.ShapeDtypeStruct((128, 128), F32),
        ),
        in_specs=[pl.BlockSpec(memory_space=pltpu.SMEM), vmem, HBM, HBM, vmem],
        out_specs=(vmem, vmem),
        scratch_shapes=[
            pltpu.VMEM((CELLS_IN, C), BF16),
            pltpu.VMEM((C, C), BF16),
            pltpu.SemaphoreType.DMA,
            pltpu.SemaphoreType.DMA,
        ],
        compiler_params=params(),
    )(flags, parts, in_hbm(coarse), in_hbm(w_proj), up)


def back_kernel(c0, c1, c2, weight, out):
    windows = (c0, c1, c2)
    total = jnp.zeros((512, C), F32)
    for a in range(3):
        for b in range(3):
            window = windows[2 - b][16 * (2 - a) : 16 * (2 - a) + 512, :]
            total = total + dot(window, weight[3 * a + b], ((1,), (1,)))
    out[...] = total


def back_conv(windows, weight):
    return pl.pallas_call(
        back_kernel,
        out_shape=jax.ShapeDtypeStruct((512, C), F32),
        compiler_params=params(),
        cost_estimate=pl.CostEstimate(
            flops=9 * 2 * 512 * C * C, bytes_accessed=3 * 10**6, transcendentals=0
        ),
    )(*windows, weight)


def hidden_kernel(
    flags,
    merged,
    up,
    stats,
    gain,
    bias,
    cot,
    grad_hidden,
    kept,
    given,
    hidden_far,
    hidden,
    sem,
):
    mean, inverse = combine_groups(stats[...])
    row = iota((WIN, C), 0)
    col = row & 15
    for b in range(3):
        field = dot(up[b * WIN : (b + 1) * WIN, :], merged[...])
        xhat = (field - mean) * inverse
        shifted = xhat * gain[...] + bias[...]
        sig = 0.5 * jnp.tanh(0.5 * shifted) + 0.5
        outside = ((row < 16) & (flags[0] == 1)) | ((row >= 528) & (flags[1] == 1))
        if b == 0:
            outside = outside | ((col == 0) & (flags[2] == 1))
        if b == 2:
            outside = outside | ((col == 15) & (flags[3] == 1))
        hidden[b] = jnp.where(outside, 0.0, shifted * sig).astype(BF16)
        if b == 1:
            inner = slice(16, 528)
            s, t = sig[inner], shifted[inner]
            grad_shift = grad_hidden[...] * s * (1.0 + t * (1.0 - s))
            sum_w = jnp.sum(grad_shift * xhat[inner], axis=0, keepdims=True)
            sum_b = jnp.sum(grad_shift, axis=0, keepdims=True)
            rows = []
            for part in range(3):
                for value in (sum_w, sum_b):
                    piece = split3(value)[part].astype(F32)
                    rows += [piece[:, :128], piece[:, 128:]]
            tail = jnp.concatenate(rows + [jnp.zeros((4, 128), F32)], axis=0).astype(BF16)
            kept[2304:, :] = tail
            given[2304:, :] = tail
    keep = pltpu.make_async_copy(hidden, hidden_far, sem)
    keep.start()
    first = flags[4] == 0
    for a in range(3):
        for b in range(3):
            rows = slice((3 * a + b) * C, (3 * a + b + 1) * C)
            product = dot(hidden[b, 16 * a : 16 * a + 512, :], cot[...], ((0,), (0,)))
            left, right = product[:, :128].astype(BF16), product[:, 128:].astype(BF16)
            kept[rows, :] = jnp.where(first, left, right)
            given[rows, :] = jnp.where(first, right, left)
    keep.wait()


def hidden_and_kernel_gradient(flags, merged, up, stats, gain, bias, cot, grad_hidden):
    vmem = pl.BlockSpec(memory_space=pltpu.VMEM)
    return pl.pallas_call(
        hidden_kernel,
        out_shape=(
            jax.ShapeDtypeStruct((2320, 128), BF16),
            jax.ShapeDtypeStruct((2320, 128), BF16),
            pltpu.HBM((3, WIN, C), BF16),
        ),
        in_specs=[pl.BlockSpec(memory_space=pltpu.SMEM)] + [vmem] * 7,
        out_specs=(vmem, vmem, HBM),
        scratch_shapes=[pltpu.VMEM((3, WIN, C), BF16), pltpu.SemaphoreType.DMA],
        compiler_params=params(),
    )(flags, merged, up, stats, gain, bias, cot, grad_hidden)


def conv_kernel(hidden, weight, conv_bias, fine_out):
    total = jnp.zeros((512, C), F32) + conv_bias[...]
    for a in range(3):
        for b in range(3):
            total = total + dot(hidden[b, 16 * a : 16 * a + 512, :], weight[3 * a + b])
    fine_out[...] = total.astype(BF16)


def conv(hidden, weight, conv_bias):
    return pl.pallas_call(
        conv_kernel,
        out_shape=jax.ShapeDtypeStruct((512, C), BF16),
        compiler_params=params(),
        cost_estimate=pl.CostEstimate(
            flops=9 * 2 * 512 * C * C, bytes_accessed=3 * 10**6, transcendentals=0
        ),
    )(hidden, weight, conv_bias)


def pair_kernel(kept, got, out_far, total, out, sems):
    total[...] = kept[...].astype(F32) + got[...].astype(F32)
    tails = [r[2304:, :].astype(F32) for r in (kept, got)]
    sums = sum(t[0:4] + t[4:8] + t[8:12] for t in tails)
    parts = [p.astype(F32) for p in split3(sums)]
    tail = jnp.concatenate([jnp.zeros((36, 128), F32)] + parts, axis=0)
    own = iota((48, 128), 0) < 36
    copies = []
    for i in range(64):
        out[i] = jnp.where(own, total[36 * i : 36 * i + 48, :], tail).astype(BF16)
        if i % 16 == 15:
            part = pl.ds(i - 15, 16)
            copies.append(pltpu.make_async_copy(out.at[part], out_far.at[part], sems.at[i // 16]))
            copies[-1].start()
    for copy in copies:
        copy.wait()


def pair_sum(kept, got):
    return pl.pallas_call(
        pair_kernel,
        out_shape=pltpu.HBM((64, 48, 128), BF16),
        out_specs=HBM,
        scratch_shapes=[
            pltpu.VMEM((2320, 128), F32),
            pltpu.VMEM((64, 48, 128), BF16),
            pltpu.SemaphoreType.DMA((4,)),
        ],
        compiler_params=params(),
    )(kept, got)


def share_kernel(got, out_far, sums, chunk, sems):
    total = jnp.sum(got[...].astype(F32), axis=0)
    chunk[...] = jnp.broadcast_to((total[:40] * (1.0 / 256.0)).astype(BF16)[None], chunk.shape)
    size = chunk.shape[0]
    copies = [
        pltpu.make_async_copy(chunk, out_far.at[pl.ds(size * i, size)], sems.at[i])
        for i in range(out_far.shape[0] // size)
    ]
    for copy in copies:
        copy.start()
    quarters = total[36:40] + total[40:44] + total[44:48]
    weight = jnp.concatenate([quarters[0:1], quarters[1:2]], axis=1)
    shift_sum = jnp.concatenate([quarters[2:3], quarters[3:4]], axis=1)
    sums[...] = jnp.concatenate([weight, shift_sum, jnp.zeros((6, C), F32)], axis=0)
    for copy in copies:
        copy.wait()


def share_sum(got):
    vmem = pl.BlockSpec(memory_space=pltpu.VMEM)
    return pl.pallas_call(
        share_kernel,
        out_shape=(pltpu.HBM((64, 40, 128), BF16), jax.ShapeDtypeStruct((8, C), F32)),
        in_specs=[vmem],
        out_specs=(HBM, vmem),
        scratch_shapes=[pltpu.VMEM((16, 40, 128), BF16), pltpu.SemaphoreType.DMA((4,))],
        compiler_params=params(),
    )(got)


def field_kernel(merged, up, stats, gain, bias, grad_hidden, sums, field_out, norm_out):
    mean, inverse = combine_groups(stats[...])
    value = dot(up[WIN + 16 : WIN + 528, :], merged[...])
    xhat = (value - mean) * inverse
    shifted = xhat * gain[...] + bias[...]
    sig = 0.5 * jnp.tanh(0.5 * shifted) + 0.5
    grad_shift = grad_hidden[...] * sig * (1.0 + shifted * (1.0 - sig))
    same = jnp.where((iota((C, C), 0) >> 3) == (iota((C, C), 1) >> 3), 1.0, 0.0)
    means = dot_exact(sums[...] * gain[...], same) * (1.0 / (65536 * SHARE))
    field = inverse * (grad_shift * gain[...] - means[1:2] - xhat * means[0:1])
    field_out[...] = field.astype(BF16)
    norm_out[...] = sums[:2] * (1.0 / 256.0)


def field_gradient(merged, up, stats, gain, bias, grad_hidden, sums):
    return pl.pallas_call(
        field_kernel,
        out_shape=(
            jax.ShapeDtypeStruct((512, C), BF16),
            jax.ShapeDtypeStruct((2, C), F32),
        ),
        compiler_params=params(),
        cost_estimate=pl.CostEstimate(
            flops=10**9, bytes_accessed=2 * 10**6, transcendentals=2 * 10**5
        ),
    )(merged, up, stats, gain, bias, grad_hidden, sums)


def layout_kernel(flags, mine, other, out_far, out, sems):
    first = flags[4] == 0
    copies = []
    for i in range(0, 64, 2):
        halves = []
        for ref in (mine, other):
            pair = [ref[i + k].astype(F32)[:36] for k in range(2)]
            halves.append(jnp.concatenate(pair, axis=0))
        rows = slice(36 * i, 36 * i + 72)
        out[rows, :128] = jnp.where(first, halves[0], halves[1])
        out[rows, 128:] = jnp.where(first, halves[1], halves[0])
        if i % 8 == 6:
            part = pl.ds(36 * (i - 6), 288)
            copies.append(pltpu.make_async_copy(out.at[part], out_far.at[part], sems.at[i // 8]))
            copies[-1].start()
    for copy in copies:
        copy.wait()


def lay_out(flags, mine, other):
    vmem = pl.BlockSpec(memory_space=pltpu.VMEM)
    return pl.pallas_call(
        layout_kernel,
        out_shape=pltpu.HBM((2304, C), F32),
        in_specs=[pl.BlockSpec(memory_space=pltpu.SMEM), vmem, vmem],
        out_specs=HBM,
        scratch_shapes=[pltpu.VMEM((2304, C), F32), pltpu.SemaphoreType.DMA((8,))],
        compiler_params=params(),
    )(flags, mine, other)


def copies_kernel(cells, out_far, sems):
    copies = [
        pltpu.make_async_copy(cells, out_far.at[i], sems.at[i]) for i in range(out_far.shape[0])
    ]
    for copy in copies:
        copy.start()
    for copy in copies:
        copy.wait()


def copies_of(cells):
    return pl.pallas_call(
        copies_kernel,
        out_shape=pltpu.HBM((16, 128, C), BF16),
        in_specs=[pl.BlockSpec(memory_space=pltpu.VMEM)],
        out_specs=HBM,
        scratch_shapes=[pltpu.SemaphoreType.DMA((16,))],
        compiler_params=params(),
    )(cells)


def shift(value, axis, count, step):
    return lax.ppermute(value, axis, [((i + step) % count, i) for i in range(count)])


def per_device(
    coarse,
    norm1_gain,
    norm1_bias,
    w_qkv,
    w_proj,
    second_norm2_gain,
    second_norm2_bias,
    conv_weight,
    conv_bias,
    cotangent,
):
    y, c = lax.axis_index("y"), lax.axis_index("c")
    block = lax.axis_index(ZXC)
    flags = jnp.stack([y == 0, y == 3, block == 0, block == 31, c == 1]).astype(jnp.int32)
    up = jnp.asarray(UPSAMPLE, BF16)
    taps = conv_weight.reshape(9, C, C)

    own = coarse.reshape(128, C)
    cells = lax.all_to_all(copies_of(own), ("z", "x"), 0, 0, tiled=True).reshape(2048, C)


    first = jnp.concatenate([coarse[:, 0], cotangent[:, 0]], axis=0)
    last = jnp.concatenate([coarse[:, -1], cotangent[:, -1]], axis=0)
    before = lax.ppermute(last, ZXC, [(i, i + 1) for i in range(31)])[:, None]
    after = lax.ppermute(first, ZXC, [(i + 1, i) for i in range(31)])[:, None]
    wide = jnp.concatenate([before[:16], coarse, after[:16]], axis=1).reshape(160, C)
    grad = jnp.concatenate([before[16:], cotangent, after[16:]], axis=1)
    edges = jnp.pad(jnp.stack([grad[0], grad[-1]]), ((0, 0), (0, 14), (0, 0)))
    other = shift(cells, "c", 2, 1)

    near, last, far = stats_and_rows(cells, other, wide, edges)
    below, above, far = (
        shift(near, "y", 4, 1),
        shift(last, "y", 4, 3),
        shift(far, "y", 4, 2),
    )
    top = jnp.where(y == 0, 0, above[176:194])[None].astype(BF16)
    bottom = jnp.where(y == 3, 0, below[176:194])[None].astype(BF16)
    grad = jnp.concatenate([top, grad, bottom], axis=0)
    windows = [grad[:, b : b + 16].reshape(WIN, C) for b in range(3)]
    order = jnp.stack([(y + k) % 4 for k in range(4)]).astype(jnp.int32)

    partial, block = partial_attention(
        order, cells, other, near, far, below, above, norm1_gain[None], norm1_bias[None], w_qkv
    )
    partial = lax.all_to_all(partial, "y", 0, 0, tiled=True)
    merged, stats2 = merge(flags, partial, block, w_proj, up)
    stats2 = lax.all_to_all(stats2.reshape(128, 1, 128), ALL, 0, 0, tiled=True)
    stats2 = stats2.reshape(128, 128)
    grad_hidden = back_conv(windows, taps)
    gain2, bias2 = second_norm2_gain[None], second_norm2_bias[None]
    kept, given, hidden = hidden_and_kernel_gradient(
        flags, merged, up, stats2, gain2, bias2, cotangent.reshape(512, C), grad_hidden
    )

    sent = pair_sum(kept, shift(given, "c", 2, 1))
    got = lax.all_to_all(sent, ("y", "z", "x"), 0, 0, tiled=True)
    fine = conv(hidden, taps, conv_bias[None])
    got, fine = lax.optimization_barrier((got, fine))

    chunk, sums = share_sum(got)
    spread = lax.all_to_all(chunk, ("y", "z", "x"), 0, 0, tiled=True)
    field, grad_norm = field_gradient(merged, up, stats2, gain2, bias2, grad_hidden, sums)
    spread, field = lax.optimization_barrier((spread, field))
    grad_conv = lay_out(flags, spread, shift(spread, "c", 2, 1)).reshape(3, 3, C, C)
    return (
        fine.reshape(32, 16, C),
        field.reshape(32, 16, C),
        grad_conv,
        grad_norm,
    )


def solution(mesh):
    split = Mesh(mesh.devices.reshape(4, 4, 4, 2), ALL)
    cells = P("y", ZXC, None)
    return jax.shard_map(
        per_device,
        mesh=split,
        in_specs=(cells,) + (P(),) * 8 + (cells,),
        out_specs=(cells, cells, P(), P()),
        check_vma=False,
    )
```

```python
import functools

import jax
import jax.numpy as jnp
import numpy as np
from jax import lax
from jax.experimental import pallas as pl
from jax.experimental.pallas import tpu as pltpu
from jax.sharding import Mesh, PartitionSpec as P

HEADS = 4
HD = 64
C = 256
SHARE = 8
EPS = 1e-05
F32 = jnp.float32
BF16 = jnp.bfloat16
VMEM_LIMIT = 50 * 2**20
HBM = pl.BlockSpec(memory_space=pltpu.HBM)
ZXC = ("z", "x", "c")
ALL = ("y", "z", "x", "c")

CELLS_IN = 192
PART = CELLS_IN + 16
STRIP = 672
KEY_BLOCK = 512
FINE_ROWS = 34
WIN = FINE_ROWS * 16


def upsample_matrix():
    def line(f):
        i = f // 2
        return {i: 0.75, (i - 1 if f % 2 == 0 else i + 1): 0.25}

    table = np.zeros((3, FINE_ROWS, 16, CELLS_IN), np.float32)
    for b in range(3):
        for fr in range(FINE_ROWS):
            for j in range(16):
                for r, wr in line(fr - 1).items():
                    for c, wc in line(j + b - 1).items():
                        table[b, fr, j, (r + 1) * 10 + c + 1] += wr * wc
    return table.reshape(3 * WIN, CELLS_IN)


UPSAMPLE = upsample_matrix()


def params(grid=None):
    return pltpu.CompilerParams(
        vmem_limit_bytes=VMEM_LIMIT,
        dimension_semantics=None if grid is None else ("arbitrary",) * grid,
    )


def in_vmem(value):
    return pltpu.with_memory_space_constraint(value, pltpu.VMEM)


def in_hbm(value):
    return pltpu.with_memory_space_constraint(value, pltpu.HBM)


def dot(a, b, contract=((1,), (0,))):
    return lax.dot_general(a, b, (contract, ((), ())), preferred_element_type=F32)


def dot_exact(a, b):
    size = a.shape[0]
    parts = jnp.concatenate([p.astype(F32) for p in split3(a)], axis=0).astype(BF16)
    result = dot(parts, b.astype(BF16))
    return result[:size] + result[size : 2 * size] + result[2 * size :]


def iota(shape, dim):
    return lax.broadcasted_iota(jnp.int32, shape, dim)


def split3(value):
    high = value.astype(BF16)
    rest = value - high.astype(F32)
    middle = rest.astype(BF16)
    low = (rest - middle.astype(F32)).astype(BF16)
    return high, middle, low


def group_row(mean_c, var_c):
    same = jnp.where((iota((C, C), 0) >> 3) == (iota((C, C), 1) >> 3), 1.0 / SHARE, 0.0)
    mean8 = jnp.broadcast_to(mean_c, (8, C))
    spread = mean8 - dot_exact(mean8, same)
    var8 = jnp.broadcast_to(var_c, (8, C)) + spread * spread
    to_group = jnp.where(iota((C, 128), 1) == (iota((C, 128), 0) >> 3), 1.0 / SHARE, 0.0)
    both = dot_exact(jnp.concatenate([mean8, var8], axis=0), to_group)
    return both[:8] + pltpu.roll(both[8:], 32, 1)


def combine_groups(rows):
    count = rows.shape[0]
    mean = jnp.sum(rows, axis=0, keepdims=True) / count
    off = rows - mean
    scatter = jnp.sum(off * off, axis=0, keepdims=True) / count
    mean8 = jnp.broadcast_to(mean, (8, 128))
    var8 = pltpu.roll(mean8, 96, 1) + scatter
    from_group = jnp.where(iota((128, C), 0) == (iota((128, C), 1) >> 3), 1.0, 0.0)
    both = dot_exact(jnp.concatenate([mean8, var8], axis=0), from_group)
    return both[:1], lax.rsqrt(both[8:9] + EPS)


def channel_stats(value):
    count = value.shape[0]
    mean = jnp.sum(value, axis=0, keepdims=True) / count
    off = value - mean
    return mean, jnp.sum(off * off, axis=0, keepdims=True) / count


def stats_rows(cells):
    mean, var = channel_stats(cells[...].astype(F32))
    high, middle, low = [p.astype(F32)[:1] for p in split3(group_row(mean, var))]
    upper = jnp.concatenate([high, middle], axis=1)
    return [upper, jnp.concatenate([low, jnp.zeros_like(low)], axis=1)]


def stats_kernel(cells, out):
    out[...] = jnp.concatenate(stats_rows(cells) + [jnp.zeros((6, C), F32)], axis=0)


def local_stats(cells):
    return pl.pallas_call(
        stats_kernel,
        out_shape=jax.ShapeDtypeStruct((8, C), F32),
        compiler_params=params(),
        cost_estimate=pl.CostEstimate(
            flops=3 * cells.size, bytes_accessed=2 * cells.size, transcendentals=0
        ),
    )(cells)


def rows_kernel(first, other, wide, edges, next_out, last_out, far_out):
    rows = [first[0:2, :]] + stats_rows(other) + [jnp.zeros((12, C), F32)]
    packed = jnp.concatenate(rows, axis=0).astype(BF16)
    for out in (next_out, last_out, far_out):
        out[:16, :] = packed
        out[16:176, :] = wide[...]
    next_out[176:, :] = edges[0]
    last_out[176:, :] = edges[1]


def stats_and_rows(first, other, wide, edges):
    return pl.pallas_call(
        rows_kernel,
        out_shape=(
            pltpu.VMEM((208, C), BF16),
            pltpu.VMEM((208, C), BF16),
            pltpu.VMEM((176, C), BF16),
        ),
        compiler_params=params(),
    )(first, other, wide, edges)


def attention_kernel(
    mine,
    other,
    near,
    far,
    down,
    up,
    gain,
    bias,
    w_far,
    out1,
    out2,
    out3,
    kept_far,
    keys,
    values,
    strip,
    w_qkv,
    kept,
    w_sem,
    block_sem,
    kept_sem,
):
    load = pltpu.make_async_copy(w_far, w_qkv, w_sem)
    load.start()
    rows = []
    for ref in (near, down, far, up):
        packed = ref[:16, :].astype(F32)
        for i in (0, 2):
            upper, lower = packed[i : i + 1], packed[i + 1 : i + 2]
            rows.append(upper[:, :128] + upper[:, 128:] + lower[:, :128])
    mean, inverse = combine_groups(jnp.concatenate(rows, axis=0))

    def norm(cells):
        normed = (cells.astype(F32) - mean) * inverse
        return (normed * gain[...] + bias[...]).astype(BF16)

    for i, ref in enumerate((near, down, far, up)):
        cells = ref[16:176, :].astype(F32)
        strip[10 + 160 * i : 170 + 160 * i, :] = cells
        if i == 0:
            strip[650:660, :] = cells[:10]
        if i == 3:
            strip[:10, :] = cells[150:]
    strip[660:, :] = jnp.zeros((STRIP - 660, C), F32)
    kept[PART:, :] = strip[:CELLS_IN, :].astype(BF16)
    tail = pl.ds(PART, CELLS_IN)
    keep = pltpu.make_async_copy(kept.at[tail], kept_far.at[tail], block_sem)
    keep.start()
    load.wait()

    head_of = iota((512, C), 1) >> 6
    ones = jnp.ones((512, C), BF16)
    for i in range(8):
        rows = slice(512 * i, 512 * i + 512)
        cells = (mine, other)[i // 4][512 * (i % 4) : 512 * (i % 4) + 512, :]
        both = dot(norm(cells), w_qkv[:, C:])
        both = both.astype(BF16)
        keys[rows, :] = both[:, :C]
        for head in range(HEADS):
            values[head, rows, :] = jnp.where(head_of == head, both[:, C:], ones)

    scale = HD**-0.5 * float(np.log2(np.e))
    queries = (dot(norm(strip[...]), w_qkv[:, :C]) * scale).astype(BF16)
    head_of = iota((STRIP, C), 1) >> 6
    lane = iota((STRIP, 128), 1)
    result = jnp.zeros((STRIP, C), F32)
    totals = jnp.ones((STRIP, C), F32)
    logs = jnp.zeros((STRIP, 128), F32)
    tops = jnp.zeros((STRIP, 128), F32)
    for head in range(HEADS):
        own = head_of == head
        masked = jnp.where(own, queries, jnp.zeros_like(queries))
        best, mixed = None, None
        for i in range(4096 // KEY_BLOCK):
            rows = slice(KEY_BLOCK * i, KEY_BLOCK * (i + 1))
            scores = dot(masked, keys[rows, :], ((1,), (1,)))
            top = jnp.max(scores, axis=1, keepdims=True)
            fresh = top if i == 0 else jnp.maximum(best, top)
            product = dot(jnp.exp2(scores - fresh).astype(BF16), values[head, rows, :])
            mixed = product if i == 0 else mixed * jnp.exp2(best - fresh) + product
            best = fresh
        result = jnp.where(own, mixed, result)
        totals = jnp.where(own, pltpu.roll(mixed, HD, 1), totals)
        spot = 0 if head else 128
        logs = jnp.where(lane == head, mixed[:, spot : spot + 128], logs)
        tops = jnp.where(lane == head, best, tops)
    result = (result / totals).astype(BF16)
    logs = tops + jnp.log2(jnp.where(lane < HEADS, logs, 1.0))
    high, middle, low = [p.astype(F32) for p in split3(logs)]
    packed = high + pltpu.roll(middle, 4, 1) + pltpu.roll(low, 8, 1)
    head = pl.ds(0, PART)
    copy = pltpu.make_async_copy(kept.at[head], kept_far.at[head], kept_sem)
    for step, out in enumerate((kept, out1, out2, out3)):
        rows = slice(160 * step, 160 * step + CELLS_IN)
        out[:CELLS_IN, :] = result[rows]
        turned = jnp.concatenate([packed[rows], jnp.zeros((64, 128), F32)], axis=0).T[:16]
        out[CELLS_IN:PART, :] = turned.astype(BF16)
        if step == 0:
            copy.start()
    keep.wait()
    copy.wait()


def partial_attention(mine, other, near, far, down, up, gain, bias, w_qkv):
    vmem = pl.BlockSpec(memory_space=pltpu.VMEM)
    return pl.pallas_call(
        attention_kernel,
        out_shape=(jax.ShapeDtypeStruct((PART, C), BF16),) * 3
        + (pltpu.HBM((PART + CELLS_IN, C), BF16),),
        in_specs=[vmem] * 8 + [HBM],
        out_specs=(vmem, vmem, vmem, HBM),
        scratch_shapes=[
            pltpu.VMEM((4096, C), BF16),
            pltpu.VMEM((HEADS, 4096, C), BF16),
            pltpu.VMEM((STRIP, C), F32),
            pltpu.VMEM((C, 3 * C), BF16),
            pltpu.VMEM((PART + CELLS_IN, C), BF16),
            pltpu.SemaphoreType.DMA,
            pltpu.SemaphoreType.DMA,
            pltpu.SemaphoreType.DMA,
        ],
        compiler_params=params(),
    )(mine, other, near, in_vmem(far), in_vmem(down), in_vmem(up), gain, bias, in_hbm(w_qkv))


def merge_kernel(
    flags, p1, p2, p3, kept_far, w_far, up, merged_out, stats_out, kept, w_proj, kept_sem, w_sem
):
    loads = [
        pltpu.make_async_copy(kept_far, kept, kept_sem),
        pltpu.make_async_copy(w_far, w_proj, w_sem),
    ]
    for load in loads:
        load.start()
    parts = (p1, p2, p3, kept)
    logs = []
    for part in parts:
        if part is kept:
            loads[0].wait()
        tail = part[CELLS_IN:PART, :].astype(F32)
        logs.append(tail[0:4] + tail[4:8] + tail[8:12])
    top = functools.reduce(jnp.maximum, logs)
    shares = [jnp.exp2(v - top) for v in logs]
    total = sum(shares)
    spread = jnp.where((iota((16, C), 1) >> 6) == (iota((16, C), 0) & 3), 1.0, 0.0).astype(BF16)
    attended = jnp.zeros((CELLS_IN, C), F32)
    for i, part in enumerate(parts):
        pieces = [p.astype(F32) for p in split3((shares[i] / total)[:, :CELLS_IN])]
        pieces.append(jnp.zeros_like(pieces[0]))
        wide = dot(jnp.concatenate(pieces, axis=0).astype(BF16), spread, ((0,), (0,)))
        attended = attended + wide * part[:CELLS_IN, :].astype(F32)
    loads[1].wait()
    merged = kept[PART:, :].astype(F32) + dot(attended.astype(BF16), w_proj[...])
    cell = iota((CELLS_IN, C), 0)
    col = lax.rem(cell, 10)
    outside = (
        ((cell < 10) & (flags[0] == 1))
        | ((cell >= 170) & (flags[1] == 1))
        | ((col == 0) & (flags[2] == 1))
        | ((col == 9) & (flags[3] == 1))
        | (cell >= 180)
    )
    merged = jnp.where(outside, 0.0, merged).astype(BF16)
    merged_out[...] = merged
    field = dot(up[WIN + 16 : WIN + 528, :], merged)
    mean, var = channel_stats(field)
    stats_out[...] = jnp.broadcast_to(group_row(mean, var)[:1], stats_out.shape)


def merge(flags, parts, kept, w_proj, up):
    vmem = pl.BlockSpec(memory_space=pltpu.VMEM)
    return pl.pallas_call(
        merge_kernel,
        out_shape=(
            jax.ShapeDtypeStruct((CELLS_IN, C), BF16),
            jax.ShapeDtypeStruct((128, 128), F32),
        ),
        in_specs=[pl.BlockSpec(memory_space=pltpu.SMEM), vmem, vmem, vmem, HBM, HBM, vmem],
        out_specs=(vmem, vmem),
        scratch_shapes=[
            pltpu.VMEM((PART + CELLS_IN, C), BF16),
            pltpu.VMEM((C, C), BF16),
            pltpu.SemaphoreType.DMA,
            pltpu.SemaphoreType.DMA,
        ],
        compiler_params=params(),
    )(flags, *parts, in_hbm(kept), in_hbm(w_proj), up)


def back_kernel(c0, c1, c2, weight, out):
    windows = (c0, c1, c2)
    total = jnp.zeros((512, C), F32)
    for a in range(3):
        for b in range(3):
            window = windows[2 - b][16 * (2 - a) : 16 * (2 - a) + 512, :]
            total = total + dot(window, weight[3 * a + b], ((1,), (1,)))
    out[...] = total


def back_conv(windows, weight):
    return pl.pallas_call(
        back_kernel,
        out_shape=jax.ShapeDtypeStruct((512, C), F32),
        compiler_params=params(),
        cost_estimate=pl.CostEstimate(
            flops=9 * 2 * 512 * C * C, bytes_accessed=3 * 10**6, transcendentals=0
        ),
    )(*windows, weight)


def hidden_kernel(
    flags,
    merged,
    up,
    stats,
    gain,
    bias,
    cot,
    grad_hidden,
    kept,
    given,
    hidden_far,
    hidden,
    sem,
):
    mean, inverse = combine_groups(stats[...])
    row = iota((WIN, C), 0)
    col = row & 15
    for b in range(3):
        field = dot(up[b * WIN : (b + 1) * WIN, :], merged[...])
        xhat = (field - mean) * inverse
        shifted = xhat * gain[...] + bias[...]
        sig = 0.5 * jnp.tanh(0.5 * shifted) + 0.5
        outside = ((row < 16) & (flags[0] == 1)) | ((row >= 528) & (flags[1] == 1))
        if b == 0:
            outside = outside | ((col == 0) & (flags[2] == 1))
        if b == 2:
            outside = outside | ((col == 15) & (flags[3] == 1))
        hidden[b] = jnp.where(outside, 0.0, shifted * sig).astype(BF16)
        if b == 1:
            inner = slice(16, 528)
            s, t = sig[inner], shifted[inner]
            grad_shift = grad_hidden[...] * s * (1.0 + t * (1.0 - s))
            sum_w = jnp.sum(grad_shift * xhat[inner], axis=0, keepdims=True)
            sum_b = jnp.sum(grad_shift, axis=0, keepdims=True)
            rows = []
            for part in range(3):
                for value in (sum_w, sum_b):
                    piece = split3(value)[part].astype(F32)
                    rows += [piece[:, :128], piece[:, 128:]]
            tail = jnp.concatenate(rows + [jnp.zeros((4, 128), F32)], axis=0).astype(BF16)
            kept[2304:, :] = tail
            given[2304:, :] = tail
    keep = pltpu.make_async_copy(hidden, hidden_far, sem)
    keep.start()
    first = flags[4] == 0
    for a in range(3):
        for b in range(3):
            rows = slice((3 * a + b) * C, (3 * a + b + 1) * C)
            product = dot(hidden[b, 16 * a : 16 * a + 512, :], cot[...], ((0,), (0,)))
            left, right = product[:, :128].astype(BF16), product[:, 128:].astype(BF16)
            kept[rows, :] = jnp.where(first, left, right)
            given[rows, :] = jnp.where(first, right, left)
    keep.wait()


def hidden_and_kernel_gradient(flags, merged, up, stats, gain, bias, cot, grad_hidden):
    vmem = pl.BlockSpec(memory_space=pltpu.VMEM)
    return pl.pallas_call(
        hidden_kernel,
        out_shape=(
            jax.ShapeDtypeStruct((2320, 128), BF16),
            jax.ShapeDtypeStruct((2320, 128), BF16),
            pltpu.HBM((3, WIN, C), BF16),
        ),
        in_specs=[pl.BlockSpec(memory_space=pltpu.SMEM)] + [vmem] * 7,
        out_specs=(vmem, vmem, HBM),
        scratch_shapes=[pltpu.VMEM((3, WIN, C), BF16), pltpu.SemaphoreType.DMA],
        compiler_params=params(),
    )(flags, merged, up, stats, gain, bias, cot, grad_hidden)


def conv_kernel(hidden, weight, conv_bias, fine_out):
    total = jnp.zeros((512, C), F32) + conv_bias[...]
    for a in range(3):
        for b in range(3):
            total = total + dot(hidden[b, 16 * a : 16 * a + 512, :], weight[3 * a + b])
    fine_out[...] = total.astype(BF16)


def conv(hidden, weight, conv_bias):
    return pl.pallas_call(
        conv_kernel,
        out_shape=jax.ShapeDtypeStruct((512, C), BF16),
        compiler_params=params(),
        cost_estimate=pl.CostEstimate(
            flops=9 * 2 * 512 * C * C, bytes_accessed=3 * 10**6, transcendentals=0
        ),
    )(hidden, weight, conv_bias)


def pair_kernel(kept, got, out_far, total, out, sems):
    total[...] = kept[...].astype(F32) + got[...].astype(F32)
    tails = [r[2304:, :].astype(F32) for r in (kept, got)]
    sums = sum(t[0:4] + t[4:8] + t[8:12] for t in tails)
    parts = [p.astype(F32) for p in split3(sums)]
    tail = jnp.concatenate([jnp.zeros((36, 128), F32)] + parts, axis=0)
    own = iota((48, 128), 0) < 36
    copies = []
    for i in range(64):
        out[i] = jnp.where(own, total[36 * i : 36 * i + 48, :], tail).astype(BF16)
        if i % 16 == 15:
            part = pl.ds(i - 15, 16)
            copies.append(pltpu.make_async_copy(out.at[part], out_far.at[part], sems.at[i // 16]))
            copies[-1].start()
    for copy in copies:
        copy.wait()


def pair_sum(kept, got):
    return pl.pallas_call(
        pair_kernel,
        out_shape=pltpu.HBM((64, 48, 128), BF16),
        out_specs=HBM,
        scratch_shapes=[
            pltpu.VMEM((2320, 128), F32),
            pltpu.VMEM((64, 48, 128), BF16),
            pltpu.SemaphoreType.DMA((4,)),
        ],
        compiler_params=params(),
    )(kept, got)


def share_kernel(got, out_far, sums, chunk, sems):
    total = jnp.sum(got[...].astype(F32), axis=0)
    chunk[...] = jnp.broadcast_to((total[:40] * (1.0 / 256.0)).astype(BF16)[None], chunk.shape)
    size = chunk.shape[0]
    copies = [
        pltpu.make_async_copy(chunk, out_far.at[pl.ds(size * i, size)], sems.at[i])
        for i in range(out_far.shape[0] // size)
    ]
    for copy in copies:
        copy.start()
    quarters = total[36:40] + total[40:44] + total[44:48]
    weight = jnp.concatenate([quarters[0:1], quarters[1:2]], axis=1)
    shift_sum = jnp.concatenate([quarters[2:3], quarters[3:4]], axis=1)
    sums[...] = jnp.concatenate([weight, shift_sum, jnp.zeros((6, C), F32)], axis=0)
    for copy in copies:
        copy.wait()


def share_sum(got):
    vmem = pl.BlockSpec(memory_space=pltpu.VMEM)
    return pl.pallas_call(
        share_kernel,
        out_shape=(pltpu.HBM((64, 40, 128), BF16), jax.ShapeDtypeStruct((8, C), F32)),
        in_specs=[vmem],
        out_specs=(HBM, vmem),
        scratch_shapes=[pltpu.VMEM((16, 40, 128), BF16), pltpu.SemaphoreType.DMA((4,))],
        compiler_params=params(),
    )(got)


def field_kernel(merged, up, stats, gain, bias, grad_hidden, sums, field_out, norm_out):
    mean, inverse = combine_groups(stats[...])
    value = dot(up[WIN + 16 : WIN + 528, :], merged[...])
    xhat = (value - mean) * inverse
    shifted = xhat * gain[...] + bias[...]
    sig = 0.5 * jnp.tanh(0.5 * shifted) + 0.5
    grad_shift = grad_hidden[...] * sig * (1.0 + shifted * (1.0 - sig))
    same = jnp.where((iota((C, C), 0) >> 3) == (iota((C, C), 1) >> 3), 1.0, 0.0)
    means = dot_exact(sums[...] * gain[...], same) * (1.0 / (65536 * SHARE))
    field = inverse * (grad_shift * gain[...] - means[1:2] - xhat * means[0:1])
    field_out[...] = field.astype(BF16)
    norm_out[...] = sums[:2] * (1.0 / 256.0)


def field_gradient(merged, up, stats, gain, bias, grad_hidden, sums):
    return pl.pallas_call(
        field_kernel,
        out_shape=(
            jax.ShapeDtypeStruct((512, C), BF16),
            jax.ShapeDtypeStruct((2, C), F32),
        ),
        compiler_params=params(),
        cost_estimate=pl.CostEstimate(
            flops=10**9, bytes_accessed=2 * 10**6, transcendentals=2 * 10**5
        ),
    )(merged, up, stats, gain, bias, grad_hidden, sums)


def layout_kernel(flags, mine, other, out_far, out, sems):
    first = flags[4] == 0
    copies = []
    for i in range(0, 64, 2):
        halves = []
        for ref in (mine, other):
            pair = [ref[i + k].astype(F32)[:36] for k in range(2)]
            halves.append(jnp.concatenate(pair, axis=0))
        rows = slice(36 * i, 36 * i + 72)
        out[rows, :128] = jnp.where(first, halves[0], halves[1])
        out[rows, 128:] = jnp.where(first, halves[1], halves[0])
        if i % 8 == 6:
            part = pl.ds(36 * (i - 6), 288)
            copies.append(pltpu.make_async_copy(out.at[part], out_far.at[part], sems.at[i // 8]))
            copies[-1].start()
    for copy in copies:
        copy.wait()


def lay_out(flags, mine, other):
    vmem = pl.BlockSpec(memory_space=pltpu.VMEM)
    return pl.pallas_call(
        layout_kernel,
        out_shape=pltpu.HBM((2304, C), F32),
        in_specs=[pl.BlockSpec(memory_space=pltpu.SMEM), vmem, vmem],
        out_specs=HBM,
        scratch_shapes=[pltpu.VMEM((2304, C), F32), pltpu.SemaphoreType.DMA((8,))],
        compiler_params=params(),
    )(flags, mine, other)


def copies_kernel(cells, out_far, sems):
    copies = [
        pltpu.make_async_copy(cells, out_far.at[i], sems.at[i]) for i in range(out_far.shape[0])
    ]
    for copy in copies:
        copy.start()
    for copy in copies:
        copy.wait()


def copies_of(cells):
    return pl.pallas_call(
        copies_kernel,
        out_shape=pltpu.HBM((16, 128, C), BF16),
        in_specs=[pl.BlockSpec(memory_space=pltpu.VMEM)],
        out_specs=HBM,
        scratch_shapes=[pltpu.SemaphoreType.DMA((16,))],
        compiler_params=params(),
    )(cells)


def shift(value, axis, count, step):
    return lax.ppermute(value, axis, [((i + step) % count, i) for i in range(count)])


def per_device(
    coarse,
    norm1_gain,
    norm1_bias,
    w_qkv,
    w_proj,
    second_norm2_gain,
    second_norm2_bias,
    conv_weight,
    conv_bias,
    cotangent,
):
    y, c = lax.axis_index("y"), lax.axis_index("c")
    block = lax.axis_index(ZXC)
    flags = jnp.stack([y == 0, y == 3, block == 0, block == 31, c == 1]).astype(jnp.int32)
    up = jnp.asarray(UPSAMPLE, BF16)
    taps = conv_weight.reshape(9, C, C)

    own = coarse.reshape(128, C)
    cells = lax.all_to_all(copies_of(own), ("z", "x"), 0, 0, tiled=True).reshape(2048, C)


    first = jnp.concatenate([coarse[:, 0], cotangent[:, 0]], axis=0)
    last = jnp.concatenate([coarse[:, -1], cotangent[:, -1]], axis=0)
    before = lax.ppermute(last, ZXC, [(i, i + 1) for i in range(31)])[:, None]
    after = lax.ppermute(first, ZXC, [(i + 1, i) for i in range(31)])[:, None]
    wide = jnp.concatenate([before[:16], coarse, after[:16]], axis=1).reshape(160, C)
    grad = jnp.concatenate([before[16:], cotangent, after[16:]], axis=1)
    edges = jnp.pad(jnp.stack([grad[0], grad[-1]]), ((0, 0), (0, 14), (0, 0)))
    other = shift(cells, "c", 2, 1)

    near, last, far = stats_and_rows(local_stats(cells), other, wide, edges)
    below, above, far = (
        shift(near, "y", 4, 1),
        shift(last, "y", 4, 3),
        shift(far, "y", 4, 2),
    )
    top = jnp.where(y == 0, 0, above[176:194])[None].astype(BF16)
    bottom = jnp.where(y == 3, 0, below[176:194])[None].astype(BF16)
    grad = jnp.concatenate([top, grad, bottom], axis=0)
    windows = [grad[:, b : b + 16].reshape(WIN, C) for b in range(3)]
    *sent, kept = partial_attention(
        cells, other, near, far, below, above, norm1_gain[None], norm1_bias[None], w_qkv
    )
    parts = [shift(part, "y", 4, 4 - k) for k, part in zip((1, 2, 3), sent)]
    merged, stats2 = merge(flags, parts, kept, w_proj, up)
    stats2 = lax.all_to_all(stats2.reshape(128, 1, 128), ALL, 0, 0, tiled=True)
    stats2 = stats2.reshape(128, 128)
    grad_hidden = back_conv(windows, taps)
    gain2, bias2 = second_norm2_gain[None], second_norm2_bias[None]
    kept, given, hidden = hidden_and_kernel_gradient(
        flags, merged, up, stats2, gain2, bias2, cotangent.reshape(512, C), grad_hidden
    )

    sent = pair_sum(kept, shift(given, "c", 2, 1))
    got = lax.all_to_all(sent, ("y", "z", "x"), 0, 0, tiled=True)
    fine = conv(hidden, taps, conv_bias[None])
    got, fine = lax.optimization_barrier((got, fine))

    chunk, sums = share_sum(got)
    spread = lax.all_to_all(chunk, ("y", "z", "x"), 0, 0, tiled=True)
    field, grad_norm = field_gradient(merged, up, stats2, gain2, bias2, grad_hidden, sums)
    spread, field = lax.optimization_barrier((spread, field))
    grad_conv = lay_out(flags, spread, shift(spread, "c", 2, 1)).reshape(3, 3, C, C)
    return (
        fine.reshape(32, 16, C),
        field.reshape(32, 16, C),
        grad_conv,
        grad_norm,
    )


def solution(mesh):
    split = Mesh(mesh.devices.reshape(4, 4, 4, 2), ALL)
    cells = P("y", ZXC, None)
    return jax.shard_map(
        per_device,
        mesh=split,
        in_specs=(cells,) + (P(),) * 8 + (cells,),
        out_specs=(cells, cells, P(), P()),
        check_vma=False,
    )
```

```python
import functools

import jax
import jax.numpy as jnp
import numpy as np
from jax import lax
from jax.experimental import pallas as pl
from jax.experimental.pallas import tpu as pltpu
from jax.sharding import Mesh, PartitionSpec as P

HEADS = 4
HD = 64
C = 256
SHARE = 8
EPS = 1e-05
F32 = jnp.float32
BF16 = jnp.bfloat16
VMEM_LIMIT = 50 * 2**20
HBM = pl.BlockSpec(memory_space=pltpu.HBM)
ZXC = ("z", "x", "c")
ALL = ("y", "z", "x", "c")

CELLS_IN = 192
PART = CELLS_IN + 16
STRIP = 672
KEY_BLOCK = 512
FINE_ROWS = 34
WIN = FINE_ROWS * 16


def upsample_matrix():
    def line(f):
        i = f // 2
        return {i: 0.75, (i - 1 if f % 2 == 0 else i + 1): 0.25}

    table = np.zeros((3, FINE_ROWS, 16, CELLS_IN), np.float32)
    for b in range(3):
        for fr in range(FINE_ROWS):
            for j in range(16):
                for r, wr in line(fr - 1).items():
                    for c, wc in line(j + b - 1).items():
                        table[b, fr, j, (r + 1) * 10 + c + 1] += wr * wc
    return table.reshape(3 * WIN, CELLS_IN)


UPSAMPLE = upsample_matrix()


def params(grid=None):
    return pltpu.CompilerParams(
        vmem_limit_bytes=VMEM_LIMIT,
        dimension_semantics=None if grid is None else ("arbitrary",) * grid,
    )


def in_vmem(value):
    return pltpu.with_memory_space_constraint(value, pltpu.VMEM)


def in_hbm(value):
    return pltpu.with_memory_space_constraint(value, pltpu.HBM)


def dot(a, b, contract=((1,), (0,))):
    return lax.dot_general(a, b, (contract, ((), ())), preferred_element_type=F32)


def dot_exact(a, b):
    size = a.shape[0]
    parts = jnp.concatenate([p.astype(F32) for p in split3(a)], axis=0).astype(BF16)
    result = dot(parts, b.astype(BF16))
    return result[:size] + result[size : 2 * size] + result[2 * size :]


def iota(shape, dim):
    return lax.broadcasted_iota(jnp.int32, shape, dim)


def flag(flags, index, shape):
    return jnp.broadcast_to(flags[index : index + 1, : shape[1]], shape) == 1


def split3(value):
    high = value.astype(BF16)
    rest = value - high.astype(F32)
    middle = rest.astype(BF16)
    low = (rest - middle.astype(F32)).astype(BF16)
    return high, middle, low


def group_row(mean_c, var_c):
    same = jnp.where((iota((C, C), 0) >> 3) == (iota((C, C), 1) >> 3), 1.0 / SHARE, 0.0)
    mean8 = jnp.broadcast_to(mean_c, (8, C))
    spread = mean8 - dot_exact(mean8, same)
    var8 = jnp.broadcast_to(var_c, (8, C)) + spread * spread
    to_group = jnp.where(iota((C, 128), 1) == (iota((C, 128), 0) >> 3), 1.0 / SHARE, 0.0)
    both = dot_exact(jnp.concatenate([mean8, var8], axis=0), to_group)
    return both[:8] + pltpu.roll(both[8:], 32, 1)


def combine_groups(rows):
    count = rows.shape[0]
    mean = jnp.sum(rows, axis=0, keepdims=True) / count
    off = rows - mean
    scatter = jnp.sum(off * off, axis=0, keepdims=True) / count
    mean8 = jnp.broadcast_to(mean, (8, 128))
    var8 = pltpu.roll(mean8, 96, 1) + scatter
    from_group = jnp.where(iota((128, C), 0) == (iota((128, C), 1) >> 3), 1.0, 0.0)
    both = dot_exact(jnp.concatenate([mean8, var8], axis=0), from_group)
    return both[:1], lax.rsqrt(both[8:9] + EPS)


def channel_stats(value):
    count = value.shape[0]
    mean = jnp.sum(value, axis=0, keepdims=True) / count
    off = value - mean
    return mean, jnp.sum(off * off, axis=0, keepdims=True) / count


def stats_rows(cells):
    mean, var = channel_stats(cells[...].astype(F32))
    high, middle, low = [p.astype(F32)[:1] for p in split3(group_row(mean, var))]
    upper = jnp.concatenate([high, middle], axis=1)
    return [upper, jnp.concatenate([low, jnp.zeros_like(low)], axis=1)]


def stats_kernel(cells, out):
    out[...] = jnp.concatenate(stats_rows(cells) + [jnp.zeros((6, C), F32)], axis=0)


def local_stats(cells):
    return pl.pallas_call(
        stats_kernel,
        out_shape=jax.ShapeDtypeStruct((8, C), F32),
        compiler_params=params(),
        cost_estimate=pl.CostEstimate(
            flops=3 * cells.size, bytes_accessed=2 * cells.size, transcendentals=0
        ),
    )(cells)


def rows_kernel(first, other, wide, edges, next_out, last_out, far_out):
    rows = [first[0:2, :]] + stats_rows(other) + [jnp.zeros((12, C), F32)]
    packed = jnp.concatenate(rows, axis=0).astype(BF16)
    for out in (next_out, last_out, far_out):
        out[:16, :] = packed
        out[16:176, :] = wide[...]
    next_out[176:, :] = edges[0]
    last_out[176:, :] = edges[1]


def stats_and_rows(first, other, wide, edges):
    return pl.pallas_call(
        rows_kernel,
        out_shape=(
            pltpu.VMEM((208, C), BF16),
            pltpu.VMEM((208, C), BF16),
            pltpu.VMEM((176, C), BF16),
        ),
        compiler_params=params(),
    )(first, other, wide, edges)


def attention_kernel(
    mine,
    other,
    near,
    far,
    down,
    up,
    gain,
    bias,
    w_far,
    out1,
    out2,
    out3,
    kept_far,
    keys,
    values,
    strip,
    w_qkv,
    kept,
    w_sem,
    block_sem,
    kept_sem,
):
    load = pltpu.make_async_copy(w_far, w_qkv, w_sem)
    load.start()
    rows = []
    for ref in (near, down, far, up):
        packed = ref[:16, :].astype(F32)
        for i in (0, 2):
            upper, lower = packed[i : i + 1], packed[i + 1 : i + 2]
            rows.append(upper[:, :128] + upper[:, 128:] + lower[:, :128])
    mean, inverse = combine_groups(jnp.concatenate(rows, axis=0))

    def norm(cells):
        normed = (cells.astype(F32) - mean) * inverse
        return (normed * gain[...] + bias[...]).astype(BF16)

    for i, ref in enumerate((near, down, far, up)):
        cells = ref[16:176, :].astype(F32)
        strip[10 + 160 * i : 170 + 160 * i, :] = cells
        if i == 0:
            strip[650:660, :] = cells[:10]
        if i == 3:
            strip[:10, :] = cells[150:]
    strip[660:, :] = jnp.zeros((STRIP - 660, C), F32)
    kept[PART:, :] = strip[:CELLS_IN, :].astype(BF16)
    tail = pl.ds(PART, CELLS_IN)
    keep = pltpu.make_async_copy(kept.at[tail], kept_far.at[tail], block_sem)
    keep.start()
    load.wait()

    head_of = iota((512, C), 1) >> 6
    ones = jnp.ones((512, C), BF16)
    for i in range(8):
        rows = slice(512 * i, 512 * i + 512)
        cells = (mine, other)[i // 4][512 * (i % 4) : 512 * (i % 4) + 512, :]
        both = dot(norm(cells), w_qkv[:, C:])
        both = both.astype(BF16)
        keys[rows, :] = both[:, :C]
        for head in range(HEADS):
            values[head, rows, :] = jnp.where(head_of == head, both[:, C:], ones)

    scale = HD**-0.5 * float(np.log2(np.e))
    queries = (dot(norm(strip[...]), w_qkv[:, :C]) * scale).astype(BF16)
    head_of = iota((STRIP, C), 1) >> 6
    lane = iota((STRIP, 128), 1)
    result = jnp.zeros((STRIP, C), F32)
    totals = jnp.ones((STRIP, C), F32)
    logs = jnp.zeros((STRIP, 128), F32)
    tops = jnp.zeros((STRIP, 128), F32)
    for head in range(HEADS):
        own = head_of == head
        masked = jnp.where(own, queries, jnp.zeros_like(queries))
        best, mixed = None, None
        for i in range(4096 // KEY_BLOCK):
            rows = slice(KEY_BLOCK * i, KEY_BLOCK * (i + 1))
            scores = dot(masked, keys[rows, :], ((1,), (1,)))
            top = jnp.max(scores, axis=1, keepdims=True)
            fresh = top if i == 0 else jnp.maximum(best, top)
            product = dot(jnp.exp2(scores - fresh).astype(BF16), values[head, rows, :])
            mixed = product if i == 0 else mixed * jnp.exp2(best - fresh) + product
            best = fresh
        result = jnp.where(own, mixed, result)
        totals = jnp.where(own, pltpu.roll(mixed, HD, 1), totals)
        spot = 0 if head else 128
        logs = jnp.where(lane == head, mixed[:, spot : spot + 128], logs)
        tops = jnp.where(lane == head, best, tops)
    result = (result / totals).astype(BF16)
    logs = tops + jnp.log2(jnp.where(lane < HEADS, logs, 1.0))
    high, middle, low = [p.astype(F32) for p in split3(logs)]
    packed = high + pltpu.roll(middle, 4, 1) + pltpu.roll(low, 8, 1)
    head = pl.ds(0, PART)
    copy = pltpu.make_async_copy(kept.at[head], kept_far.at[head], kept_sem)
    for step, out in enumerate((kept, out1, out2, out3)):
        rows = slice(160 * step, 160 * step + CELLS_IN)
        out[:CELLS_IN, :] = result[rows]
        turned = jnp.concatenate([packed[rows], jnp.zeros((64, 128), F32)], axis=0).T[:16]
        out[CELLS_IN:PART, :] = turned.astype(BF16)
        if step == 0:
            copy.start()
    keep.wait()
    copy.wait()


def partial_attention(mine, other, near, far, down, up, gain, bias, w_qkv):
    vmem = pl.BlockSpec(memory_space=pltpu.VMEM)
    return pl.pallas_call(
        attention_kernel,
        out_shape=(jax.ShapeDtypeStruct((PART, C), BF16),) * 3
        + (pltpu.HBM((PART + CELLS_IN, C), BF16),),
        in_specs=[vmem] * 8 + [HBM],
        out_specs=(vmem, vmem, vmem, HBM),
        scratch_shapes=[
            pltpu.VMEM((4096, C), BF16),
            pltpu.VMEM((HEADS, 4096, C), BF16),
            pltpu.VMEM((STRIP, C), F32),
            pltpu.VMEM((C, 3 * C), BF16),
            pltpu.VMEM((PART + CELLS_IN, C), BF16),
            pltpu.SemaphoreType.DMA,
            pltpu.SemaphoreType.DMA,
            pltpu.SemaphoreType.DMA,
        ],
        compiler_params=params(),
    )(mine, other, near, in_vmem(far), in_vmem(down), in_vmem(up), gain, bias, in_hbm(w_qkv))


def merge_kernel(
    flags, p1, p2, p3, kept_far, w_far, up, merged_out, stats_out, kept, w_proj, kept_sem, w_sem
):
    loads = [
        pltpu.make_async_copy(kept_far, kept, kept_sem),
        pltpu.make_async_copy(w_far, w_proj, w_sem),
    ]
    for load in loads:
        load.start()
    parts = (p1, p2, p3, kept)
    logs = []
    for part in parts:
        if part is kept:
            loads[0].wait()
        tail = part[CELLS_IN:PART, :].astype(F32)
        logs.append(tail[0:4] + tail[4:8] + tail[8:12])
    top = functools.reduce(jnp.maximum, logs)
    shares = [jnp.exp2(v - top) for v in logs]
    total = sum(shares)
    spread = jnp.where((iota((16, C), 1) >> 6) == (iota((16, C), 0) & 3), 1.0, 0.0).astype(BF16)
    attended = jnp.zeros((CELLS_IN, C), F32)
    for i, part in enumerate(parts):
        pieces = [p.astype(F32) for p in split3((shares[i] / total)[:, :CELLS_IN])]
        pieces.append(jnp.zeros_like(pieces[0]))
        wide = dot(jnp.concatenate(pieces, axis=0).astype(BF16), spread, ((0,), (0,)))
        attended = attended + wide * part[:CELLS_IN, :].astype(F32)
    loads[1].wait()
    merged = kept[PART:, :].astype(F32) + dot(attended.astype(BF16), w_proj[...])
    cell = iota((CELLS_IN, C), 0)
    col = lax.rem(cell, 10)
    outside = (
        ((cell < 10) & flag(flags, 0, cell.shape))
        | ((cell >= 170) & flag(flags, 1, cell.shape))
        | ((col == 0) & flag(flags, 2, cell.shape))
        | ((col == 9) & flag(flags, 3, cell.shape))
        | (cell >= 180)
    )
    merged = jnp.where(outside, 0.0, merged).astype(BF16)
    merged_out[...] = merged
    field = dot(up[WIN + 16 : WIN + 528, :], merged)
    mean, var = channel_stats(field)
    stats_out[...] = jnp.broadcast_to(group_row(mean, var)[:1], stats_out.shape)


def merge(flags, parts, kept, w_proj, up):
    vmem = pl.BlockSpec(memory_space=pltpu.VMEM)
    return pl.pallas_call(
        merge_kernel,
        out_shape=(
            jax.ShapeDtypeStruct((CELLS_IN, C), BF16),
            jax.ShapeDtypeStruct((128, 128), F32),
        ),
        in_specs=[pl.BlockSpec(memory_space=pltpu.VMEM), vmem, vmem, vmem, HBM, HBM, vmem],
        out_specs=(vmem, vmem),
        scratch_shapes=[
            pltpu.VMEM((PART + CELLS_IN, C), BF16),
            pltpu.VMEM((C, C), BF16),
            pltpu.SemaphoreType.DMA,
            pltpu.SemaphoreType.DMA,
        ],
        compiler_params=params(),
    )(flags, *parts, in_hbm(kept), in_hbm(w_proj), up)


def back_kernel(c0, c1, c2, weight, out):
    windows = (c0, c1, c2)
    total = jnp.zeros((512, C), F32)
    for a in range(3):
        for b in range(3):
            window = windows[2 - b][16 * (2 - a) : 16 * (2 - a) + 512, :]
            total = total + dot(window, weight[3 * a + b], ((1,), (1,)))
    out[...] = total


def back_conv(windows, weight):
    return pl.pallas_call(
        back_kernel,
        out_shape=jax.ShapeDtypeStruct((512, C), F32),
        compiler_params=params(),
        cost_estimate=pl.CostEstimate(
            flops=9 * 2 * 512 * C * C, bytes_accessed=3 * 10**6, transcendentals=0
        ),
    )(*windows, weight)


def hidden_kernel(
    flags,
    merged,
    up,
    stats,
    gain,
    bias,
    cot,
    grad_hidden,
    kept,
    given,
    hidden_far,
    hidden,
    sem,
):
    mean, inverse = combine_groups(stats[...])
    row = iota((WIN, C), 0)
    col = row & 15
    for b in range(3):
        field = dot(up[b * WIN : (b + 1) * WIN, :], merged[...])
        xhat = (field - mean) * inverse
        shifted = xhat * gain[...] + bias[...]
        sig = 0.5 * jnp.tanh(0.5 * shifted) + 0.5
        outside = ((row < 16) & flag(flags, 0, row.shape)) | (
            (row >= 528) & flag(flags, 1, row.shape)
        )
        if b == 0:
            outside = outside | ((col == 0) & flag(flags, 2, row.shape))
        if b == 2:
            outside = outside | ((col == 15) & flag(flags, 3, row.shape))
        hidden[b] = jnp.where(outside, 0.0, shifted * sig).astype(BF16)
        if b == 1:
            inner = slice(16, 528)
            s, t = sig[inner], shifted[inner]
            grad_shift = grad_hidden[...] * s * (1.0 + t * (1.0 - s))
            sum_w = jnp.sum(grad_shift * xhat[inner], axis=0, keepdims=True)
            sum_b = jnp.sum(grad_shift, axis=0, keepdims=True)
            rows = []
            for part in range(3):
                for value in (sum_w, sum_b):
                    piece = split3(value)[part].astype(F32)
                    rows += [piece[:, :128], piece[:, 128:]]
            tail = jnp.concatenate(rows + [jnp.zeros((4, 128), F32)], axis=0).astype(BF16)
            kept[2304:, :] = tail
            given[2304:, :] = tail
    keep = pltpu.make_async_copy(hidden, hidden_far, sem)
    keep.start()
    second = flag(flags, 4, (C, 128))
    for a in range(3):
        for b in range(3):
            rows = slice((3 * a + b) * C, (3 * a + b + 1) * C)
            product = dot(hidden[b, 16 * a : 16 * a + 512, :], cot[...], ((0,), (0,)))
            left, right = product[:, :128], product[:, 128:]
            kept[rows, :] = jnp.where(second, right, left).astype(BF16)
            given[rows, :] = jnp.where(second, left, right).astype(BF16)
    keep.wait()


def hidden_and_kernel_gradient(flags, merged, up, stats, gain, bias, cot, grad_hidden):
    vmem = pl.BlockSpec(memory_space=pltpu.VMEM)
    return pl.pallas_call(
        hidden_kernel,
        out_shape=(
            jax.ShapeDtypeStruct((2320, 128), BF16),
            jax.ShapeDtypeStruct((2320, 128), BF16),
            pltpu.HBM((3, WIN, C), BF16),
        ),
        in_specs=[pl.BlockSpec(memory_space=pltpu.VMEM)] + [vmem] * 7,
        out_specs=(vmem, vmem, HBM),
        scratch_shapes=[pltpu.VMEM((3, WIN, C), BF16), pltpu.SemaphoreType.DMA],
        compiler_params=params(),
    )(flags, merged, up, stats, gain, bias, cot, grad_hidden)


def conv_kernel(hidden, weight, conv_bias, fine_out):
    total = jnp.zeros((512, C), F32) + conv_bias[...]
    for a in range(3):
        for b in range(3):
            total = total + dot(hidden[b, 16 * a : 16 * a + 512, :], weight[3 * a + b])
    fine_out[...] = total.astype(BF16)


def conv(hidden, weight, conv_bias):
    return pl.pallas_call(
        conv_kernel,
        out_shape=jax.ShapeDtypeStruct((512, C), BF16),
        compiler_params=params(),
        cost_estimate=pl.CostEstimate(
            flops=9 * 2 * 512 * C * C, bytes_accessed=3 * 10**6, transcendentals=0
        ),
    )(hidden, weight, conv_bias)


def pair_kernel(flags, kept, got, out_far, total, out, sems):
    total[...] = kept[...].astype(F32) + got[...].astype(F32)
    tails = [r[2304:, :].astype(F32) for r in (kept, got)]
    sums = sum(t[0:4] + t[4:8] + t[8:12] for t in tails)
    sums = jnp.where(flag(flags, 4, (2, 128)), sums[2:4], sums[0:2])
    parts = [p.astype(F32) for p in split3(sums)[:2]]
    tail = jnp.concatenate([jnp.zeros((36, 128), F32)] + parts, axis=0)
    own = iota((40, 128), 0) < 36
    copies = []
    for i in range(64):
        out[i] = jnp.where(own, total[36 * i : 36 * i + 40, :], tail).astype(BF16)
        if i % 16 == 15:
            part = pl.ds(i - 15, 16)
            copies.append(pltpu.make_async_copy(out.at[part], out_far.at[part], sems.at[i // 16]))
            copies[-1].start()
    for copy in copies:
        copy.wait()


def pair_sum(flags, kept, got):
    return pl.pallas_call(
        pair_kernel,
        out_shape=pltpu.HBM((64, 40, 128), BF16),
        in_specs=[
            pl.BlockSpec(memory_space=pltpu.VMEM),
            pl.BlockSpec(memory_space=pltpu.VMEM),
            pl.BlockSpec(memory_space=pltpu.VMEM),
        ],
        out_specs=HBM,
        scratch_shapes=[
            pltpu.VMEM((2320, 128), F32),
            pltpu.VMEM((64, 40, 128), BF16),
            pltpu.SemaphoreType.DMA((4,)),
        ],
        compiler_params=params(),
    )(flags, kept, got)


def share_kernel(got, out_far, sums, chunk, sems):
    total = jnp.sum(got[...].astype(F32), axis=0)
    chunk[...] = jnp.broadcast_to((total * (1.0 / 256.0)).astype(BF16)[None], chunk.shape)
    size = chunk.shape[0]
    copies = [
        pltpu.make_async_copy(chunk, out_far.at[pl.ds(size * i, size)], sems.at[i])
        for i in range(out_far.shape[0] // size)
    ]
    for copy in copies:
        copy.start()
    halves = total[36:38] + total[38:40]
    row = jnp.concatenate([halves[0:1], halves[1:2]], axis=1)
    sums[...] = jnp.broadcast_to(row, sums.shape)
    for copy in copies:
        copy.wait()


def share_sum(got):
    vmem = pl.BlockSpec(memory_space=pltpu.VMEM)
    return pl.pallas_call(
        share_kernel,
        out_shape=(pltpu.HBM((64, 40, 128), BF16), jax.ShapeDtypeStruct((8, C), F32)),
        in_specs=[vmem],
        out_specs=(HBM, vmem),
        scratch_shapes=[pltpu.VMEM((16, 40, 128), BF16), pltpu.SemaphoreType.DMA((4,))],
        compiler_params=params(),
    )(got)


def field_kernel(
    flags, merged, up, stats, gain, bias, grad_hidden, mine, other, field_out, norm_out
):
    second = flag(flags, 4, (8, C))
    weight = jnp.where(second, other[...], mine[...])
    plain = jnp.where(second, mine[...], other[...])
    sums = jnp.where(iota((8, C), 0) == 0, weight, plain)
    mean, inverse = combine_groups(stats[...])
    value = dot(up[WIN + 16 : WIN + 528, :], merged[...])
    xhat = (value - mean) * inverse
    shifted = xhat * gain[...] + bias[...]
    sig = 0.5 * jnp.tanh(0.5 * shifted) + 0.5
    grad_shift = grad_hidden[...] * sig * (1.0 + shifted * (1.0 - sig))
    same = jnp.where((iota((C, C), 0) >> 3) == (iota((C, C), 1) >> 3), 1.0, 0.0)
    means = dot_exact(sums * gain[...], same) * (1.0 / (65536 * SHARE))
    field = inverse * (grad_shift * gain[...] - means[1:2] - xhat * means[0:1])
    field_out[...] = field.astype(BF16)
    norm_out[...] = sums[:2] * (1.0 / 256.0)


def field_gradient(flags, merged, up, stats, gain, bias, grad_hidden, mine, other):
    vmem = pl.BlockSpec(memory_space=pltpu.VMEM)
    return pl.pallas_call(
        field_kernel,
        out_shape=(
            jax.ShapeDtypeStruct((512, C), BF16),
            jax.ShapeDtypeStruct((2, C), F32),
        ),
        in_specs=[pl.BlockSpec(memory_space=pltpu.VMEM)] + [vmem] * 8,
        compiler_params=params(),
        cost_estimate=pl.CostEstimate(
            flops=10**9, bytes_accessed=2 * 10**6, transcendentals=2 * 10**5
        ),
    )(flags, merged, up, stats, gain, bias, grad_hidden, mine, other)


def layout_kernel(flags, mine, other, out_far, out, sems):
    second = flag(flags, 4, (72, 128))
    copies = []
    for i in range(0, 64, 2):
        halves = []
        for ref in (mine, other):
            pair = [ref[i + k].astype(F32)[:36] for k in range(2)]
            halves.append(jnp.concatenate(pair, axis=0))
        rows = slice(36 * i, 36 * i + 72)
        out[rows, :128] = jnp.where(second, halves[1], halves[0])
        out[rows, 128:] = jnp.where(second, halves[0], halves[1])
        if i % 8 == 6:
            part = pl.ds(36 * (i - 6), 288)
            copies.append(pltpu.make_async_copy(out.at[part], out_far.at[part], sems.at[i // 8]))
            copies[-1].start()
    for copy in copies:
        copy.wait()


def lay_out(flags, mine, other):
    vmem = pl.BlockSpec(memory_space=pltpu.VMEM)
    return pl.pallas_call(
        layout_kernel,
        out_shape=pltpu.HBM((2304, C), F32),
        in_specs=[pl.BlockSpec(memory_space=pltpu.VMEM), vmem, vmem],
        out_specs=HBM,
        scratch_shapes=[pltpu.VMEM((2304, C), F32), pltpu.SemaphoreType.DMA((8,))],
        compiler_params=params(),
    )(flags, mine, other)


def copies_kernel(cells_far, out_far, cells, sem, sems):
    load = pltpu.make_async_copy(cells_far, cells, sem)
    load.start()
    load.wait()
    copies = [
        pltpu.make_async_copy(cells, out_far.at[i], sems.at[i]) for i in range(out_far.shape[0])
    ]
    for copy in copies:
        copy.start()
    for copy in copies:
        copy.wait()


def copies_of(cells):
    return pl.pallas_call(
        copies_kernel,
        out_shape=pltpu.HBM((16, 128, C), BF16),
        in_specs=[HBM],
        out_specs=HBM,
        scratch_shapes=[
            pltpu.VMEM((128, C), BF16),
            pltpu.SemaphoreType.DMA,
            pltpu.SemaphoreType.DMA((16,)),
        ],
        compiler_params=params(),
    )(in_hbm(cells))


def shift(value, axis, count, step):
    return lax.ppermute(value, axis, [((i + step) % count, i) for i in range(count)])


def per_device(
    coarse,
    norm1_gain,
    norm1_bias,
    w_qkv,
    w_proj,
    second_norm2_gain,
    second_norm2_bias,
    conv_weight,
    conv_bias,
    cotangent,
):
    y, c = lax.axis_index("y"), lax.axis_index("c")
    block = lax.axis_index(ZXC)
    marks = [y == 0, y == 3, block == 0, block == 31, c == 1, c == 1, c == 1, c == 1]
    flags = jnp.broadcast_to(jnp.stack(marks).astype(jnp.int32)[:, None], (8, C))
    up = jnp.asarray(UPSAMPLE, BF16)
    taps = conv_weight.reshape(9, C, C)

    own = coarse.reshape(128, C)
    cells = lax.all_to_all(copies_of(own), ("z", "x"), 0, 0, tiled=True).reshape(2048, C)


    first = jnp.concatenate([coarse[:, 0], cotangent[:, 0]], axis=0)
    last = jnp.concatenate([coarse[:, -1], cotangent[:, -1]], axis=0)
    before = lax.ppermute(last, ZXC, [(i, i + 1) for i in range(31)])[:, None]
    after = lax.ppermute(first, ZXC, [(i + 1, i) for i in range(31)])[:, None]
    wide = jnp.concatenate([before[:16], coarse, after[:16]], axis=1).reshape(160, C)
    grad = jnp.concatenate([before[16:], cotangent, after[16:]], axis=1)
    edges = jnp.pad(jnp.stack([grad[0], grad[-1]]), ((0, 0), (0, 14), (0, 0)))
    other = shift(cells, "c", 2, 1)

    near, last, far = stats_and_rows(local_stats(cells), other, wide, edges)
    below, above, far = (
        shift(near, "y", 4, 1),
        shift(last, "y", 4, 3),
        shift(far, "y", 4, 2),
    )
    top = jnp.where(y == 0, 0, above[176:194])[None].astype(BF16)
    bottom = jnp.where(y == 3, 0, below[176:194])[None].astype(BF16)
    grad = jnp.concatenate([top, grad, bottom], axis=0)
    windows = [grad[:, b : b + 16].reshape(WIN, C) for b in range(3)]
    *sent, kept = partial_attention(
        cells, other, near, far, below, above, norm1_gain[None], norm1_bias[None], w_qkv
    )
    parts = [shift(part, "y", 4, 4 - k) for k, part in zip((1, 2, 3), sent)]
    merged, stats2 = merge(flags, parts, kept, w_proj, up)
    stats2 = lax.all_to_all(stats2.reshape(128, 1, 128), ALL, 0, 0, tiled=True)
    stats2 = stats2.reshape(128, 128)
    grad_hidden = back_conv(windows, taps)
    gain2, bias2 = second_norm2_gain[None], second_norm2_bias[None]
    kept, given, hidden = hidden_and_kernel_gradient(
        flags, merged, up, stats2, gain2, bias2, cotangent.reshape(512, C), grad_hidden
    )

    sent = pair_sum(flags, kept, shift(given, "c", 2, 1))
    got = lax.all_to_all(sent, ("y", "z", "x"), 0, 0, tiled=True)
    fine = conv(hidden, taps, conv_bias[None])
    got, fine = lax.optimization_barrier((got, fine))

    chunk, sums = share_sum(got)
    spread = lax.all_to_all(chunk, ("y", "z", "x"), 0, 0, tiled=True)
    field, grad_norm = field_gradient(
        flags, merged, up, stats2, gain2, bias2, grad_hidden, sums, shift(sums, "c", 2, 1)
    )
    spread, field = lax.optimization_barrier((spread, field))
    grad_conv = lay_out(flags, spread, shift(spread, "c", 2, 1)).reshape(3, 3, C, C)
    return (
        fine.reshape(32, 16, C),
        field.reshape(32, 16, C),
        grad_conv,
        grad_norm,
    )


def solution(mesh):
    split = Mesh(mesh.devices.reshape(4, 4, 4, 2), ALL)
    cells = P("y", ZXC, None)
    return jax.shard_map(
        per_device,
        mesh=split,
        in_specs=(cells,) + (P(),) * 8 + (cells,),
        out_specs=(cells, cells, P(), P()),
        check_vma=False,
    )
```

```python
import functools

import jax
import jax.numpy as jnp
import numpy as np
from jax import lax
from jax.experimental import pallas as pl
from jax.experimental.pallas import tpu as pltpu
from jax.sharding import Mesh, PartitionSpec as P

HEADS = 4
HD = 64
C = 256
SHARE = 8
EPS = 1e-05
F32 = jnp.float32
BF16 = jnp.bfloat16
VMEM_LIMIT = 50 * 2**20
HBM = pl.BlockSpec(memory_space=pltpu.HBM)
ZXC = ("z", "x", "c")
ALL = ("y", "z", "x", "c")

CELLS_IN = 192
PART = CELLS_IN + 16
STRIP = 672
KEY_BLOCK = 512
FINE_ROWS = 34
WIN = FINE_ROWS * 16


def upsample_matrix():
    def line(f):
        i = f // 2
        return {i: 0.75, (i - 1 if f % 2 == 0 else i + 1): 0.25}

    table = np.zeros((3, FINE_ROWS, 16, CELLS_IN), np.float32)
    for b in range(3):
        for fr in range(FINE_ROWS):
            for j in range(16):
                for r, wr in line(fr - 1).items():
                    for c, wc in line(j + b - 1).items():
                        table[b, fr, j, (r + 1) * 10 + c + 1] += wr * wc
    return table.reshape(3 * WIN, CELLS_IN)


UPSAMPLE = upsample_matrix()


def params(grid=None):
    return pltpu.CompilerParams(
        vmem_limit_bytes=VMEM_LIMIT,
        dimension_semantics=None if grid is None else ("arbitrary",) * grid,
    )


def in_vmem(value):
    return pltpu.with_memory_space_constraint(value, pltpu.VMEM)


def in_hbm(value):
    return pltpu.with_memory_space_constraint(value, pltpu.HBM)


def dot(a, b, contract=((1,), (0,))):
    return lax.dot_general(a, b, (contract, ((), ())), preferred_element_type=F32)


def dot_exact(a, b):
    size = a.shape[0]
    parts = jnp.concatenate([p.astype(F32) for p in split3(a)], axis=0).astype(BF16)
    result = dot(parts, b.astype(BF16))
    return result[:size] + result[size : 2 * size] + result[2 * size :]


def iota(shape, dim):
    return lax.broadcasted_iota(jnp.int32, shape, dim)


def flag(flags, index, shape):
    return jnp.broadcast_to(flags[index : index + 1, : shape[1]], shape) == 1


def split3(value):
    high = value.astype(BF16)
    rest = value - high.astype(F32)
    middle = rest.astype(BF16)
    low = (rest - middle.astype(F32)).astype(BF16)
    return high, middle, low


def group_row(mean_c, var_c):
    same = jnp.where((iota((C, C), 0) >> 3) == (iota((C, C), 1) >> 3), 1.0 / SHARE, 0.0)
    mean8 = jnp.broadcast_to(mean_c, (8, C))
    spread = mean8 - dot_exact(mean8, same)
    var8 = jnp.broadcast_to(var_c, (8, C)) + spread * spread
    to_group = jnp.where(iota((C, 128), 1) == (iota((C, 128), 0) >> 3), 1.0 / SHARE, 0.0)
    both = dot_exact(jnp.concatenate([mean8, var8], axis=0), to_group)
    return both[:8] + pltpu.roll(both[8:], 32, 1)


def combine_groups(rows):
    count = rows.shape[0]
    mean = jnp.sum(rows, axis=0, keepdims=True) / count
    off = rows - mean
    scatter = jnp.sum(off * off, axis=0, keepdims=True) / count
    mean8 = jnp.broadcast_to(mean, (8, 128))
    var8 = pltpu.roll(mean8, 96, 1) + scatter
    from_group = jnp.where(iota((128, C), 0) == (iota((128, C), 1) >> 3), 1.0, 0.0)
    both = dot_exact(jnp.concatenate([mean8, var8], axis=0), from_group)
    return both[:1], lax.rsqrt(both[8:9] + EPS)


def channel_stats(value):
    count = value.shape[0]
    mean = jnp.sum(value, axis=0, keepdims=True) / count
    off = value - mean
    return mean, jnp.sum(off * off, axis=0, keepdims=True) / count


def stats_rows(cells):
    mean, var = channel_stats(cells[...].astype(F32))
    high, middle, low = [p.astype(F32)[:1] for p in split3(group_row(mean, var))]
    upper = jnp.concatenate([high, middle], axis=1)
    return [upper, jnp.concatenate([low, jnp.zeros_like(low)], axis=1)]


def stats_kernel(cells, out):
    out[...] = jnp.concatenate(stats_rows(cells) + [jnp.zeros((6, C), F32)], axis=0)


def local_stats(cells):
    return pl.pallas_call(
        stats_kernel,
        out_shape=jax.ShapeDtypeStruct((8, C), F32),
        compiler_params=params(),
        cost_estimate=pl.CostEstimate(
            flops=3 * cells.size, bytes_accessed=2 * cells.size, transcendentals=0
        ),
    )(cells)


def rows_kernel(first, other, wide, edges, next_out, last_out, far_out):
    rows = [first[0:2, :], other[0:2, :], jnp.zeros((12, C), F32)]
    packed = jnp.concatenate(rows, axis=0).astype(BF16)
    for out in (next_out, last_out, far_out):
        out[:16, :] = packed
        out[16:176, :] = wide[...]
    next_out[176:, :] = edges[0]
    last_out[176:, :] = edges[1]


def stats_and_rows(first, other, wide, edges):
    return pl.pallas_call(
        rows_kernel,
        out_shape=(
            pltpu.VMEM((208, C), BF16),
            pltpu.VMEM((208, C), BF16),
            pltpu.VMEM((176, C), BF16),
        ),
        compiler_params=params(),
    )(first, other, wide, edges)


def attention_kernel(
    mine,
    other,
    near,
    far,
    down,
    up,
    gain,
    bias,
    w_far,
    out1,
    out2,
    out3,
    kept_far,
    keys,
    values,
    strip,
    w_qkv,
    kept,
    w_sem,
    block_sem,
    kept_sem,
):
    load = pltpu.make_async_copy(w_far, w_qkv, w_sem)
    load.start()
    rows = []
    for ref in (near, down, far, up):
        packed = ref[:16, :].astype(F32)
        for i in (0, 2):
            upper, lower = packed[i : i + 1], packed[i + 1 : i + 2]
            rows.append(upper[:, :128] + upper[:, 128:] + lower[:, :128])
    mean, inverse = combine_groups(jnp.concatenate(rows, axis=0))

    def norm(cells):
        normed = (cells.astype(F32) - mean) * inverse
        return (normed * gain[...] + bias[...]).astype(BF16)

    for i, ref in enumerate((near, down, far, up)):
        cells = ref[16:176, :].astype(F32)
        strip[10 + 160 * i : 170 + 160 * i, :] = cells
        if i == 0:
            strip[650:660, :] = cells[:10]
        if i == 3:
            strip[:10, :] = cells[150:]
    strip[660:, :] = jnp.zeros((STRIP - 660, C), F32)
    kept[PART:, :] = strip[:CELLS_IN, :].astype(BF16)
    tail = pl.ds(PART, CELLS_IN)
    keep = pltpu.make_async_copy(kept.at[tail], kept_far.at[tail], block_sem)
    keep.start()
    load.wait()

    head_of = iota((512, C), 1) >> 6
    ones = jnp.ones((512, C), BF16)
    for i in range(8):
        rows = slice(512 * i, 512 * i + 512)
        cells = (mine, other)[i // 4][512 * (i % 4) : 512 * (i % 4) + 512, :]
        both = dot(norm(cells), w_qkv[:, C:])
        both = both.astype(BF16)
        keys[rows, :] = both[:, :C]
        for head in range(HEADS):
            values[head, rows, :] = jnp.where(head_of == head, both[:, C:], ones)

    scale = HD**-0.5 * float(np.log2(np.e))
    queries = (dot(norm(strip[...]), w_qkv[:, :C]) * scale).astype(BF16)
    head_of = iota((STRIP, C), 1) >> 6
    lane = iota((STRIP, 128), 1)
    result = jnp.zeros((STRIP, C), F32)
    totals = jnp.ones((STRIP, C), F32)
    logs = jnp.zeros((STRIP, 128), F32)
    tops = jnp.zeros((STRIP, 128), F32)
    for head in range(HEADS):
        own = head_of == head
        masked = jnp.where(own, queries, jnp.zeros_like(queries))
        best, mixed = None, None
        for i in range(4096 // KEY_BLOCK):
            rows = slice(KEY_BLOCK * i, KEY_BLOCK * (i + 1))
            scores = dot(masked, keys[rows, :], ((1,), (1,)))
            top = jnp.max(scores, axis=1, keepdims=True)
            fresh = top if i == 0 else jnp.maximum(best, top)
            product = dot(jnp.exp2(scores - fresh).astype(BF16), values[head, rows, :])
            mixed = product if i == 0 else mixed * jnp.exp2(best - fresh) + product
            best = fresh
        result = jnp.where(own, mixed, result)
        totals = jnp.where(own, pltpu.roll(mixed, HD, 1), totals)
        spot = 0 if head else 128
        logs = jnp.where(lane == head, mixed[:, spot : spot + 128], logs)
        tops = jnp.where(lane == head, best, tops)
    result = (result / totals).astype(BF16)
    logs = tops + jnp.log2(jnp.where(lane < HEADS, logs, 1.0))
    high, middle, low = [p.astype(F32) for p in split3(logs)]
    packed = high + pltpu.roll(middle, 4, 1) + pltpu.roll(low, 8, 1)
    head = pl.ds(0, PART)
    copy = pltpu.make_async_copy(kept.at[head], kept_far.at[head], kept_sem)
    for step, out in enumerate((kept, out1, out2, out3)):
        rows = slice(160 * step, 160 * step + CELLS_IN)
        out[:CELLS_IN, :] = result[rows]
        turned = jnp.concatenate([packed[rows], jnp.zeros((64, 128), F32)], axis=0).T[:16]
        out[CELLS_IN:PART, :] = turned.astype(BF16)
        if step == 0:
            copy.start()
    keep.wait()
    copy.wait()


def partial_attention(mine, other, near, far, down, up, gain, bias, w_qkv):
    vmem = pl.BlockSpec(memory_space=pltpu.VMEM)
    return pl.pallas_call(
        attention_kernel,
        out_shape=(jax.ShapeDtypeStruct((PART, C), BF16),) * 3
        + (pltpu.HBM((PART + CELLS_IN, C), BF16),),
        in_specs=[vmem] * 8 + [HBM],
        out_specs=(vmem, vmem, vmem, HBM),
        scratch_shapes=[
            pltpu.VMEM((4096, C), BF16),
            pltpu.VMEM((HEADS, 4096, C), BF16),
            pltpu.VMEM((STRIP, C), F32),
            pltpu.VMEM((C, 3 * C), BF16),
            pltpu.VMEM((PART + CELLS_IN, C), BF16),
            pltpu.SemaphoreType.DMA,
            pltpu.SemaphoreType.DMA,
            pltpu.SemaphoreType.DMA,
        ],
        compiler_params=params(),
    )(mine, other, near, in_vmem(far), in_vmem(down), in_vmem(up), gain, bias, in_hbm(w_qkv))


def merge_kernel(
    flags, p1, p2, p3, kept_far, w_far, up, merged_out, stats_out, kept, w_proj, kept_sem, w_sem
):
    loads = [
        pltpu.make_async_copy(kept_far, kept, kept_sem),
        pltpu.make_async_copy(w_far, w_proj, w_sem),
    ]
    for load in loads:
        load.start()
    parts = (p1, p2, p3, kept)
    logs = []
    for part in parts:
        if part is kept:
            loads[0].wait()
        tail = part[CELLS_IN:PART, :].astype(F32)
        logs.append(tail[0:4] + tail[4:8] + tail[8:12])
    top = functools.reduce(jnp.maximum, logs)
    shares = [jnp.exp2(v - top) for v in logs]
    total = sum(shares)
    spread = jnp.where((iota((16, C), 1) >> 6) == (iota((16, C), 0) & 3), 1.0, 0.0).astype(BF16)
    attended = jnp.zeros((CELLS_IN, C), F32)
    for i, part in enumerate(parts):
        pieces = [p.astype(F32) for p in split3((shares[i] / total)[:, :CELLS_IN])]
        pieces.append(jnp.zeros_like(pieces[0]))
        wide = dot(jnp.concatenate(pieces, axis=0).astype(BF16), spread, ((0,), (0,)))
        attended = attended + wide * part[:CELLS_IN, :].astype(F32)
    loads[1].wait()
    merged = kept[PART:, :].astype(F32) + dot(attended.astype(BF16), w_proj[...])
    cell = iota((CELLS_IN, C), 0)
    col = lax.rem(cell, 10)
    outside = (
        ((cell < 10) & flag(flags, 0, cell.shape))
        | ((cell >= 170) & flag(flags, 1, cell.shape))
        | ((col == 0) & flag(flags, 2, cell.shape))
        | ((col == 9) & flag(flags, 3, cell.shape))
        | (cell >= 180)
    )
    merged = jnp.where(outside, 0.0, merged).astype(BF16)
    merged_out[...] = merged
    field = dot(up[WIN + 16 : WIN + 528, :], merged)
    mean, var = channel_stats(field)
    stats_out[...] = jnp.broadcast_to(group_row(mean, var)[:1], stats_out.shape)


def merge(flags, parts, kept, w_proj, up):
    vmem = pl.BlockSpec(memory_space=pltpu.VMEM)
    return pl.pallas_call(
        merge_kernel,
        out_shape=(
            jax.ShapeDtypeStruct((CELLS_IN, C), BF16),
            jax.ShapeDtypeStruct((128, 128), F32),
        ),
        in_specs=[pl.BlockSpec(memory_space=pltpu.VMEM), vmem, vmem, vmem, HBM, HBM, vmem],
        out_specs=(vmem, vmem),
        scratch_shapes=[
            pltpu.VMEM((PART + CELLS_IN, C), BF16),
            pltpu.VMEM((C, C), BF16),
            pltpu.SemaphoreType.DMA,
            pltpu.SemaphoreType.DMA,
        ],
        compiler_params=params(),
    )(flags, *parts, in_hbm(kept), in_hbm(w_proj), up)


def back_kernel(c0, c1, c2, weight, out):
    windows = (c0, c1, c2)
    total = jnp.zeros((512, C), F32)
    for a in range(3):
        for b in range(3):
            window = windows[2 - b][16 * (2 - a) : 16 * (2 - a) + 512, :]
            total = total + dot(window, weight[3 * a + b], ((1,), (1,)))
    out[...] = total


def back_conv(windows, weight):
    return pl.pallas_call(
        back_kernel,
        out_shape=jax.ShapeDtypeStruct((512, C), F32),
        compiler_params=params(),
        cost_estimate=pl.CostEstimate(
            flops=9 * 2 * 512 * C * C, bytes_accessed=3 * 10**6, transcendentals=0
        ),
    )(*windows, weight)


def hidden_kernel(
    flags,
    merged,
    up,
    stats,
    gain,
    bias,
    cot,
    grad_hidden,
    kept,
    given,
    hidden_far,
    hidden,
    sem,
):
    mean, inverse = combine_groups(stats[...])
    row = iota((WIN, C), 0)
    col = row & 15
    for b in range(3):
        field = dot(up[b * WIN : (b + 1) * WIN, :], merged[...])
        xhat = (field - mean) * inverse
        shifted = xhat * gain[...] + bias[...]
        sig = 0.5 * jnp.tanh(0.5 * shifted) + 0.5
        outside = ((row < 16) & flag(flags, 0, row.shape)) | (
            (row >= 528) & flag(flags, 1, row.shape)
        )
        if b == 0:
            outside = outside | ((col == 0) & flag(flags, 2, row.shape))
        if b == 2:
            outside = outside | ((col == 15) & flag(flags, 3, row.shape))
        hidden[b] = jnp.where(outside, 0.0, shifted * sig).astype(BF16)
        if b == 1:
            inner = slice(16, 528)
            s, t = sig[inner], shifted[inner]
            grad_shift = grad_hidden[...] * s * (1.0 + t * (1.0 - s))
            sum_w = jnp.sum(grad_shift * xhat[inner], axis=0, keepdims=True)
            sum_b = jnp.sum(grad_shift, axis=0, keepdims=True)
            rows = []
            for part in range(3):
                for value in (sum_w, sum_b):
                    piece = split3(value)[part].astype(F32)
                    rows += [piece[:, :128], piece[:, 128:]]
            tail = jnp.concatenate(rows + [jnp.zeros((4, 128), F32)], axis=0).astype(BF16)
            kept[2304:, :] = tail
            given[2304:, :] = tail
    keep = pltpu.make_async_copy(hidden, hidden_far, sem)
    keep.start()
    second = flag(flags, 4, (C, 128))
    for a in range(3):
        for b in range(3):
            rows = slice((3 * a + b) * C, (3 * a + b + 1) * C)
            product = dot(hidden[b, 16 * a : 16 * a + 512, :], cot[...], ((0,), (0,)))
            left, right = product[:, :128], product[:, 128:]
            kept[rows, :] = jnp.where(second, right, left).astype(BF16)
            given[rows, :] = jnp.where(second, left, right).astype(BF16)
    keep.wait()


def hidden_and_kernel_gradient(flags, merged, up, stats, gain, bias, cot, grad_hidden):
    vmem = pl.BlockSpec(memory_space=pltpu.VMEM)
    return pl.pallas_call(
        hidden_kernel,
        out_shape=(
            jax.ShapeDtypeStruct((2320, 128), BF16),
            jax.ShapeDtypeStruct((2320, 128), BF16),
            pltpu.HBM((3, WIN, C), BF16),
        ),
        in_specs=[pl.BlockSpec(memory_space=pltpu.VMEM)] + [vmem] * 7,
        out_specs=(vmem, vmem, HBM),
        scratch_shapes=[pltpu.VMEM((3, WIN, C), BF16), pltpu.SemaphoreType.DMA],
        compiler_params=params(),
    )(flags, merged, up, stats, gain, bias, cot, grad_hidden)


def conv_kernel(hidden, weight, conv_bias, fine_out):
    total = jnp.zeros((512, C), F32) + conv_bias[...]
    for a in range(3):
        for b in range(3):
            total = total + dot(hidden[b, 16 * a : 16 * a + 512, :], weight[3 * a + b])
    fine_out[...] = total.astype(BF16)


def conv(hidden, weight, conv_bias):
    return pl.pallas_call(
        conv_kernel,
        out_shape=jax.ShapeDtypeStruct((512, C), BF16),
        compiler_params=params(),
        cost_estimate=pl.CostEstimate(
            flops=9 * 2 * 512 * C * C, bytes_accessed=3 * 10**6, transcendentals=0
        ),
    )(hidden, weight, conv_bias)


def pair_kernel(flags, kept, got, out_far, total, out, sems):
    total[...] = kept[...].astype(F32) + got[...].astype(F32)
    tails = [r[2304:, :].astype(F32) for r in (kept, got)]
    sums = sum(t[0:4] + t[4:8] + t[8:12] for t in tails)
    sums = jnp.where(flag(flags, 4, (2, 128)), sums[2:4], sums[0:2])
    parts = [p.astype(F32) for p in split3(sums)[:2]]
    tail = jnp.concatenate([jnp.zeros((36, 128), F32)] + parts, axis=0)
    own = iota((40, 128), 0) < 36
    copies = []
    for i in range(64):
        out[i] = jnp.where(own, total[36 * i : 36 * i + 40, :], tail).astype(BF16)
        if i % 16 == 15:
            part = pl.ds(i - 15, 16)
            copies.append(pltpu.make_async_copy(out.at[part], out_far.at[part], sems.at[i // 16]))
            copies[-1].start()
    for copy in copies:
        copy.wait()


def pair_sum(flags, kept, got):
    return pl.pallas_call(
        pair_kernel,
        out_shape=pltpu.HBM((64, 40, 128), BF16),
        in_specs=[
            pl.BlockSpec(memory_space=pltpu.VMEM),
            pl.BlockSpec(memory_space=pltpu.VMEM),
            pl.BlockSpec(memory_space=pltpu.VMEM),
        ],
        out_specs=HBM,
        scratch_shapes=[
            pltpu.VMEM((2320, 128), F32),
            pltpu.VMEM((64, 40, 128), BF16),
            pltpu.SemaphoreType.DMA((4,)),
        ],
        compiler_params=params(),
    )(flags, kept, got)


def share_kernel(got, out_far, sums, chunk, sems):
    total = jnp.sum(got[...].astype(F32), axis=0)
    chunk[...] = jnp.broadcast_to((total * (1.0 / 256.0)).astype(BF16)[None], chunk.shape)
    size = chunk.shape[0]
    copies = [
        pltpu.make_async_copy(chunk, out_far.at[pl.ds(size * i, size)], sems.at[i])
        for i in range(out_far.shape[0] // size)
    ]
    for copy in copies:
        copy.start()
    halves = total[36:38] + total[38:40]
    row = jnp.concatenate([halves[0:1], halves[1:2]], axis=1)
    sums[...] = jnp.broadcast_to(row, sums.shape)
    for copy in copies:
        copy.wait()


def share_sum(got):
    vmem = pl.BlockSpec(memory_space=pltpu.VMEM)
    return pl.pallas_call(
        share_kernel,
        out_shape=(pltpu.HBM((64, 40, 128), BF16), jax.ShapeDtypeStruct((8, C), F32)),
        in_specs=[vmem],
        out_specs=(HBM, vmem),
        scratch_shapes=[pltpu.VMEM((16, 40, 128), BF16), pltpu.SemaphoreType.DMA((4,))],
        compiler_params=params(),
    )(got)


def field_kernel(
    flags, merged, up, stats, gain, bias, grad_hidden, mine, other, field_out, norm_out
):
    second = flag(flags, 4, (8, C))
    weight = jnp.where(second, other[...], mine[...])
    plain = jnp.where(second, mine[...], other[...])
    sums = jnp.where(iota((8, C), 0) == 0, weight, plain)
    mean, inverse = combine_groups(stats[...])
    value = dot(up[WIN + 16 : WIN + 528, :], merged[...])
    xhat = (value - mean) * inverse
    shifted = xhat * gain[...] + bias[...]
    sig = 0.5 * jnp.tanh(0.5 * shifted) + 0.5
    grad_shift = grad_hidden[...] * sig * (1.0 + shifted * (1.0 - sig))
    same = jnp.where((iota((C, C), 0) >> 3) == (iota((C, C), 1) >> 3), 1.0, 0.0)
    means = dot_exact(sums * gain[...], same) * (1.0 / (65536 * SHARE))
    field = inverse * (grad_shift * gain[...] - means[1:2] - xhat * means[0:1])
    field_out[...] = field.astype(BF16)
    norm_out[...] = sums[:2] * (1.0 / 256.0)


def field_gradient(flags, merged, up, stats, gain, bias, grad_hidden, mine, other):
    vmem = pl.BlockSpec(memory_space=pltpu.VMEM)
    return pl.pallas_call(
        field_kernel,
        out_shape=(
            jax.ShapeDtypeStruct((512, C), BF16),
            jax.ShapeDtypeStruct((2, C), F32),
        ),
        in_specs=[pl.BlockSpec(memory_space=pltpu.VMEM)] + [vmem] * 8,
        compiler_params=params(),
        cost_estimate=pl.CostEstimate(
            flops=10**9, bytes_accessed=2 * 10**6, transcendentals=2 * 10**5
        ),
    )(flags, merged, up, stats, gain, bias, grad_hidden, mine, other)


def layout_kernel(flags, mine, other, out_far, out, sems):
    second = flag(flags, 4, (72, 128))
    copies = []
    for i in range(0, 64, 2):
        halves = []
        for ref in (mine, other):
            pair = [ref[i + k].astype(F32)[:36] for k in range(2)]
            halves.append(jnp.concatenate(pair, axis=0))
        rows = slice(36 * i, 36 * i + 72)
        out[rows, :128] = jnp.where(second, halves[1], halves[0])
        out[rows, 128:] = jnp.where(second, halves[0], halves[1])
        if i % 8 == 6:
            part = pl.ds(36 * (i - 6), 288)
            copies.append(pltpu.make_async_copy(out.at[part], out_far.at[part], sems.at[i // 8]))
            copies[-1].start()
    for copy in copies:
        copy.wait()


def lay_out(flags, mine, other):
    vmem = pl.BlockSpec(memory_space=pltpu.VMEM)
    return pl.pallas_call(
        layout_kernel,
        out_shape=pltpu.HBM((2304, C), F32),
        in_specs=[pl.BlockSpec(memory_space=pltpu.VMEM), vmem, vmem],
        out_specs=HBM,
        scratch_shapes=[pltpu.VMEM((2304, C), F32), pltpu.SemaphoreType.DMA((8,))],
        compiler_params=params(),
    )(flags, mine, other)


def copies_kernel(cells_far, out_far, cells, sem, sems):
    load = pltpu.make_async_copy(cells_far, cells, sem)
    load.start()
    load.wait()
    copies = [
        pltpu.make_async_copy(cells, out_far.at[i], sems.at[i]) for i in range(out_far.shape[0])
    ]
    for copy in copies:
        copy.start()
    for copy in copies:
        copy.wait()


def copies_of(cells):
    return pl.pallas_call(
        copies_kernel,
        out_shape=pltpu.HBM((16, 128, C), BF16),
        in_specs=[HBM],
        out_specs=HBM,
        scratch_shapes=[
            pltpu.VMEM((128, C), BF16),
            pltpu.SemaphoreType.DMA,
            pltpu.SemaphoreType.DMA((16,)),
        ],
        compiler_params=params(),
    )(in_hbm(cells))


def shift(value, axis, count, step):
    return lax.ppermute(value, axis, [((i + step) % count, i) for i in range(count)])


def per_device(
    coarse,
    norm1_gain,
    norm1_bias,
    w_qkv,
    w_proj,
    second_norm2_gain,
    second_norm2_bias,
    conv_weight,
    conv_bias,
    cotangent,
):
    y, c = lax.axis_index("y"), lax.axis_index("c")
    block = lax.axis_index(ZXC)
    marks = [y == 0, y == 3, block == 0, block == 31, c == 1, c == 1, c == 1, c == 1]
    flags = jnp.broadcast_to(jnp.stack(marks).astype(jnp.int32)[:, None], (8, C))
    up = jnp.asarray(UPSAMPLE, BF16)
    taps = conv_weight.reshape(9, C, C)

    own = coarse.reshape(128, C)
    cells = lax.all_to_all(copies_of(own), ("z", "x"), 0, 0, tiled=True).reshape(2048, C)


    first = jnp.concatenate([coarse[:, 0], cotangent[:, 0]], axis=0)
    last = jnp.concatenate([coarse[:, -1], cotangent[:, -1]], axis=0)
    before = lax.ppermute(last, ZXC, [(i, i + 1) for i in range(31)])[:, None]
    after = lax.ppermute(first, ZXC, [(i + 1, i) for i in range(31)])[:, None]
    wide = jnp.concatenate([before[:16], coarse, after[:16]], axis=1).reshape(160, C)
    grad = jnp.concatenate([before[16:], cotangent, after[16:]], axis=1)
    edges = jnp.pad(jnp.stack([grad[0], grad[-1]]), ((0, 0), (0, 14), (0, 0)))
    other = shift(cells, "c", 2, 1)

    stats = local_stats(cells)
    near, last, far = stats_and_rows(stats, shift(stats, "c", 2, 1), wide, edges)
    below, above, far = (
        shift(near, "y", 4, 1),
        shift(last, "y", 4, 3),
        shift(far, "y", 4, 2),
    )
    top = jnp.where(y == 0, 0, above[176:194])[None].astype(BF16)
    bottom = jnp.where(y == 3, 0, below[176:194])[None].astype(BF16)
    grad = jnp.concatenate([top, grad, bottom], axis=0)
    windows = [grad[:, b : b + 16].reshape(WIN, C) for b in range(3)]
    *sent, kept = partial_attention(
        cells, other, near, far, below, above, norm1_gain[None], norm1_bias[None], w_qkv
    )
    parts = [shift(part, "y", 4, 4 - k) for k, part in zip((1, 2, 3), sent)]
    merged, stats2 = merge(flags, parts, kept, w_proj, up)
    stats2 = lax.all_to_all(stats2.reshape(128, 1, 128), ALL, 0, 0, tiled=True)
    stats2 = stats2.reshape(128, 128)
    grad_hidden = back_conv(windows, taps)
    gain2, bias2 = second_norm2_gain[None], second_norm2_bias[None]
    kept, given, hidden = hidden_and_kernel_gradient(
        flags, merged, up, stats2, gain2, bias2, cotangent.reshape(512, C), grad_hidden
    )

    sent = pair_sum(flags, kept, shift(given, "c", 2, 1))
    got = lax.all_to_all(sent, ("y", "z", "x"), 0, 0, tiled=True)
    fine = conv(hidden, taps, conv_bias[None])
    got, fine = lax.optimization_barrier((got, fine))

    chunk, sums = share_sum(got)
    spread = lax.all_to_all(chunk, ("y", "z", "x"), 0, 0, tiled=True)
    field, grad_norm = field_gradient(
        flags, merged, up, stats2, gain2, bias2, grad_hidden, sums, shift(sums, "c", 2, 1)
    )
    spread, field = lax.optimization_barrier((spread, field))
    grad_conv = lay_out(flags, spread, shift(spread, "c", 2, 1)).reshape(3, 3, C, C)
    return (
        fine.reshape(32, 16, C),
        field.reshape(32, 16, C),
        grad_conv,
        grad_norm,
    )


def solution(mesh):
    split = Mesh(mesh.devices.reshape(4, 4, 4, 2), ALL)
    cells = P("y", ZXC, None)
    return jax.shard_map(
        per_device,
        mesh=split,
        in_specs=(cells,) + (P(),) * 8 + (cells,),
        out_specs=(cells, cells, P(), P()),
        check_vma=False,
    )
```

```python
import functools

import jax
import jax.numpy as jnp
import numpy as np
from jax import lax
from jax.experimental import pallas as pl
from jax.experimental.pallas import tpu as pltpu
from jax.sharding import Mesh, PartitionSpec as P

HEADS = 4
HD = 64
C = 256
SHARE = 8
EPS = 1e-05
F32 = jnp.float32
BF16 = jnp.bfloat16
VMEM_LIMIT = 50 * 2**20
HBM = pl.BlockSpec(memory_space=pltpu.HBM)
ZXC = ("z", "x", "c")
ALL = ("y", "z", "x", "c")

CELLS_IN = 192
PART = CELLS_IN + 16
STRIP = 672
KEY_BLOCK = 512
FINE_ROWS = 34
WIN = FINE_ROWS * 16


def upsample_matrix():
    def line(f):
        i = f // 2
        return {i: 0.75, (i - 1 if f % 2 == 0 else i + 1): 0.25}

    table = np.zeros((3, FINE_ROWS, 16, CELLS_IN), np.float32)
    for b in range(3):
        for fr in range(FINE_ROWS):
            for j in range(16):
                for r, wr in line(fr - 1).items():
                    for c, wc in line(j + b - 1).items():
                        table[b, fr, j, (r + 1) * 10 + c + 1] += wr * wc
    return table.reshape(3 * WIN, CELLS_IN)


UPSAMPLE = upsample_matrix()


def params(grid=None):
    return pltpu.CompilerParams(
        vmem_limit_bytes=VMEM_LIMIT,
        dimension_semantics=None if grid is None else ("arbitrary",) * grid,
    )


def in_vmem(value):
    return pltpu.with_memory_space_constraint(value, pltpu.VMEM)


def in_hbm(value):
    return pltpu.with_memory_space_constraint(value, pltpu.HBM)


def dot(a, b, contract=((1,), (0,))):
    return lax.dot_general(a, b, (contract, ((), ())), preferred_element_type=F32)


def dot_exact(a, b):
    size = a.shape[0]
    parts = jnp.concatenate([p.astype(F32) for p in split3(a)], axis=0).astype(BF16)
    result = dot(parts, b.astype(BF16))
    return result[:size] + result[size : 2 * size] + result[2 * size :]


def iota(shape, dim):
    return lax.broadcasted_iota(jnp.int32, shape, dim)


def flag(flags, index, shape):
    return jnp.broadcast_to(flags[index : index + 1, : shape[1]], shape) == 1


def split3(value):
    high = value.astype(BF16)
    rest = value - high.astype(F32)
    middle = rest.astype(BF16)
    low = (rest - middle.astype(F32)).astype(BF16)
    return high, middle, low


def group_row(mean_c, var_c):
    same = jnp.where((iota((C, C), 0) >> 3) == (iota((C, C), 1) >> 3), 1.0 / SHARE, 0.0)
    mean8 = jnp.broadcast_to(mean_c, (8, C))
    spread = mean8 - dot_exact(mean8, same)
    var8 = jnp.broadcast_to(var_c, (8, C)) + spread * spread
    to_group = jnp.where(iota((C, 128), 1) == (iota((C, 128), 0) >> 3), 1.0 / SHARE, 0.0)
    both = dot_exact(jnp.concatenate([mean8, var8], axis=0), to_group)
    return both[:8] + pltpu.roll(both[8:], 32, 1)


def combine_groups(rows):
    count = rows.shape[0]
    mean = jnp.sum(rows, axis=0, keepdims=True) / count
    off = rows - mean
    scatter = jnp.sum(off * off, axis=0, keepdims=True) / count
    mean8 = jnp.broadcast_to(mean, (8, 128))
    var8 = pltpu.roll(mean8, 96, 1) + scatter
    from_group = jnp.where(iota((128, C), 0) == (iota((128, C), 1) >> 3), 1.0, 0.0)
    both = dot_exact(jnp.concatenate([mean8, var8], axis=0), from_group)
    return both[:1], lax.rsqrt(both[8:9] + EPS)


def channel_stats(value):
    count = value.shape[0]
    mean = jnp.sum(value, axis=0, keepdims=True) / count
    off = value - mean
    return mean, jnp.sum(off * off, axis=0, keepdims=True) / count


def stats_rows(cells):
    mean, var = channel_stats(cells[...].astype(F32))
    high, middle, low = [p.astype(F32)[:1] for p in split3(group_row(mean, var))]
    upper = jnp.concatenate([high, middle], axis=1)
    return [upper, jnp.concatenate([low, jnp.zeros_like(low)], axis=1)]


def stats_kernel(cells, out):
    out[...] = jnp.concatenate(stats_rows(cells) + [jnp.zeros((6, C), F32)], axis=0)


def local_stats(cells):
    return pl.pallas_call(
        stats_kernel,
        out_shape=jax.ShapeDtypeStruct((8, C), F32),
        compiler_params=params(),
        cost_estimate=pl.CostEstimate(
            flops=3 * cells.size, bytes_accessed=2 * cells.size, transcendentals=0
        ),
    )(cells)


def rows_kernel(first, other, wide, edges, next_out, last_out, far_out):
    rows = [first[0:2, :], other[0:2, :], jnp.zeros((12, C), F32)]
    packed = jnp.concatenate(rows, axis=0).astype(BF16)
    for out in (next_out, last_out, far_out):
        out[:16, :] = packed
        out[16:176, :] = wide[...]
    next_out[176:, :] = edges[0]
    last_out[176:, :] = edges[1]


def stats_and_rows(first, other, wide, edges):
    return pl.pallas_call(
        rows_kernel,
        out_shape=(
            pltpu.VMEM((208, C), BF16),
            pltpu.VMEM((208, C), BF16),
            pltpu.VMEM((176, C), BF16),
        ),
        compiler_params=params(),
    )(first, other, wide, edges)


def attention_kernel(
    mine,
    other,
    near,
    far,
    down,
    up,
    gain,
    bias,
    w_far,
    out1,
    out2,
    out3,
    kept_far,
    keys,
    values,
    strip,
    w_qkv,
    kept,
    w_sem,
    block_sem,
    kept_sem,
):
    load = pltpu.make_async_copy(w_far, w_qkv, w_sem)
    load.start()
    rows = []
    for ref in (near, down, far, up):
        packed = ref[:16, :].astype(F32)
        for i in (0, 2):
            upper, lower = packed[i : i + 1], packed[i + 1 : i + 2]
            rows.append(upper[:, :128] + upper[:, 128:] + lower[:, :128])
    mean, inverse = combine_groups(jnp.concatenate(rows, axis=0))

    def norm(cells):
        normed = (cells.astype(F32) - mean) * inverse
        return (normed * gain[...] + bias[...]).astype(BF16)

    for i, ref in enumerate((near, down, far, up)):
        cells = ref[16:176, :].astype(F32)
        strip[10 + 160 * i : 170 + 160 * i, :] = cells
        if i == 0:
            strip[650:660, :] = cells[:10]
        if i == 3:
            strip[:10, :] = cells[150:]
    strip[660:, :] = jnp.zeros((STRIP - 660, C), F32)
    kept[PART:, :] = strip[:CELLS_IN, :].astype(BF16)
    tail = pl.ds(PART, CELLS_IN)
    keep = pltpu.make_async_copy(kept.at[tail], kept_far.at[tail], block_sem)
    keep.start()
    load.wait()

    head_of = iota((512, C), 1) >> 6
    ones = jnp.ones((512, C), BF16)
    for i in range(8):
        rows = slice(512 * i, 512 * i + 512)
        cells = (mine, other)[i // 4][512 * (i % 4) : 512 * (i % 4) + 512, :]
        both = dot(norm(cells), w_qkv[:, C:])
        both = both.astype(BF16)
        keys[rows, :] = both[:, :C]
        for head in range(HEADS):
            values[head, rows, :] = jnp.where(head_of == head, both[:, C:], ones)

    scale = HD**-0.5 * float(np.log2(np.e))
    queries = (dot(norm(strip[...]), w_qkv[:, :C]) * scale).astype(BF16)
    head_of = iota((STRIP, C), 1) >> 6
    lane = iota((STRIP, 128), 1)
    result = jnp.zeros((STRIP, C), F32)
    totals = jnp.ones((STRIP, C), F32)
    logs = jnp.zeros((STRIP, 128), F32)
    tops = jnp.zeros((STRIP, 128), F32)
    for head in range(HEADS):
        own = head_of == head
        masked = jnp.where(own, queries, jnp.zeros_like(queries))
        best, mixed = None, None
        for i in range(4096 // KEY_BLOCK):
            rows = slice(KEY_BLOCK * i, KEY_BLOCK * (i + 1))
            scores = dot(masked, keys[rows, :], ((1,), (1,)))
            top = jnp.max(scores, axis=1, keepdims=True)
            fresh = top if i == 0 else jnp.maximum(best, top)
            product = dot(jnp.exp2(scores - fresh).astype(BF16), values[head, rows, :])
            mixed = product if i == 0 else mixed * jnp.exp2(best - fresh) + product
            best = fresh
        result = jnp.where(own, mixed, result)
        totals = jnp.where(own, pltpu.roll(mixed, HD, 1), totals)
        spot = 0 if head else 128
        logs = jnp.where(lane == head, mixed[:, spot : spot + 128], logs)
        tops = jnp.where(lane == head, best, tops)
    result = (result / totals).astype(BF16)
    logs = tops + jnp.log2(jnp.where(lane < HEADS, logs, 1.0))
    high, middle, low = [p.astype(F32) for p in split3(logs)]
    packed = high + pltpu.roll(middle, 4, 1) + pltpu.roll(low, 8, 1)
    head = pl.ds(0, PART)
    copy = pltpu.make_async_copy(kept.at[head], kept_far.at[head], kept_sem)
    for step, out in enumerate((kept, out1, out2, out3)):
        rows = slice(160 * step, 160 * step + CELLS_IN)
        out[:CELLS_IN, :] = result[rows]
        turned = jnp.concatenate([packed[rows], jnp.zeros((64, 128), F32)], axis=0).T[:16]
        out[CELLS_IN:PART, :] = turned.astype(BF16)
        if step == 0:
            copy.start()
    keep.wait()
    copy.wait()


def partial_attention(mine, other, near, far, down, up, gain, bias, w_qkv):
    vmem = pl.BlockSpec(memory_space=pltpu.VMEM)
    return pl.pallas_call(
        attention_kernel,
        out_shape=(jax.ShapeDtypeStruct((PART, C), BF16),) * 3
        + (pltpu.HBM((PART + CELLS_IN, C), BF16),),
        in_specs=[vmem] * 8 + [HBM],
        out_specs=(vmem, vmem, vmem, HBM),
        scratch_shapes=[
            pltpu.VMEM((4096, C), BF16),
            pltpu.VMEM((HEADS, 4096, C), BF16),
            pltpu.VMEM((STRIP, C), F32),
            pltpu.VMEM((C, 3 * C), BF16),
            pltpu.VMEM((PART + CELLS_IN, C), BF16),
            pltpu.SemaphoreType.DMA,
            pltpu.SemaphoreType.DMA,
            pltpu.SemaphoreType.DMA,
        ],
        compiler_params=params(),
    )(mine, other, near, in_vmem(far), in_vmem(down), in_vmem(up), gain, bias, in_hbm(w_qkv))


def merge_kernel(
    flags, p1, p2, p3, kept_far, w_far, up, merged_out, stats_out, kept, w_proj, kept_sem, w_sem
):
    loads = [
        pltpu.make_async_copy(kept_far, kept, kept_sem),
        pltpu.make_async_copy(w_far, w_proj, w_sem),
    ]
    for load in loads:
        load.start()
    parts = (p1, p2, p3, kept)
    logs = []
    for part in parts:
        if part is kept:
            loads[0].wait()
        tail = part[CELLS_IN:PART, :].astype(F32)
        logs.append(tail[0:4] + tail[4:8] + tail[8:12])
    top = functools.reduce(jnp.maximum, logs)
    shares = [jnp.exp2(v - top) for v in logs]
    total = sum(shares)
    spread = jnp.where((iota((16, C), 1) >> 6) == (iota((16, C), 0) & 3), 1.0, 0.0).astype(BF16)
    attended = jnp.zeros((CELLS_IN, C), F32)
    for i, part in enumerate(parts):
        pieces = [p.astype(F32) for p in split3((shares[i] / total)[:, :CELLS_IN])]
        pieces.append(jnp.zeros_like(pieces[0]))
        wide = dot(jnp.concatenate(pieces, axis=0).astype(BF16), spread, ((0,), (0,)))
        attended = attended + wide * part[:CELLS_IN, :].astype(F32)
    loads[1].wait()
    merged = kept[PART:, :].astype(F32) + dot(attended.astype(BF16), w_proj[...])
    cell = iota((CELLS_IN, C), 0)
    col = cell - 10 * ((cell * 6554) >> 16)
    outside = (
        ((cell < 10) & flag(flags, 0, cell.shape))
        | ((cell >= 170) & flag(flags, 1, cell.shape))
        | ((col == 0) & flag(flags, 2, cell.shape))
        | ((col == 9) & flag(flags, 3, cell.shape))
        | (cell >= 180)
    )
    merged = jnp.where(outside, 0.0, merged).astype(BF16)
    merged_out[...] = merged
    field = dot(up[WIN + 16 : WIN + 528, :], merged)
    mean, var = channel_stats(field)
    stats_out[...] = jnp.broadcast_to(group_row(mean, var)[:1], stats_out.shape)


def merge(flags, parts, kept, w_proj, up):
    vmem = pl.BlockSpec(memory_space=pltpu.VMEM)
    return pl.pallas_call(
        merge_kernel,
        out_shape=(
            jax.ShapeDtypeStruct((CELLS_IN, C), BF16),
            jax.ShapeDtypeStruct((128, 128), F32),
        ),
        in_specs=[pl.BlockSpec(memory_space=pltpu.VMEM), vmem, vmem, vmem, HBM, HBM, vmem],
        out_specs=(vmem, vmem),
        scratch_shapes=[
            pltpu.VMEM((PART + CELLS_IN, C), BF16),
            pltpu.VMEM((C, C), BF16),
            pltpu.SemaphoreType.DMA,
            pltpu.SemaphoreType.DMA,
        ],
        compiler_params=params(),
    )(flags, *parts, in_hbm(kept), in_hbm(w_proj), up)


def back_kernel(c0, c1, c2, weight, out):
    windows = (c0, c1, c2)
    total = jnp.zeros((512, C), F32)
    for a in range(3):
        for b in range(3):
            window = windows[2 - b][16 * (2 - a) : 16 * (2 - a) + 512, :]
            total = total + dot(window, weight[3 * a + b], ((1,), (1,)))
    out[...] = total


def back_conv(windows, weight):
    return pl.pallas_call(
        back_kernel,
        out_shape=jax.ShapeDtypeStruct((512, C), F32),
        compiler_params=params(),
        cost_estimate=pl.CostEstimate(
            flops=9 * 2 * 512 * C * C, bytes_accessed=3 * 10**6, transcendentals=0
        ),
    )(*windows, weight)


def hidden_kernel(
    flags,
    merged,
    up,
    stats,
    gain,
    bias,
    cot,
    grad_hidden,
    kept,
    given,
    hidden_far,
    hidden,
    sem,
):
    mean, inverse = combine_groups(stats[...])
    row = iota((WIN, C), 0)
    col = row & 15
    for b in range(3):
        field = dot(up[b * WIN : (b + 1) * WIN, :], merged[...])
        xhat = (field - mean) * inverse
        shifted = xhat * gain[...] + bias[...]
        sig = 0.5 * jnp.tanh(0.5 * shifted) + 0.5
        outside = ((row < 16) & flag(flags, 0, row.shape)) | (
            (row >= 528) & flag(flags, 1, row.shape)
        )
        if b == 0:
            outside = outside | ((col == 0) & flag(flags, 2, row.shape))
        if b == 2:
            outside = outside | ((col == 15) & flag(flags, 3, row.shape))
        hidden[b] = jnp.where(outside, 0.0, shifted * sig).astype(BF16)
        if b == 1:
            inner = slice(16, 528)
            s, t = sig[inner], shifted[inner]
            grad_shift = grad_hidden[...] * s * (1.0 + t * (1.0 - s))
            sum_w = jnp.sum(grad_shift * xhat[inner], axis=0, keepdims=True)
            sum_b = jnp.sum(grad_shift, axis=0, keepdims=True)
            rows = []
            for part in range(3):
                for value in (sum_w, sum_b):
                    piece = split3(value)[part].astype(F32)
                    rows += [piece[:, :128], piece[:, 128:]]
            tail = jnp.concatenate(rows + [jnp.zeros((4, 128), F32)], axis=0).astype(BF16)
            kept[2304:, :] = tail
            given[2304:, :] = tail
    keep = pltpu.make_async_copy(hidden, hidden_far, sem)
    keep.start()
    second = flag(flags, 4, (C, 128))
    for a in range(3):
        for b in range(3):
            rows = slice((3 * a + b) * C, (3 * a + b + 1) * C)
            product = dot(hidden[b, 16 * a : 16 * a + 512, :], cot[...], ((0,), (0,)))
            left, right = product[:, :128], product[:, 128:]
            kept[rows, :] = jnp.where(second, right, left).astype(BF16)
            given[rows, :] = jnp.where(second, left, right).astype(BF16)
    keep.wait()


def hidden_and_kernel_gradient(flags, merged, up, stats, gain, bias, cot, grad_hidden):
    vmem = pl.BlockSpec(memory_space=pltpu.VMEM)
    return pl.pallas_call(
        hidden_kernel,
        out_shape=(
            jax.ShapeDtypeStruct((2320, 128), BF16),
            jax.ShapeDtypeStruct((2320, 128), BF16),
            pltpu.HBM((3, WIN, C), BF16),
        ),
        in_specs=[pl.BlockSpec(memory_space=pltpu.VMEM)] + [vmem] * 7,
        out_specs=(vmem, vmem, HBM),
        scratch_shapes=[pltpu.VMEM((3, WIN, C), BF16), pltpu.SemaphoreType.DMA],
        compiler_params=params(),
    )(flags, merged, up, stats, gain, bias, cot, grad_hidden)


def conv_kernel(hidden, weight, conv_bias, fine_out):
    total = jnp.zeros((512, C), F32) + conv_bias[...]
    for a in range(3):
        for b in range(3):
            total = total + dot(hidden[b, 16 * a : 16 * a + 512, :], weight[3 * a + b])
    fine_out[...] = total.astype(BF16)


def conv(hidden, weight, conv_bias):
    return pl.pallas_call(
        conv_kernel,
        out_shape=jax.ShapeDtypeStruct((512, C), BF16),
        compiler_params=params(),
        cost_estimate=pl.CostEstimate(
            flops=9 * 2 * 512 * C * C, bytes_accessed=3 * 10**6, transcendentals=0
        ),
    )(hidden, weight, conv_bias)


def pair_kernel(flags, kept, got, out_far, total, out, sems):
    total[...] = kept[...].astype(F32) + got[...].astype(F32)
    tails = [r[2304:, :].astype(F32) for r in (kept, got)]
    sums = sum(t[0:4] + t[4:8] + t[8:12] for t in tails)
    sums = jnp.where(flag(flags, 4, (2, 128)), sums[2:4], sums[0:2])
    parts = [p.astype(F32) for p in split3(sums)[:2]]
    tail = jnp.concatenate([jnp.zeros((36, 128), F32)] + parts, axis=0)
    own = iota((40, 128), 0) < 36
    copies = []
    for i in range(64):
        out[i] = jnp.where(own, total[36 * i : 36 * i + 40, :], tail).astype(BF16)
        if i % 16 == 15:
            part = pl.ds(i - 15, 16)
            copies.append(pltpu.make_async_copy(out.at[part], out_far.at[part], sems.at[i // 16]))
            copies[-1].start()
    for copy in copies:
        copy.wait()


def pair_sum(flags, kept, got):
    return pl.pallas_call(
        pair_kernel,
        out_shape=pltpu.HBM((64, 40, 128), BF16),
        in_specs=[
            pl.BlockSpec(memory_space=pltpu.VMEM),
            pl.BlockSpec(memory_space=pltpu.VMEM),
            pl.BlockSpec(memory_space=pltpu.VMEM),
        ],
        out_specs=HBM,
        scratch_shapes=[
            pltpu.VMEM((2320, 128), F32),
            pltpu.VMEM((64, 40, 128), BF16),
            pltpu.SemaphoreType.DMA((4,)),
        ],
        compiler_params=params(),
    )(flags, kept, got)


def share_kernel(got, out_far, sums, chunk, sems):
    total = jnp.sum(got[...].astype(F32), axis=0)
    chunk[...] = jnp.broadcast_to((total * (1.0 / 256.0)).astype(BF16)[None], chunk.shape)
    size = chunk.shape[0]
    copies = [
        pltpu.make_async_copy(chunk, out_far.at[pl.ds(size * i, size)], sems.at[i])
        for i in range(out_far.shape[0] // size)
    ]
    for copy in copies:
        copy.start()
    halves = total[36:38] + total[38:40]
    row = jnp.concatenate([halves[0:1], halves[1:2]], axis=1)
    sums[...] = jnp.broadcast_to(row, sums.shape)
    for copy in copies:
        copy.wait()


def share_sum(got):
    vmem = pl.BlockSpec(memory_space=pltpu.VMEM)
    return pl.pallas_call(
        share_kernel,
        out_shape=(pltpu.HBM((64, 40, 128), BF16), jax.ShapeDtypeStruct((8, C), F32)),
        in_specs=[vmem],
        out_specs=(HBM, vmem),
        scratch_shapes=[pltpu.VMEM((16, 40, 128), BF16), pltpu.SemaphoreType.DMA((4,))],
        compiler_params=params(),
    )(got)


def field_kernel(
    flags, merged, up, stats, gain, bias, grad_hidden, mine, other, field_out, norm_out
):
    second = flag(flags, 4, (8, C))
    weight = jnp.where(second, other[...], mine[...])
    plain = jnp.where(second, mine[...], other[...])
    sums = jnp.where(iota((8, C), 0) == 0, weight, plain)
    mean, inverse = combine_groups(stats[...])
    value = dot(up[WIN + 16 : WIN + 528, :], merged[...])
    xhat = (value - mean) * inverse
    shifted = xhat * gain[...] + bias[...]
    sig = 0.5 * jnp.tanh(0.5 * shifted) + 0.5
    grad_shift = grad_hidden[...] * sig * (1.0 + shifted * (1.0 - sig))
    same = jnp.where((iota((C, C), 0) >> 3) == (iota((C, C), 1) >> 3), 1.0, 0.0)
    means = dot_exact(sums * gain[...], same) * (1.0 / (65536 * SHARE))
    field = inverse * (grad_shift * gain[...] - means[1:2] - xhat * means[0:1])
    field_out[...] = field.astype(BF16)
    norm_out[...] = sums[:2] * (1.0 / 256.0)


def field_gradient(flags, merged, up, stats, gain, bias, grad_hidden, mine, other):
    vmem = pl.BlockSpec(memory_space=pltpu.VMEM)
    return pl.pallas_call(
        field_kernel,
        out_shape=(
            jax.ShapeDtypeStruct((512, C), BF16),
            jax.ShapeDtypeStruct((2, C), F32),
        ),
        in_specs=[pl.BlockSpec(memory_space=pltpu.VMEM)] + [vmem] * 8,
        compiler_params=params(),
        cost_estimate=pl.CostEstimate(
            flops=10**9, bytes_accessed=2 * 10**6, transcendentals=2 * 10**5
        ),
    )(flags, merged, up, stats, gain, bias, grad_hidden, mine, other)


def layout_kernel(flags, mine, other, out_far, out, sems):
    second = flag(flags, 4, (72, 128))
    copies = []
    for i in range(0, 64, 2):
        halves = []
        for ref in (mine, other):
            pair = [ref[i + k].astype(F32)[:36] for k in range(2)]
            halves.append(jnp.concatenate(pair, axis=0))
        rows = slice(36 * i, 36 * i + 72)
        out[rows, :128] = jnp.where(second, halves[1], halves[0])
        out[rows, 128:] = jnp.where(second, halves[0], halves[1])
        if i % 8 == 6:
            part = pl.ds(36 * (i - 6), 288)
            copies.append(pltpu.make_async_copy(out.at[part], out_far.at[part], sems.at[i // 8]))
            copies[-1].start()
    for copy in copies:
        copy.wait()


def lay_out(flags, mine, other):
    vmem = pl.BlockSpec(memory_space=pltpu.VMEM)
    return pl.pallas_call(
        layout_kernel,
        out_shape=pltpu.HBM((2304, C), F32),
        in_specs=[pl.BlockSpec(memory_space=pltpu.VMEM), vmem, vmem],
        out_specs=HBM,
        scratch_shapes=[pltpu.VMEM((2304, C), F32), pltpu.SemaphoreType.DMA((8,))],
        compiler_params=params(),
    )(flags, mine, other)


def copies_kernel(cells_far, out_far, cells, sem, sems):
    load = pltpu.make_async_copy(cells_far, cells, sem)
    load.start()
    load.wait()
    copies = [
        pltpu.make_async_copy(cells, out_far.at[i], sems.at[i]) for i in range(out_far.shape[0])
    ]
    for copy in copies:
        copy.start()
    for copy in copies:
        copy.wait()


def copies_of(cells):
    return pl.pallas_call(
        copies_kernel,
        out_shape=pltpu.HBM((16, 128, C), BF16),
        in_specs=[HBM],
        out_specs=HBM,
        scratch_shapes=[
            pltpu.VMEM((128, C), BF16),
            pltpu.SemaphoreType.DMA,
            pltpu.SemaphoreType.DMA((16,)),
        ],
        compiler_params=params(),
    )(in_hbm(cells))


def shift(value, axis, count, step):
    return lax.ppermute(value, axis, [((i + step) % count, i) for i in range(count)])


def per_device(
    coarse,
    norm1_gain,
    norm1_bias,
    w_qkv,
    w_proj,
    second_norm2_gain,
    second_norm2_bias,
    conv_weight,
    conv_bias,
    cotangent,
):
    y, c = lax.axis_index("y"), lax.axis_index("c")
    block = lax.axis_index(ZXC)
    marks = [y == 0, y == 3, block == 0, block == 31, c == 1, c == 1, c == 1, c == 1]
    flags = jnp.broadcast_to(jnp.stack(marks).astype(jnp.int32)[:, None], (8, C))
    up = jnp.asarray(UPSAMPLE, BF16)
    taps = conv_weight.reshape(9, C, C)

    own = coarse.reshape(128, C)
    cells = lax.all_to_all(copies_of(own), ("z", "x"), 0, 0, tiled=True).reshape(2048, C)


    first = jnp.concatenate([coarse[:, 0], cotangent[:, 0]], axis=0)
    last = jnp.concatenate([coarse[:, -1], cotangent[:, -1]], axis=0)
    before = lax.ppermute(last, ZXC, [(i, i + 1) for i in range(31)])[:, None]
    after = lax.ppermute(first, ZXC, [(i + 1, i) for i in range(31)])[:, None]
    wide = jnp.concatenate([before[:16], coarse, after[:16]], axis=1).reshape(160, C)
    grad = jnp.concatenate([before[16:], cotangent, after[16:]], axis=1)
    edges = jnp.pad(jnp.stack([grad[0], grad[-1]]), ((0, 0), (0, 14), (0, 0)))
    other = shift(cells, "c", 2, 1)

    stats = local_stats(cells)
    near, last, far = stats_and_rows(stats, shift(stats, "c", 2, 1), wide, edges)
    below, above, far = (
        shift(near, "y", 4, 1),
        shift(last, "y", 4, 3),
        shift(far, "y", 4, 2),
    )
    top = jnp.where(y == 0, 0, above[176:194])[None].astype(BF16)
    bottom = jnp.where(y == 3, 0, below[176:194])[None].astype(BF16)
    grad = jnp.concatenate([top, grad, bottom], axis=0)
    windows = [grad[:, b : b + 16].reshape(WIN, C) for b in range(3)]
    *sent, kept = partial_attention(
        cells, other, near, far, below, above, norm1_gain[None], norm1_bias[None], w_qkv
    )
    parts = [shift(part, "y", 4, 4 - k) for k, part in zip((1, 2, 3), sent)]
    merged, stats2 = merge(flags, parts, kept, w_proj, up)
    stats2 = lax.all_to_all(stats2.reshape(128, 1, 128), ALL, 0, 0, tiled=True)
    stats2 = stats2.reshape(128, 128)
    grad_hidden = back_conv(windows, taps)
    gain2, bias2 = second_norm2_gain[None], second_norm2_bias[None]
    kept, given, hidden = hidden_and_kernel_gradient(
        flags, merged, up, stats2, gain2, bias2, cotangent.reshape(512, C), grad_hidden
    )

    sent = pair_sum(flags, kept, shift(given, "c", 2, 1))
    got = lax.all_to_all(sent, ("y", "z", "x"), 0, 0, tiled=True)
    fine = conv(hidden, taps, conv_bias[None])
    got, fine = lax.optimization_barrier((got, fine))

    chunk, sums = share_sum(got)
    spread = lax.all_to_all(chunk, ("y", "z", "x"), 0, 0, tiled=True)
    field, grad_norm = field_gradient(
        flags, merged, up, stats2, gain2, bias2, grad_hidden, sums, shift(sums, "c", 2, 1)
    )
    spread, field = lax.optimization_barrier((spread, field))
    grad_conv = lay_out(flags, spread, shift(spread, "c", 2, 1)).reshape(3, 3, C, C)
    return (
        fine.reshape(32, 16, C),
        field.reshape(32, 16, C),
        grad_conv,
        grad_norm,
    )


def solution(mesh):
    split = Mesh(mesh.devices.reshape(4, 4, 4, 2), ALL)
    cells = P("y", ZXC, None)
    return jax.shard_map(
        per_device,
        mesh=split,
        in_specs=(cells,) + (P(),) * 8 + (cells,),
        out_specs=(cells, cells, P(), P()),
        check_vma=False,
    )
```
